1024 devices in a mesh: dp: 128 (over z, x), mp: 8 (over y, core).
Axes of the slice: x: 4, y: 4, z: 32, core: 2. Of those that a mesh axis runs over, the one named last changes fastest.
Arguments:
- embeddings: bfloat16 [262144, 1024], P(('dp', 'mp')), may hold values from -6 to 6
- assignments: int32 [262144], P(('dp', 'mp')), may hold values from 0 to 2047
- old_centroids: float32 [2048, 1024], P('dp', 'mp'), may hold values from -6 to 6
- slab_rows: int32 [2048, 128], P(('dp', 'mp')), may hold values from 0 to 2047
- slab_len: int32 [2048], P(('dp', 'mp')), may hold values from 2 to 128
Outputs:
- centroids: float32 [2048, 1024], P('dp', 'mp')
- best_cosine: float32 [2048, 128], P(('dp', 'mp'))
The draws below stay inside these ranges and needn't reach their ends.
Inputs may be any that keep to these rules, and one draw needn't show every extreme that they name: `slab_rows`: entries index rows of the slab's own group of 2048 rows, those held by one index of dp.
All inputs are finite; a program needn't handle non-finite values.
Results may differ from the reference program's by a relative error of at most 0.0004.
Values may be sent and summed in bfloat16 or wider, within the bound.
No kernel may reach another device: no remote copies, remote signals or barrier semaphores. Data moves between devices by JAX's collectives and lax.ppermute only.
A program may use at most 32 MiB of HBM per device.

```python
import math
import jax
import jax.numpy as jnp
import numpy as np
from jax import lax

D = 1024
SLAB_DEV = 2
M = 128
ROWS = 262144
GROUP = 2048
K = 2048
SLABS = 2048
N_DP = 128
N_MP = 8


def with_ends(values, key, low, high):
    extent = values.shape
    index_at = [jax.random.randint(jax.random.fold_in(key, axis), (), 0, extent[axis]) for axis in range(len(extent))]
    values = values.at[tuple(index_at)].set(low)
    longest = extent.index(max(extent))
    index_at[longest] = (index_at[longest] + 1) % extent[longest]
    return values.at[tuple(index_at)].set(high)


def steps_of(own_key, extent, shards, low, high):
    gain = 1.0
    for dim, shards_of in shards:
        steps = jax.random.uniform(jax.random.fold_in(jax.random.fold_in(own_key, 6), dim), (shards_of,), jnp.float32, low / len(shards), high / len(shards))
        gain = gain * jnp.repeat(jnp.exp(steps), extent[dim] // shards_of).reshape((-1,) + (1,) * (len(extent) - 1 - dim))
    return gain


def cumulative_ranks(count, slope):
    portions = [(1 << 20) // math.isqrt(standing ** slope) + 1 for standing in range(1, count + 1)]
    deviation = 1 + sum(portions) // (1 << 30)
    return np.cumsum(np.array([max(1, weight // deviation) for weight in portions]))


def skewed_ids(rng, dims, amount, skew):
    listing = cumulative_ranks(amount, skew)
    lot = jax.random.randint(jax.random.fold_in(rng, 1), dims, 0, int(listing[amount - 1]))
    rank = jnp.searchsorted(jnp.asarray(listing, jnp.int32), lot, side="right")
    return jax.random.permutation(jax.random.fold_in(rng, 2), amount)[rank].astype(jnp.int32)


def noise(key, dims, deviation, limit, pieces=(), kind=jnp.bfloat16):
    loudness = steps_of(key, dims, pieces, -0.22, 0.18) if pieces else 1.0
    entries = jax.random.normal(key, dims, jnp.float32) * deviation * loudness
    return jnp.minimum(jnp.maximum(entries, -limit), limit).astype(kind)


def setup_inputs(seed: int = 0) -> dict:
    arg_keys = jax.random.split(jax.random.key(seed), 6)
    return {
        "embeddings": noise(arg_keys[0], (ROWS, D), 1.0, 6.0, ((0, 1024),)),
        "assignments": with_ends(skewed_ids(arg_keys[1], (ROWS,), K, 2), jax.random.fold_in(arg_keys[1], 3), 0, K - 1).astype(jnp.int32),
        "old_centroids": noise(arg_keys[2], (K, D), 1.0, 6.0, ((0, 128), (1, 8)), jnp.float32),
        "slab_rows": with_ends(jax.random.randint(arg_keys[3], (SLABS, M), 0, GROUP), jax.random.fold_in(arg_keys[3], 1), 0, GROUP - 1).astype(jnp.int32),
        "slab_len": with_ends(jax.random.randint(arg_keys[4], (SLABS,), 2, M + 1), jax.random.fold_in(arg_keys[4], 1), 2, M).astype(jnp.int32),
    }


def best_match(gram_tile, length):
    diagonal_part = jnp.diagonal(gram_tile, axis1=-2, axis2=-1)
    inverse_norm = lax.rsqrt(diagonal_part + 1e-06)
    cosine = gram_tile * inverse_norm[..., :, None] * inverse_norm[..., None, :]
    position = jnp.arange(gram_tile.shape[-1], dtype=jnp.int32)
    live = position < jnp.asarray(length)[..., None]
    pair_mask = live[..., None, :] & (position[:, None] != position[None, :])
    largest = lax.optimization_barrier(jnp.max(jnp.where(pair_mask, cosine, -2.0), axis=-1))
    return jnp.where(live, largest, 0.0)

def reference(embeddings, assignments, old_centroids, slab_rows, slab_len):

    def accumulate(running, group_index):
        group_block = lax.dynamic_slice_in_dim(embeddings, group_index * GROUP, GROUP, 0).astype(jnp.float32)
        group_labels = lax.dynamic_slice_in_dim(assignments, group_index * GROUP, GROUP, 0)
        return (running + jax.ops.segment_sum(group_block, group_labels, num_segments=K), None)
    summed, _ = lax.scan(accumulate, jnp.zeros((K, D), jnp.float32), jnp.arange(N_DP, dtype=jnp.int32))
    counts = jax.ops.segment_sum(jnp.ones((ROWS,), jnp.float32), assignments, num_segments=K)
    centroids = (summed + old_centroids) / (counts[:, None] + 1.0)

    def slab_score(slab_index):
        group_index = slab_index // (SLAB_DEV * N_MP)
        row_index = (group_index * GROUP + slab_rows[slab_index]).astype(jnp.int32)
        members = embeddings[row_index].astype(jnp.float32)
        gram_tile = jnp.dot(members, members.T, precision=lax.Precision.HIGHEST)
        return best_match(gram_tile, slab_len[slab_index])
    best_cosine = lax.map(slab_score, jnp.arange(SLABS, dtype=jnp.int32))
    return (centroids, best_cosine)
```

```python
import jax
import jax.numpy as jnp
from jax import lax
from jax.experimental import pallas as pl
from jax.experimental.pallas import tpu as pltpu
from jax.sharding import Mesh, PartitionSpec as P

F32, BF16, I32 = jnp.float32, jnp.bfloat16, jnp.int32
SIZES = (8, 4, 4, 4, 2)
NAMES = ("zh", "zl", "x", "y", "c")
BLOCK = 32
ROWS = 256
FEATS = 32
MSG = 80
MIB = 1 << 20


def params(mib):
    return pltpu.CompilerParams(vmem_limit_bytes=mib * MIB)


def cost(flops, moved):
    return pl.CostEstimate(flops=flops, bytes_accessed=moved, transcendentals=0)


def pack_kernel(emb_ref, label_ref, out_ref):
    turned = emb_ref[...].T
    c = label_ref[...]
    high = ((c >> 6) & 3) * 64 + (c >> 8) * 8 + ((c >> 4) & 3) * 2 + (c & 1)
    low = ((c >> 1) & 1) * 4 + ((c >> 2) & 3)
    row = lax.broadcasted_iota(I32, (16, 128), 0)
    codes = jnp.where(row == 0, high[0:1], 0)
    codes = jnp.where(row == 1, high[1:2], codes)
    codes = jnp.where(row == 2, low[0:1], codes)
    codes = jnp.where(row == 3, low[1:2], codes)
    codes = codes.astype(F32).astype(BF16)
    for x in range(4):
        for mp in range(8):
            d, f = x * 8 + mp, (mp * 4 + x) * FEATS
            out_ref[d, 0:32, :] = turned[f : f + FEATS, 0:128]
            out_ref[d, 32:64, :] = turned[f : f + FEATS, 128:256]
            out_ref[d, 64:80, :] = codes


def sum_kernel(msg_ref, out_ref, a_ref, b_ref, p_ref, q_ref):
    cluster = lax.broadcasted_iota(I32, (256, 128), 0)
    group = lax.broadcasted_iota(I32, (128, 128), 0)

    def build(s, carry):
        codes = msg_ref[s, 64:80, :].astype(F32).astype(I32)
        for t in range(2):
            high, low = codes[t : t + 1], codes[2 + t : 3 + t]
            at = pl.ds(pl.multiple_of(s * 256 + t * 128, 128), 128)
            a_ref[:, at] = jnp.where(cluster == high, 1.0, 0.0).astype(BF16)
            part = msg_ref[s, 32 * t : 32 * t + 32, :]
            for g in range(8):
                b_ref[32 * g : 32 * g + 32, at] = part * jnp.where(low == g, 1.0, 0.0).astype(BF16)
            within = ((high >> 1) & 7) * 16 + (low & 3) * 4 + (low >> 2) * 2 + (high & 1)
            p_ref[:, at] = jnp.where(cluster[0:16] == (high >> 4), 1.0, 0.0).astype(BF16)
            q_ref[:, at] = jnp.where(group == within, 1.0, 0.0).astype(BF16)
        return carry

    lax.fori_loop(0, BLOCK, build, 0)
    contract = (((1,), (1,)), ((), ()))
    sums = lax.dot_general(a_ref[...], b_ref[...], contract, preferred_element_type=F32)
    counts = lax.dot_general(p_ref[...], q_ref[...], contract, preferred_element_type=F32)
    for zl in range(4):
        out_ref[zl, 0:64, :] = sums[zl * 64 : zl * 64 + 64, 0:128]
        out_ref[zl, 64:128, :] = sums[zl * 64 : zl * 64 + 64, 128:256]
        out_ref[zl, 128:132, :] = counts[zl * 4 : zl * 4 + 4, :]
        out_ref[zl, 132:136, :] = jnp.zeros((4, 128), F32)


def regroup_kernel(in_ref, out_ref, s_ref):
    s_ref[...] = (in_ref[0] + in_ref[1]) + (in_ref[2] + in_ref[3])
    for m in range(32):
        out_ref[5 * m : 5 * m + 2, :] = s_ref[2 * m : 2 * m + 2, :]
        out_ref[5 * m + 2 : 5 * m + 4, :] = s_ref[64 + 2 * m : 66 + 2 * m, :]
        out_ref[5 * m + 4 : 5 * m + 5, :] = s_ref[128 + m // 8 : 129 + m // 8, :]


def finish_kernel(at_ref, in_ref, old_ref, out_ref):
    slot = lax.broadcasted_iota(I32, (4, 128), 1) // FEATS
    parts = []
    for x in range(4):
        total = in_ref[5 * x : 5 * x + 4, :]
        for zh in range(1, 8):
            m = zh * 4 + x
            total = total + in_ref[5 * m : 5 * m + 4, :]
        parts.append(total)
    count_row = in_ref[4:5, :]
    for zh in range(1, 8):
        count_row = count_row + in_ref[20 * zh + 4 : 20 * zh + 5, :]
    lane = lax.broadcasted_iota(I32, (16, 128), 1)
    own = lane == at_ref[0] + lax.broadcasted_iota(I32, (16, 128), 0)
    counts = jnp.sum(jnp.where(own, count_row, 0.0), axis=1, keepdims=True)
    for low in range(4):
        rows = jnp.zeros((4, 128), F32)
        for x in range(4):
            shift = ((x - low) * FEATS) % 128
            moved = pltpu.roll(parts[x], shift, 1) if shift else parts[x]
            rows = jnp.where(slot == x, moved, rows)
        j = slice(4 * low, 4 * low + 4)
        out_ref[j, :] = (rows + old_ref[j, :]) / (counts[j] + 1.0)


def match_kernel(len_ref, rows_ref, emb_ref, out_ref):
    row = lax.broadcasted_iota(I32, (256, 2048), 1)
    pick = jnp.where(row == rows_ref[...], 1.0, 0.0).astype(BF16)
    members = jnp.dot(pick, emb_ref[...], preferred_element_type=F32).astype(BF16)
    i = lax.broadcasted_iota(I32, (128, 128), 0)
    j = lax.broadcasted_iota(I32, (128, 128), 1)
    for s in range(2):
        one = members[128 * s : 128 * s + 128]
        gram = lax.dot_general(one, one, (((1,), (1,)), ((), ())), preferred_element_type=F32)
        diagonal = jnp.where(i == j, gram, 0.0)
        down = lax.rsqrt(jnp.sum(diagonal, axis=1, keepdims=True) + 1e-06)
        across = lax.rsqrt(jnp.sum(diagonal, axis=0, keepdims=True) + 1e-06)
        cosine = gram * down * across
        length = len_ref[s]
        largest = jnp.max(jnp.where((i < length) & (i != j), cosine, -2.0), axis=0, keepdims=True)
        out_ref[s : s + 1, :] = jnp.where(j[0:1] < length, largest, 0.0)


VMEM = pl.BlockSpec(memory_space=pltpu.VMEM)
SMEM = pl.BlockSpec(memory_space=pltpu.SMEM)


def local(embeddings, assignments, old_centroids, slab_rows, slab_len):
    gathered = lax.all_gather(embeddings, ("y", "c"), axis=0, tiled=True)
    messages = pl.pallas_call(
        pack_kernel,
        out_shape=jax.ShapeDtypeStruct((BLOCK, MSG, 128), BF16),
        in_specs=[VMEM, VMEM],
        out_specs=VMEM,
        compiler_params=params(8),
        cost_estimate=cost(1 << 20, 3 << 19),
        name="pack",
    )(embeddings, assignments.reshape(2, 128))
    messages = lax.all_to_all(messages, ("x", "y", "c"), 0, 0, tiled=True)
    parts = pl.pallas_call(
        sum_kernel,
        out_shape=jax.ShapeDtypeStruct((4, 136, 128), F32),
        in_specs=[VMEM],
        out_specs=VMEM,
        scratch_shapes=[
            pltpu.VMEM((256, 8192), BF16),
            pltpu.VMEM((256, 8192), BF16),
            pltpu.VMEM((16, 8192), BF16),
            pltpu.VMEM((128, 8192), BF16),
        ],
        compiler_params=params(20),
        cost_estimate=cost(1 << 31, 1 << 20),
        name="sums",
    )(messages)
    parts = lax.all_to_all(parts, "zl", 0, 0, tiled=True)
    parts = pl.pallas_call(
        regroup_kernel,
        out_shape=jax.ShapeDtypeStruct((160, 128), F32),
        in_specs=[VMEM],
        out_specs=VMEM,
        scratch_shapes=[pltpu.VMEM((136, 128), F32)],
        compiler_params=params(4),
        cost_estimate=cost(1 << 18, 1 << 19),
        name="regroup",
    )(parts)
    parts = lax.all_to_all(parts.reshape(32, 5, 1, 128), ("zh", "x"), 0, 0, tiled=True)
    first = ((lax.axis_index("zh") % 2) * 4 + lax.axis_index("x")) * 16
    centroids = pl.pallas_call(
        finish_kernel,
        out_shape=jax.ShapeDtypeStruct((16, 128), F32),
        in_specs=[SMEM, VMEM, VMEM],
        out_specs=VMEM,
        compiler_params=params(4),
        cost_estimate=cost(1 << 18, 1 << 18),
        name="finish",
    )(first.astype(I32).reshape(1), parts.reshape(160, 128), old_centroids)
    best_cosine = pl.pallas_call(
        match_kernel,
        out_shape=jax.ShapeDtypeStruct((2, 128), F32),
        in_specs=[SMEM, VMEM, VMEM],
        out_specs=VMEM,
        compiler_params=params(16),
        cost_estimate=cost(1 << 31, 5 << 20),
        name="match",
    )(slab_len, slab_rows.reshape(256, 1), gathered)
    return (centroids, best_cosine)


def solution(mesh):
    fine = Mesh(mesh.devices.reshape(SIZES), NAMES)
    dp, mp = ("zh", "zl", "x"), ("y", "c")
    placed = (
        P(dp + mp, None),
        P(dp + mp),
        P(dp, mp),
        P(dp + mp, None),
        P(dp + mp),
    )
    return jax.shard_map(
        local,
        mesh=fine,
        in_specs=placed,
        out_specs=(P(dp, mp), P(dp + mp, None)),
        check_vma=False,
    )
```

```python
import jax
import jax.numpy as jnp
from jax import lax
from jax.experimental import pallas as pl
from jax.experimental.pallas import tpu as pltpu
from jax.sharding import Mesh, PartitionSpec as P

F32, BF16, I32 = jnp.float32, jnp.bfloat16, jnp.int32
SIZES = (8, 4, 4, 4, 2)
NAMES = ("zh", "zl", "x", "y", "c")
BLOCK = 32
ROWS = 256
FEATS = 32
MSG = 80
MIB = 1 << 20


def params(mib):
    return pltpu.CompilerParams(vmem_limit_bytes=mib * MIB)


def cost(flops, moved):
    return pl.CostEstimate(flops=flops, bytes_accessed=moved, transcendentals=0)


def pack_kernel(emb_ref, label_ref, out_ref):
    turned = emb_ref[...].T
    c = label_ref[...]
    high = ((c >> 6) & 3) * 64 + (c >> 8) * 8 + ((c >> 4) & 3) * 2 + (c & 1)
    low = ((c >> 1) & 1) * 4 + ((c >> 2) & 3)
    row = lax.broadcasted_iota(I32, (16, 128), 0)
    codes = jnp.where(row == 0, high[0:1], 0)
    codes = jnp.where(row == 1, high[1:2], codes)
    codes = jnp.where(row == 2, low[0:1], codes)
    codes = jnp.where(row == 3, low[1:2], codes)
    codes = codes.astype(F32).astype(BF16)
    for x in range(4):
        for mp in range(8):
            d, f = x * 8 + mp, (mp * 4 + x) * FEATS
            out_ref[d, 0:32, :] = turned[f : f + FEATS, 0:128]
            out_ref[d, 32:64, :] = turned[f : f + FEATS, 128:256]
            out_ref[d, 64:80, :] = codes


def sum_kernel(msg_ref, out_ref, a_ref, b_ref, p_ref, q_ref):
    cluster = lax.broadcasted_iota(I32, (256, 128), 0)
    group = lax.broadcasted_iota(I32, (128, 128), 0)

    def build(s, carry):
        codes = msg_ref[s, 64:80, :].astype(F32).astype(I32)
        for t in range(2):
            high, low = codes[t : t + 1], codes[2 + t : 3 + t]
            at = pl.ds(pl.multiple_of(s * 256 + t * 128, 128), 128)
            a_ref[:, at] = jnp.where(cluster == high, 1.0, 0.0).astype(BF16)
            part = msg_ref[s, 32 * t : 32 * t + 32, :]
            for g in range(8):
                b_ref[32 * g : 32 * g + 32, at] = part * jnp.where(low == g, 1.0, 0.0).astype(BF16)
            within = ((high >> 1) & 7) * 16 + (low & 3) * 4 + (low >> 2) * 2 + (high & 1)
            p_ref[:, at] = jnp.where(cluster[0:16] == (high >> 4), 1.0, 0.0).astype(BF16)
            q_ref[:, at] = jnp.where(group == within, 1.0, 0.0).astype(BF16)
        return carry

    lax.fori_loop(0, BLOCK, build, 0)
    contract = (((1,), (1,)), ((), ()))
    sums = lax.dot_general(a_ref[...], b_ref[...], contract, preferred_element_type=F32)
    counts = lax.dot_general(p_ref[...], q_ref[...], contract, preferred_element_type=F32)
    for zl in range(4):
        out_ref[zl, 0:64, :] = sums[zl * 64 : zl * 64 + 64, 0:128]
        out_ref[zl, 64:128, :] = sums[zl * 64 : zl * 64 + 64, 128:256]
        out_ref[zl, 128:132, :] = counts[zl * 4 : zl * 4 + 4, :]
        out_ref[zl, 132:136, :] = jnp.zeros((4, 128), F32)


def regroup_kernel(in_ref, out_ref, s_ref):
    s_ref[...] = (in_ref[0] + in_ref[1]) + (in_ref[2] + in_ref[3])
    for m in range(32):
        out_ref[5 * m : 5 * m + 2, :] = s_ref[2 * m : 2 * m + 2, :]
        out_ref[5 * m + 2 : 5 * m + 4, :] = s_ref[64 + 2 * m : 66 + 2 * m, :]
        out_ref[5 * m + 4 : 5 * m + 5, :] = s_ref[128 + m // 8 : 129 + m // 8, :]


def finish_kernel(at_ref, in_ref, old_ref, out_ref):
    slot = lax.broadcasted_iota(I32, (4, 128), 1) // FEATS
    parts = []
    for x in range(4):
        total = in_ref[5 * x : 5 * x + 4, :]
        for zh in range(1, 8):
            m = zh * 4 + x
            total = total + in_ref[5 * m : 5 * m + 4, :]
        parts.append(total)
    count_row = in_ref[4:5, :]
    for zh in range(1, 8):
        count_row = count_row + in_ref[20 * zh + 4 : 20 * zh + 5, :]
    lane = lax.broadcasted_iota(I32, (16, 128), 1)
    own = lane == at_ref[0] + lax.broadcasted_iota(I32, (16, 128), 0)
    counts = jnp.sum(jnp.where(own, count_row, 0.0), axis=1, keepdims=True)
    for low in range(4):
        rows = jnp.zeros((4, 128), F32)
        for x in range(4):
            shift = ((x - low) * FEATS) % 128
            moved = pltpu.roll(parts[x], shift, 1) if shift else parts[x]
            rows = jnp.where(slot == x, moved, rows)
        j = slice(4 * low, 4 * low + 4)
        out_ref[j, :] = (rows + old_ref[j, :]) / (counts[j] + 1.0)


def match_kernel(place_ref, len_ref, rows_ref, own_ref, other_ref, out_ref):
    r = rows_ref[...]
    away = (r >> 9) ^ place_ref[1]
    away = jnp.where(away == 2, 3, jnp.where(away == 3, 2, away))
    at = (((r >> 8) & 1) ^ place_ref[0]) * 1024 + away * 256 + (r & 255)
    lane = lax.broadcasted_iota(I32, (256, 1024), 1)
    pick = jnp.where(lane == at, 1.0, 0.0).astype(BF16)
    members = jnp.dot(pick, own_ref[...], preferred_element_type=F32)
    pick = jnp.where(lane + 1024 == at, 1.0, 0.0).astype(BF16)
    members = members + jnp.dot(pick, other_ref[...], preferred_element_type=F32)
    members = members.astype(BF16)
    i = lax.broadcasted_iota(I32, (128, 128), 0)
    j = lax.broadcasted_iota(I32, (128, 128), 1)
    for s in range(2):
        one = members[128 * s : 128 * s + 128]
        gram = lax.dot_general(one, one, (((1,), (1,)), ((), ())), preferred_element_type=F32)
        diagonal = jnp.where(i == j, gram, 0.0)
        down = lax.rsqrt(jnp.sum(diagonal, axis=1, keepdims=True) + 1e-06)
        across = lax.rsqrt(jnp.sum(diagonal, axis=0, keepdims=True) + 1e-06)
        cosine = gram * down * across
        length = len_ref[s]
        largest = jnp.max(jnp.where((i < length) & (i != j), cosine, -2.0), axis=0, keepdims=True)
        out_ref[s : s + 1, :] = jnp.where(j[0:1] < length, largest, 0.0)


VMEM = pl.BlockSpec(memory_space=pltpu.VMEM)
SMEM = pl.BlockSpec(memory_space=pltpu.SMEM)


def local(embeddings, assignments, old_centroids, slab_rows, slab_len):
    messages = pl.pallas_call(
        pack_kernel,
        out_shape=jax.ShapeDtypeStruct((BLOCK, MSG, 128), BF16),
        in_specs=[VMEM, VMEM],
        out_specs=VMEM,
        compiler_params=params(8),
        cost_estimate=cost(1 << 20, 3 << 19),
        name="pack",
    )(embeddings, assignments.reshape(2, 128))
    line, messages = lax.optimization_barrier((embeddings, messages))
    line = [line] + [lax.ppermute(line, "y", [(i, i ^ d) for i in range(4)]) for d in (1, 3, 2)]
    messages = lax.all_to_all(messages, ("x", "y", "c"), 0, 0, tiled=True)
    parts = pl.pallas_call(
        sum_kernel,
        out_shape=jax.ShapeDtypeStruct((4, 136, 128), F32),
        in_specs=[VMEM],
        out_specs=VMEM,
        scratch_shapes=[
            pltpu.VMEM((256, 8192), BF16),
            pltpu.VMEM((256, 8192), BF16),
            pltpu.VMEM((16, 8192), BF16),
            pltpu.VMEM((128, 8192), BF16),
        ],
        compiler_params=params(20),
        cost_estimate=cost(1 << 31, 1 << 20),
        name="sums",
    )(messages)
    parts = lax.all_to_all(parts, "zl", 0, 0, tiled=True)
    parts = pl.pallas_call(
        regroup_kernel,
        out_shape=jax.ShapeDtypeStruct((160, 128), F32),
        in_specs=[VMEM],
        out_specs=VMEM,
        scratch_shapes=[pltpu.VMEM((136, 128), F32)],
        compiler_params=params(4),
        cost_estimate=cost(1 << 18, 1 << 19),
        name="regroup",
    )(parts)
    parts = lax.all_to_all(parts.reshape(32, 5, 1, 128), ("zh", "x"), 0, 0, tiled=True)
    own = jnp.concatenate(line)
    other = lax.ppermute(own, "c", [(0, 1), (1, 0)])
    place = jnp.stack([lax.axis_index("c"), lax.axis_index("y")]).astype(I32)
    best_cosine = pl.pallas_call(
        match_kernel,
        out_shape=jax.ShapeDtypeStruct((2, 128), F32),
        in_specs=[SMEM, SMEM, VMEM, VMEM, VMEM],
        out_specs=VMEM,
        compiler_params=params(16),
        cost_estimate=cost(1 << 31, 5 << 20),
        name="match",
    )(place, slab_len, slab_rows.reshape(256, 1), own, other)
    parts, best_cosine = lax.optimization_barrier((parts, best_cosine))
    first = ((lax.axis_index("zh") % 2) * 4 + lax.axis_index("x")) * 16
    centroids = pl.pallas_call(
        finish_kernel,
        out_shape=jax.ShapeDtypeStruct((16, 128), F32),
        in_specs=[SMEM, VMEM, VMEM],
        out_specs=VMEM,
        compiler_params=params(4),
        cost_estimate=cost(1 << 18, 1 << 18),
        name="finish",
    )(first.astype(I32).reshape(1), parts.reshape(160, 128), old_centroids)
    return (centroids, best_cosine)


def solution(mesh):
    fine = Mesh(mesh.devices.reshape(SIZES), NAMES)
    dp, mp = ("zh", "zl", "x"), ("y", "c")
    placed = (
        P(dp + mp, None),
        P(dp + mp),
        P(dp, mp),
        P(dp + mp, None),
        P(dp + mp),
    )
    return jax.shard_map(
        local,
        mesh=fine,
        in_specs=placed,
        out_specs=(P(dp, mp), P(dp + mp, None)),
        check_vma=False,
    )
```

```python
import jax
import jax.numpy as jnp
from jax import lax
from jax.experimental import pallas as pl
from jax.experimental.pallas import tpu as pltpu
from jax.sharding import Mesh, PartitionSpec as P

F32, BF16, I32 = jnp.float32, jnp.bfloat16, jnp.int32
SIZES = (8, 4, 4, 4, 2)
NAMES = ("zh", "zl", "x", "y", "c")
BLOCK = 32
ROWS = 256
FEATS = 32
MSG = 80
MIB = 1 << 20


def params(mib):
    return pltpu.CompilerParams(vmem_limit_bytes=mib * MIB)


def cost(flops, moved):
    return pl.CostEstimate(flops=flops, bytes_accessed=moved, transcendentals=0)


def pack_kernel(emb_ref, label_ref, out_ref):
    turned = emb_ref[...].T
    c = label_ref[...]
    high = ((c >> 6) & 3) * 64 + (c >> 8) * 8 + ((c >> 4) & 3) * 2 + (c & 1)
    low = ((c >> 1) & 1) * 4 + ((c >> 2) & 3)
    row = lax.broadcasted_iota(I32, (16, 128), 0)
    codes = jnp.where(row == 0, high[0:1], 0)
    codes = jnp.where(row == 1, high[1:2], codes)
    codes = jnp.where(row == 2, low[0:1], codes)
    codes = jnp.where(row == 3, low[1:2], codes)
    codes = codes.astype(F32).astype(BF16)
    for x in range(4):
        for mp in range(8):
            d, f = x * 8 + mp, (mp * 4 + x) * FEATS
            out_ref[d, 0:32, :] = turned[f : f + FEATS, 0:128]
            out_ref[d, 32:64, :] = turned[f : f + FEATS, 128:256]
            out_ref[d, 64:80, :] = codes


def sum_kernel(msg_ref, out_ref, a_ref, b_ref, p_ref, q_ref):
    cluster = lax.broadcasted_iota(I32, (256, 128), 0)
    group = lax.broadcasted_iota(I32, (128, 128), 0)

    def build(s, carry):
        codes = msg_ref[s, 64:80, :].astype(F32).astype(I32)
        for t in range(2):
            high, low = codes[t : t + 1], codes[2 + t : 3 + t]
            at = pl.ds(pl.multiple_of(s * 256 + t * 128, 128), 128)
            a_ref[:, at] = jnp.where(cluster == high, 1.0, 0.0).astype(BF16)
            part = msg_ref[s, 32 * t : 32 * t + 32, :]
            for g in range(8):
                b_ref[32 * g : 32 * g + 32, at] = part * jnp.where(low == g, 1.0, 0.0).astype(BF16)
            within = ((high >> 1) & 7) * 16 + (low & 3) * 4 + (low >> 2) * 2 + (high & 1)
            p_ref[:, at] = jnp.where(cluster[0:16] == (high >> 4), 1.0, 0.0).astype(BF16)
            q_ref[:, at] = jnp.where(group == within, 1.0, 0.0).astype(BF16)
        return carry

    lax.fori_loop(0, BLOCK, build, 0)
    contract = (((1,), (1,)), ((), ()))
    sums = lax.dot_general(a_ref[...], b_ref[...], contract, preferred_element_type=F32)
    counts = lax.dot_general(p_ref[...], q_ref[...], contract, preferred_element_type=F32)
    for zl in range(4):
        out_ref[zl, 0:64, :] = sums[zl * 64 : zl * 64 + 64, 0:128]
        out_ref[zl, 64:128, :] = sums[zl * 64 : zl * 64 + 64, 128:256]
        out_ref[zl, 128:132, :] = counts[zl * 4 : zl * 4 + 4, :]
        out_ref[zl, 132:136, :] = jnp.zeros((4, 128), F32)


def regroup_kernel(in_ref, out_ref, s_ref):
    s_ref[...] = (in_ref[0] + in_ref[1]) + (in_ref[2] + in_ref[3])
    for m in range(32):
        out_ref[5 * m : 5 * m + 2, :] = s_ref[2 * m : 2 * m + 2, :]
        out_ref[5 * m + 2 : 5 * m + 4, :] = s_ref[64 + 2 * m : 66 + 2 * m, :]
        out_ref[5 * m + 4 : 5 * m + 5, :] = s_ref[128 + m // 8 : 129 + m // 8, :]


def finish_kernel(at_ref, in_ref, old_ref, out_ref):
    slot = lax.broadcasted_iota(I32, (4, 128), 1) // FEATS
    parts = []
    for x in range(4):
        total = in_ref[5 * x : 5 * x + 4, :]
        for zh in range(1, 8):
            m = zh * 4 + x
            total = total + in_ref[5 * m : 5 * m + 4, :]
        parts.append(total)
    count_row = in_ref[4:5, :]
    for zh in range(1, 8):
        count_row = count_row + in_ref[20 * zh + 4 : 20 * zh + 5, :]
    lane = lax.broadcasted_iota(I32, (16, 128), 1)
    own = lane == at_ref[0] + lax.broadcasted_iota(I32, (16, 128), 0)
    counts = jnp.sum(jnp.where(own, count_row, 0.0), axis=1, keepdims=True)
    for low in range(4):
        rows = jnp.zeros((4, 128), F32)
        for x in range(4):
            shift = ((x - low) * FEATS) % 128
            moved = pltpu.roll(parts[x], shift, 1) if shift else parts[x]
            rows = jnp.where(slot == x, moved, rows)
        j = slice(4 * low, 4 * low + 4)
        out_ref[j, :] = (rows + old_ref[j, :]) / (counts[j] + 1.0)


def match_kernel(place_ref, len_ref, rows_ref, *refs):
    *line_refs, out_ref = refs
    r = rows_ref[...]
    away = (r >> 9) ^ place_ref[1]
    at = (away << 9) + ((((r >> 8) & 1) ^ place_ref[0]) << 8) + (r & 255)
    lane = lax.broadcasted_iota(I32, (256, 512), 1)
    members = jnp.zeros((256, 1024), F32)
    for away, line_ref in zip((0, 1, 3, 2), line_refs):
        pick = jnp.where(lane + 512 * away == at, 1.0, 0.0).astype(BF16)
        members = members + jnp.dot(pick, line_ref[...], preferred_element_type=F32)
    members = members.astype(BF16)
    i = lax.broadcasted_iota(I32, (128, 128), 0)
    j = lax.broadcasted_iota(I32, (128, 128), 1)
    for s in range(2):
        one = members[128 * s : 128 * s + 128]
        gram = lax.dot_general(one, one, (((1,), (1,)), ((), ())), preferred_element_type=F32)
        diagonal = jnp.where(i == j, gram, 0.0)
        down = lax.rsqrt(jnp.sum(diagonal, axis=1, keepdims=True) + 1e-06)
        across = lax.rsqrt(jnp.sum(diagonal, axis=0, keepdims=True) + 1e-06)
        cosine = gram * down * across
        length = len_ref[s]
        largest = jnp.max(jnp.where((i < length) & (i != j), cosine, -2.0), axis=0, keepdims=True)
        out_ref[s : s + 1, :] = jnp.where(j[0:1] < length, largest, 0.0)


VMEM = pl.BlockSpec(memory_space=pltpu.VMEM)
SMEM = pl.BlockSpec(memory_space=pltpu.SMEM)


def local(embeddings, assignments, old_centroids, slab_rows, slab_len):
    messages = pl.pallas_call(
        pack_kernel,
        out_shape=jax.ShapeDtypeStruct((BLOCK, MSG, 128), BF16),
        in_specs=[VMEM, VMEM],
        out_specs=VMEM,
        compiler_params=params(8),
        cost_estimate=cost(1 << 20, 3 << 19),
        name="pack",
    )(embeddings, assignments.reshape(2, 128))
    pair = jnp.concatenate([embeddings, lax.ppermute(embeddings, "c", [(0, 1), (1, 0)])])
    messages = lax.all_to_all(messages, ("x", "y", "c"), 0, 0, tiled=True)
    parts = pl.pallas_call(
        sum_kernel,
        out_shape=jax.ShapeDtypeStruct((4, 136, 128), F32),
        in_specs=[VMEM],
        out_specs=VMEM,
        scratch_shapes=[
            pltpu.VMEM((256, 8192), BF16),
            pltpu.VMEM((256, 8192), BF16),
            pltpu.VMEM((16, 8192), BF16),
            pltpu.VMEM((128, 8192), BF16),
        ],
        compiler_params=params(20),
        cost_estimate=cost(1 << 31, 1 << 20),
        name="sums",
    )(messages)
    pair, parts = lax.optimization_barrier((pair, parts))
    line = [pair] + [lax.ppermute(pair, "y", [(i, i ^ d) for i in range(4)]) for d in (1, 3, 2)]
    parts = lax.all_to_all(parts, "zl", 0, 0, tiled=True)
    parts = pl.pallas_call(
        regroup_kernel,
        out_shape=jax.ShapeDtypeStruct((160, 128), F32),
        in_specs=[VMEM],
        out_specs=VMEM,
        scratch_shapes=[pltpu.VMEM((136, 128), F32)],
        compiler_params=params(4),
        cost_estimate=cost(1 << 18, 1 << 19),
        name="regroup",
    )(parts)
    parts = lax.all_to_all(parts.reshape(32, 5, 1, 128), ("zh", "x"), 0, 0, tiled=True)
    place = jnp.stack([lax.axis_index("c"), lax.axis_index("y")]).astype(I32)
    best_cosine = pl.pallas_call(
        match_kernel,
        out_shape=jax.ShapeDtypeStruct((2, 128), F32),
        in_specs=[SMEM, SMEM] + [VMEM] * 5,
        out_specs=VMEM,
        compiler_params=params(16),
        cost_estimate=cost(1 << 31, 5 << 20),
        name="match",
    )(place, slab_len, slab_rows.reshape(256, 1), *line)
    parts, best_cosine = lax.optimization_barrier((parts, best_cosine))
    first = ((lax.axis_index("zh") % 2) * 4 + lax.axis_index("x")) * 16
    centroids = pl.pallas_call(
        finish_kernel,
        out_shape=jax.ShapeDtypeStruct((16, 128), F32),
        in_specs=[SMEM, VMEM, VMEM],
        out_specs=VMEM,
        compiler_params=params(4),
        cost_estimate=cost(1 << 18, 1 << 18),
        name="finish",
    )(first.astype(I32).reshape(1), parts.reshape(160, 128), old_centroids)
    return (centroids, best_cosine)


def solution(mesh):
    fine = Mesh(mesh.devices.reshape(SIZES), NAMES)
    dp, mp = ("zh", "zl", "x"), ("y", "c")
    placed = (
        P(dp + mp, None),
        P(dp + mp),
        P(dp, mp),
        P(dp + mp, None),
        P(dp + mp),
    )
    return jax.shard_map(
        local,
        mesh=fine,
        in_specs=placed,
        out_specs=(P(dp, mp), P(dp + mp, None)),
        check_vma=False,
    )
```

```python
import jax
import jax.numpy as jnp
from jax import lax
from jax.experimental import pallas as pl
from jax.experimental.pallas import tpu as pltpu
from jax.sharding import Mesh, PartitionSpec as P

F32, BF16, I32 = jnp.float32, jnp.bfloat16, jnp.int32
SIZES = (8, 4, 4, 4, 2)
NAMES = ("zh", "zl", "x", "y", "c")
BLOCK = 32
ROWS = 256
FEATS = 32
MSG = 80
MIB = 1 << 20


def params(mib):
    return pltpu.CompilerParams(vmem_limit_bytes=mib * MIB)


def cost(flops, moved):
    return pl.CostEstimate(flops=flops, bytes_accessed=moved, transcendentals=0)


def pack_kernel(emb_hbm, label_hbm, rows_hbm, out_ref, emb_ref, label_ref, rows_ref, sems):
    pairs = ((emb_hbm, emb_ref), (label_hbm, label_ref), (rows_hbm, rows_ref))
    copies = [pltpu.make_async_copy(a, b, sems.at[k]) for k, (a, b) in enumerate(pairs)]
    for copy in copies:
        copy.start()
    for copy in copies:
        copy.wait()
    turned = emb_ref[...].T
    c, r = label_ref[...], rows_ref[...]
    high = ((c >> 6) & 3) * 64 + (c >> 8) * 8 + ((c >> 4) & 3) * 2 + (c & 1)
    low = ((c >> 1) & 1) * 4 + ((c >> 2) & 3)
    row = lax.broadcasted_iota(I32, (16, 128), 0)
    codes = jnp.zeros((16, 128), I32)
    for k, pair in enumerate((high, low, r >> 3, r & 7)):
        codes = jnp.where(row == 2 * k, pair[0:1], codes)
        codes = jnp.where(row == 2 * k + 1, pair[1:2], codes)
    codes = codes.astype(F32).astype(BF16)
    for x in range(4):
        for mp in range(8):
            d, f = x * 8 + mp, (mp * 4 + x) * FEATS
            out_ref[d, 0:32, :] = turned[f : f + FEATS, 0:128]
            out_ref[d, 32:64, :] = turned[f : f + FEATS, 128:256]
            out_ref[d, 64:80, :] = codes


def lanes(n):
    return lax.broadcasted_iota(I32, (n, 128), 0).astype(F32).astype(BF16)


def sum_kernel(from_ref, msg_ref, out_ref, rows_ref):
    cluster = lanes(256)
    one, zero = jnp.ones((), BF16), jnp.zeros((), BF16)
    contract = (((1,), (1,)), ((), ()))
    sums = jnp.zeros((256, 256), F32)
    counts = jnp.zeros((16, 128), F32)
    for first in range(0, BLOCK, 4):
        a, b, p, q = [], [], [], []
        for s in range(first, first + 4):
            codes = msg_ref[s, 64:80, :]
            for t in range(2):
                high, low = codes[t : t + 1], codes[2 + t : 3 + t]
                part = msg_ref[s, 32 * t : 32 * t + 32, :]
                a.append(jnp.where(cluster == high, one, zero))
                b.append(jnp.concatenate([jnp.where(low == jnp.asarray(g, BF16), part, zero) for g in range(8)], 0))
                h, g = high.astype(F32).astype(I32), low.astype(F32).astype(I32)
                within = ((h >> 1) & 7) * 16 + (g & 3) * 4 + (g >> 2) * 2 + (h & 1)
                p.append(jnp.where(cluster[0:16] == (h >> 4).astype(F32).astype(BF16), one, zero))
                q.append(jnp.where(cluster[0:128] == within.astype(F32).astype(BF16), one, zero))
        a, b, p, q = (jnp.concatenate(blocks, 1) for blocks in (a, b, p, q))
        sums = sums + lax.dot_general(a, b, contract, preferred_element_type=F32)
        counts = counts + lax.dot_general(p, q, contract, preferred_element_type=F32)
    for zl in range(4):
        out_ref[zl, 0:64, :] = sums[zl * 64 : zl * 64 + 64, 0:128]
        out_ref[zl, 64:128, :] = sums[zl * 64 : zl * 64 + 64, 128:256]
        out_ref[zl, 128:132, :] = counts[zl * 4 : zl * 4 + 4, :]
        out_ref[zl, 132:136, :] = jnp.zeros((4, 128), F32)
    codes = msg_ref[from_ref[0], 64:80, :].astype(F32).astype(I32)
    rows_ref[...] = codes[4:6] * 8 + codes[6:8]


def regroup_kernel(in_ref, out_ref, s_ref):
    s_ref[...] = (in_ref[0] + in_ref[1]) + (in_ref[2] + in_ref[3])
    for m in range(32):
        out_ref[5 * m : 5 * m + 2, :] = s_ref[2 * m : 2 * m + 2, :]
        out_ref[5 * m + 2 : 5 * m + 4, :] = s_ref[64 + 2 * m : 66 + 2 * m, :]
        out_ref[5 * m + 4 : 5 * m + 5, :] = s_ref[128 + m // 8 : 129 + m // 8, :]


def finish_kernel(at_ref, in_ref, old_ref, out_ref):
    slot = lax.broadcasted_iota(I32, (4, 128), 1) // FEATS
    parts = []
    for x in range(4):
        total = in_ref[5 * x : 5 * x + 4, :]
        for zh in range(1, 8):
            m = zh * 4 + x
            total = total + in_ref[5 * m : 5 * m + 4, :]
        parts.append(total)
    count_row = in_ref[4:5, :]
    for zh in range(1, 8):
        count_row = count_row + in_ref[20 * zh + 4 : 20 * zh + 5, :]
    lane = lax.broadcasted_iota(I32, (16, 128), 1)
    own = lane == at_ref[0] + lax.broadcasted_iota(I32, (16, 128), 0)
    counts = jnp.sum(jnp.where(own, count_row, 0.0), axis=1, keepdims=True)
    for low in range(4):
        rows = jnp.zeros((4, 128), F32)
        for x in range(4):
            shift = ((x - low) * FEATS) % 128
            moved = pltpu.roll(parts[x], shift, 1) if shift else parts[x]
            rows = jnp.where(slot == x, moved, rows)
        j = slice(4 * low, 4 * low + 4)
        out_ref[j, :] = (rows + old_ref[j, :]) / (counts[j] + 1.0)


def member_kernel(place_ref, mine_ref, theirs_ref, *refs):
    *line_refs, own_ref, other_ref = refs
    core, y = place_ref[0], place_ref[1]
    lane = lax.broadcasted_iota(I32, (128, ROWS), 1)
    for out, r in ((own_ref, mine_ref[...]), (other_ref, theirs_ref[...])):
        at = jnp.where(((r >> 8) & 1) == core, (((r >> 9) ^ y) << 8) + (r & 255), -1)
        at = jnp.concatenate([at, jnp.zeros((6, 128), I32)], 0).astype(F32).T.astype(I32)
        for s in range(2):
            total = jnp.zeros((128, 1024), F32)
            for away, line_ref in zip((0, 1, 3, 2), line_refs):
                pick = jnp.where(lane + 256 * away == at[:, s : s + 1], 1.0, 0.0).astype(BF16)
                total = total + jnp.dot(pick, line_ref[...], preferred_element_type=F32)
            out[128 * s : 128 * s + 128, :] = total.astype(BF16)


def match_kernel(len_ref, own_ref, other_ref, out_ref):
    members = own_ref[...] + other_ref[...]
    i = lax.broadcasted_iota(I32, (128, 128), 0)
    j = lax.broadcasted_iota(I32, (128, 128), 1)
    for s in range(2):
        one = members[128 * s : 128 * s + 128]
        gram = lax.dot_general(one, one, (((1,), (1,)), ((), ())), preferred_element_type=F32)
        diagonal = jnp.where(i == j, gram, 0.0)
        down = lax.rsqrt(jnp.sum(diagonal, axis=1, keepdims=True) + 1e-06)
        across = lax.rsqrt(jnp.sum(diagonal, axis=0, keepdims=True) + 1e-06)
        cosine = gram * down * across
        length = len_ref[s]
        largest = jnp.max(jnp.where((i < length) & (i != j), cosine, -2.0), axis=0, keepdims=True)
        out_ref[s : s + 1, :] = jnp.where(j[0:1] < length, largest, 0.0)


VMEM = pl.BlockSpec(memory_space=pltpu.VMEM)
HBM = pl.BlockSpec(memory_space=pltpu.HBM)
SMEM = pl.BlockSpec(memory_space=pltpu.SMEM)


def local(embeddings, assignments, old_centroids, slab_rows, slab_len):
    zh, x, y, core = (lax.axis_index(name).astype(I32) for name in ("zh", "x", "y", "c"))
    messages = pl.pallas_call(
        pack_kernel,
        out_shape=pltpu.VMEM((BLOCK, MSG, 128), BF16),
        in_specs=[HBM] * 3,
        out_specs=VMEM,
        scratch_shapes=[
            pltpu.VMEM((ROWS, 1024), BF16),
            pltpu.VMEM((2, 128), I32),
            pltpu.VMEM((2, 128), I32),
            pltpu.SemaphoreType.DMA((3,)),
        ],
        compiler_params=params(8),
        cost_estimate=cost(1 << 20, 3 << 19),
        name="pack",
    )(*(pltpu.with_memory_space_constraint(a, pltpu.HBM) for a in (embeddings, assignments.reshape(2, 128), slab_rows)))
    messages = lax.all_to_all(messages, ("x", "y", "c"), 0, 0, tiled=True)
    parts, other_rows = pl.pallas_call(
        sum_kernel,
        out_shape=(pltpu.VMEM((4, 136, 128), F32), pltpu.VMEM((2, 128), I32)),
        in_specs=[SMEM, VMEM],
        out_specs=(VMEM, VMEM),
        compiler_params=params(20),
        cost_estimate=cost(1 << 31, 1 << 20),
        name="sums",
    )((x * 8 + y * 2 + 1 - core).reshape(1), messages)
    embeddings, parts = lax.optimization_barrier((embeddings, parts))
    line = [embeddings] + [lax.ppermute(embeddings, "y", [(i, i ^ d) for i in range(4)]) for d in (1, 3, 2)]
    parts = lax.all_to_all(parts, "zl", 0, 0, tiled=True)
    parts = pl.pallas_call(
        regroup_kernel,
        out_shape=pltpu.VMEM((160, 128), F32),
        in_specs=[VMEM],
        out_specs=VMEM,
        scratch_shapes=[pltpu.VMEM((136, 128), F32)],
        compiler_params=params(4),
        cost_estimate=cost(1 << 18, 1 << 19),
        name="regroup",
    )(parts)
    parts = lax.all_to_all(parts.reshape(32, 5, 1, 128), ("zh", "x"), 0, 0, tiled=True)
    members = jax.ShapeDtypeStruct((256, 1024), BF16)
    own, other = pl.pallas_call(
        member_kernel,
        out_shape=(members, members),
        in_specs=[SMEM] + [VMEM] * 6,
        out_specs=(VMEM, VMEM),
        compiler_params=params(16),
        cost_estimate=cost(1 << 31, 3 << 20),
        name="members",
    )(jnp.stack([core, y]), slab_rows, other_rows, *line)
    other = lax.ppermute(other, "c", [(0, 1), (1, 0)])
    best_cosine = pl.pallas_call(
        match_kernel,
        out_shape=jax.ShapeDtypeStruct((2, 128), F32),
        in_specs=[SMEM, VMEM, VMEM],
        out_specs=VMEM,
        compiler_params=params(8),
        cost_estimate=cost(1 << 20, 1 << 20),
        name="match",
    )(slab_len, own, other)
    parts, best_cosine = lax.optimization_barrier((parts, best_cosine))
    centroids = pl.pallas_call(
        finish_kernel,
        out_shape=jax.ShapeDtypeStruct((16, 128), F32),
        in_specs=[SMEM, VMEM, VMEM],
        out_specs=VMEM,
        compiler_params=params(4),
        cost_estimate=cost(1 << 18, 1 << 18),
        name="finish",
    )((((zh & 1) * 4 + x) * 16).reshape(1), parts.reshape(160, 128), old_centroids)
    return (centroids, best_cosine)


def solution(mesh):
    fine = Mesh(mesh.devices.reshape(SIZES), NAMES)
    dp, mp = ("zh", "zl", "x"), ("y", "c")
    placed = (
        P(dp + mp, None),
        P(dp + mp),
        P(dp, mp),
        P(dp + mp, None),
        P(dp + mp),
    )
    return jax.shard_map(
        local,
        mesh=fine,
        in_specs=placed,
        out_specs=(P(dp, mp), P(dp + mp, None)),
        check_vma=False,
    )
```

```python
import jax
import jax.numpy as jnp
from jax import lax
from jax.experimental import pallas as pl
from jax.experimental.pallas import tpu as pltpu
from jax.sharding import Mesh, PartitionSpec as P

F32, BF16, I32 = jnp.float32, jnp.bfloat16, jnp.int32
SIZES = (8, 4, 4, 4, 2)
NAMES = ("zh", "zl", "x", "y", "c")
BLOCK = 32
ROWS = 256
FEATS = 32
MSG = 80
MIB = 1 << 20


def params(mib):
    return pltpu.CompilerParams(vmem_limit_bytes=mib * MIB)


def cost(flops, moved):
    return pl.CostEstimate(flops=flops, bytes_accessed=moved, transcendentals=0)


def pack_kernel(emb_hbm, label_hbm, rows_hbm, out_hbm, emb_ref, label_ref, rows_ref, msg_ref, in_sems, out_sems, sems):
    small = [
        pltpu.make_async_copy(label_hbm, label_ref, sems.at[0]),
        pltpu.make_async_copy(rows_hbm, rows_ref, sems.at[1]),
    ]
    blocks = [
        pltpu.make_async_copy(emb_hbm.at[:, pl.ds(128 * mp, 128)], emb_ref.at[mp], in_sems.at[mp]) for mp in range(8)
    ]
    for copy in small + blocks:
        copy.start()
    for copy in small:
        copy.wait()
    c, r = label_ref[...], rows_ref[...]
    high = ((c >> 6) & 3) * 64 + ((c >> 4) & 3) * 16 + (c >> 8) * 2 + (c & 1)
    low = ((c >> 1) & 1) * 4 + ((c >> 2) & 3)
    row = lax.broadcasted_iota(I32, (16, 128), 0)
    codes = jnp.zeros((16, 128), I32)
    for k, pair in enumerate((high, low, r >> 3, r & 7)):
        codes = jnp.where(row == 2 * k, pair[0:1], codes)
        codes = jnp.where(row == 2 * k + 1, pair[1:2], codes)
    codes = codes.astype(F32).astype(BF16)
    sent = []
    for mp in range(8):
        blocks[mp].wait()
        turned = emb_ref[mp].T
        for x in range(4):
            part = turned[x * FEATS : x * FEATS + FEATS]
            msg_ref[mp, x, 0:32, :] = part[:, 0:128]
            msg_ref[mp, x, 32:64, :] = part[:, 128:256]
            msg_ref[mp, x, 64:80, :] = codes
        sent.append(pltpu.make_async_copy(msg_ref.at[mp], out_hbm.at[:, mp], out_sems.at[mp]))
        sent[mp].start()
    for copy in sent:
        copy.wait()


def lanes(n):
    return lax.broadcasted_iota(I32, (n, 128), 0).astype(F32).astype(BF16)


def sum_kernel(from_ref, msg_ref, out_ref, rows_ref):
    cluster = lanes(256)
    one, zero = jnp.ones((), BF16), jnp.zeros((), BF16)
    contract = (((1,), (1,)), ((), ()))
    sums = jnp.zeros((256, 256), F32)
    counts = jnp.zeros((16, 128), F32)
    for first in range(0, BLOCK, 4):
        a, b, p, q = [], [], [], []
        for s in range(first, first + 4):
            codes = msg_ref[s, 64:80, :]
            for t in range(2):
                high, low = codes[t : t + 1], codes[2 + t : 3 + t]
                part = msg_ref[s, 32 * t : 32 * t + 32, :]
                a.append(jnp.where(cluster == high, one, zero))
                b.append(jnp.concatenate([jnp.where(low == jnp.asarray(g, BF16), part, zero) for g in range(8)], 0))
                h, g = high.astype(F32).astype(I32), low.astype(F32).astype(I32)
                within = ((h >> 1) & 7) * 16 + (g & 3) * 4 + (g >> 2) * 2 + (h & 1)
                p.append(jnp.where(cluster[0:16] == (h >> 4).astype(F32).astype(BF16), one, zero))
                q.append(jnp.where(cluster[0:128] == within.astype(F32).astype(BF16), one, zero))
        a, b, p, q = (jnp.concatenate(blocks, 1) for blocks in (a, b, p, q))
        sums = sums + lax.dot_general(a, b, contract, preferred_element_type=F32)
        counts = counts + lax.dot_general(p, q, contract, preferred_element_type=F32)
    for m in range(16):
        out_ref[33 * m : 33 * m + 16, :] = sums[16 * m : 16 * m + 16, 0:128]
        out_ref[33 * m + 16 : 33 * m + 32, :] = sums[16 * m : 16 * m + 16, 128:256]
        out_ref[33 * m + 32 : 33 * m + 33, :] = counts[m : m + 1, :]
    codes = msg_ref[from_ref[0], 64:80, :].astype(F32).astype(I32)
    rows_ref[...] = codes[4:6] * 8 + codes[6:8]


def regroup_kernel(in_ref, out_ref, s_ref):
    slot = lax.broadcasted_iota(I32, (32, 128), 1) // FEATS
    parts = []
    for x in range(4):
        first, *others = (in_ref[33 * (4 * zl + x) : 33 * (4 * zl + x) + 32, :] for zl in range(4))
        parts.append((first + others[0]) + (others[1] + others[2]))
    first, *others = (in_ref[33 * 4 * zl + 32 : 33 * 4 * zl + 33, :] for zl in range(4))
    counts = (first + others[0]) + (others[1] + others[2])
    for low in range(4):
        rows = jnp.zeros((32, 128), F32)
        for x in range(4):
            shift = ((x - low) * FEATS) % 128
            moved = pltpu.roll(parts[x], shift, 1) if shift else parts[x]
            rows = jnp.where(slot == x, moved, rows)
        s_ref[...] = rows
        for zh in range(8):
            for r1 in range(2):
                at = 17 * zh + 4 * low + 2 * r1
                out_ref[at : at + 2, :] = s_ref[16 * r1 + 2 * zh : 16 * r1 + 2 * zh + 2, :]
    for zh in range(8):
        out_ref[17 * zh + 16 : 17 * zh + 17, :] = counts


def finish_kernel(at_ref, in_ref, old_ref, out_ref):
    sums, count_row = in_ref[0:16, :], in_ref[16:17, :]
    for zh in range(1, 8):
        sums = sums + in_ref[17 * zh : 17 * zh + 16, :]
        count_row = count_row + in_ref[17 * zh + 16 : 17 * zh + 17, :]
    lane = lax.broadcasted_iota(I32, (16, 128), 1)
    own = lane == at_ref[0] + lax.broadcasted_iota(I32, (16, 128), 0)
    counts = jnp.sum(jnp.where(own, count_row, 0.0), axis=1, keepdims=True)
    out_ref[...] = (sums + old_ref[...]) / (counts + 1.0)


def member_kernel(after_ref, place_ref, mine_ref, theirs_ref, *refs):
    *line_refs, own_ref, first_ref, second_ref = refs
    core, y = place_ref[0], place_ref[1]
    lane = lax.broadcasted_iota(I32, (128, ROWS), 1)
    outs = (own_ref.at[0:128], own_ref.at[128:256], first_ref, second_ref)
    for k, r in enumerate((mine_ref[...], theirs_ref[...])):
        at = jnp.where(((r >> 8) & 1) == core, (((r >> 9) ^ y) << 8) + (r & 255), -1)
        at = jnp.concatenate([at, jnp.zeros((6, 128), I32)], 0).astype(F32).T.astype(I32)
        for s in range(2):
            total = jnp.zeros((128, 1024), F32)
            for away, line_ref in zip((0, 1, 3, 2), line_refs):
                pick = jnp.where(lane + 256 * away == at[:, s : s + 1], 1.0, 0.0).astype(BF16)
                total = total + jnp.dot(pick, line_ref[...], preferred_element_type=F32)
            outs[2 * k + s][...] = total.astype(BF16)


def match_kernel(len_ref, own_ref, first_ref, second_ref, out_ref):
    i = lax.broadcasted_iota(I32, (128, 128), 0)
    j = lax.broadcasted_iota(I32, (128, 128), 1)
    for s, other_ref in enumerate((first_ref, second_ref)):
        one = own_ref[128 * s : 128 * s + 128, :] + other_ref[...]
        gram = lax.dot_general(one, one, (((1,), (1,)), ((), ())), preferred_element_type=F32)
        diagonal = jnp.where(i == j, gram, 0.0)
        down = lax.rsqrt(jnp.sum(diagonal, axis=1, keepdims=True) + 1e-06)
        across = lax.rsqrt(jnp.sum(diagonal, axis=0, keepdims=True) + 1e-06)
        cosine = gram * down * across
        length = len_ref[s]
        largest = jnp.max(jnp.where((i < length) & (i != j), cosine, -2.0), axis=0, keepdims=True)
        out_ref[s : s + 1, :] = jnp.where(j[0:1] < length, largest, 0.0)


VMEM = pl.BlockSpec(memory_space=pltpu.VMEM)
HBM = pl.BlockSpec(memory_space=pltpu.HBM)
SMEM = pl.BlockSpec(memory_space=pltpu.SMEM)


def local(embeddings, assignments, old_centroids, slab_rows, slab_len):
    zh, x, y, core = (lax.axis_index(name).astype(I32) for name in ("zh", "x", "y", "c"))
    messages = pl.pallas_call(
        pack_kernel,
        out_shape=pltpu.HBM((4, 8, MSG, 128), BF16),
        in_specs=[HBM] * 3,
        out_specs=HBM,
        scratch_shapes=[
            pltpu.VMEM((8, ROWS, 128), BF16),
            pltpu.VMEM((2, 128), I32),
            pltpu.VMEM((2, 128), I32),
            pltpu.VMEM((8, 4, MSG, 128), BF16),
            pltpu.SemaphoreType.DMA((8,)),
            pltpu.SemaphoreType.DMA((8,)),
            pltpu.SemaphoreType.DMA((2,)),
        ],
        compiler_params=params(8),
        cost_estimate=cost(1 << 20, 3 << 19),
        name="pack",
    )(*(pltpu.with_memory_space_constraint(a, pltpu.HBM) for a in (embeddings, assignments.reshape(2, 128), slab_rows)))
    messages = lax.all_to_all(messages.reshape(BLOCK, MSG, 128), ("x", "y", "c"), 0, 0, tiled=True)
    parts, other_rows = pl.pallas_call(
        sum_kernel,
        out_shape=(pltpu.VMEM((528, 128), F32), pltpu.VMEM((2, 128), I32)),
        in_specs=[SMEM, VMEM],
        out_specs=(VMEM, VMEM),
        compiler_params=params(20),
        cost_estimate=cost(1 << 31, 1 << 20),
        name="sums",
    )((x * 8 + y * 2 + 1 - core).reshape(1), messages)
    embeddings, parts = lax.optimization_barrier((embeddings, parts))
    line = [embeddings] + [lax.ppermute(embeddings, "y", [(i, i ^ d) for i in range(4)]) for d in (1, 3, 2)]
    parts = lax.all_to_all(parts.reshape(16, 33, 1, 128), ("zl", "x"), 0, 0, tiled=True)
    parts = pl.pallas_call(
        regroup_kernel,
        out_shape=pltpu.VMEM((136, 128), F32),
        in_specs=[VMEM],
        out_specs=VMEM,
        scratch_shapes=[pltpu.VMEM((32, 128), F32)],
        compiler_params=params(4),
        cost_estimate=cost(1 << 18, 1 << 19),
        name="regroup",
    )(parts.reshape(528, 128))
    after = parts
    parts = lax.all_to_all(parts.reshape(8, 17, 1, 128), "zh", 0, 0, tiled=True)
    members = [jax.ShapeDtypeStruct((n, 1024), BF16) for n in (256, 128, 128)]
    own, *others = pl.pallas_call(
        member_kernel,
        out_shape=members,
        in_specs=[pl.BlockSpec(memory_space=pl.ANY), SMEM] + [VMEM] * 6,
        out_specs=[VMEM] * 3,
        compiler_params=params(16),
        cost_estimate=cost(0, 0),
        name="members",
    )(after, jnp.stack([core, y]), slab_rows, other_rows, *line)
    others = [lax.ppermute(other, "c", [(0, 1), (1, 0)]) for other in others]
    best_cosine = pl.pallas_call(
        match_kernel,
        out_shape=jax.ShapeDtypeStruct((2, 128), F32),
        in_specs=[SMEM] + [VMEM] * 3,
        out_specs=VMEM,
        compiler_params=params(8),
        cost_estimate=cost(0, 0),
        name="match",
    )(slab_len, own, *others)
    parts, best_cosine = lax.optimization_barrier((parts, best_cosine))
    centroids = pl.pallas_call(
        finish_kernel,
        out_shape=jax.ShapeDtypeStruct((16, 128), F32),
        in_specs=[SMEM, VMEM, VMEM],
        out_specs=VMEM,
        compiler_params=params(4),
        cost_estimate=cost(1 << 18, 1 << 18),
        name="finish",
    )((zh * 16).reshape(1), parts.reshape(136, 128), old_centroids)
    return (centroids, best_cosine)


def solution(mesh):
    fine = Mesh(mesh.devices.reshape(SIZES), NAMES)
    dp, mp = ("zh", "zl", "x"), ("y", "c")
    placed = (
        P(dp + mp, None),
        P(dp + mp),
        P(dp, mp),
        P(dp + mp, None),
        P(dp + mp),
    )
    return jax.shard_map(
        local,
        mesh=fine,
        in_specs=placed,
        out_specs=(P(dp, mp), P(dp + mp, None)),
        check_vma=False,
    )
```

```python
import jax
import jax.numpy as jnp
from jax import lax
from jax.experimental import pallas as pl
from jax.experimental.pallas import tpu as pltpu
from jax.sharding import Mesh, PartitionSpec as P

F32, BF16, I32 = jnp.float32, jnp.bfloat16, jnp.int32
SIZES = (8, 4, 4, 4, 2)
NAMES = ("zh", "zl", "x", "y", "c")
BLOCK = 32
ROWS = 256
FEATS = 32
MSG = 80
MIB = 1 << 20
RING = [4, 5, 6, 7, 0, 1, 2, 3]


def params(mib):
    return pltpu.CompilerParams(vmem_limit_bytes=mib * MIB)


def cost(flops, moved):
    return pl.CostEstimate(flops=flops, bytes_accessed=moved, transcendentals=0)


def pack_kernel(emb_hbm, label_hbm, rows_hbm, out_hbm, emb_ref, label_ref, rows_ref, msg_ref, in_sems, out_sems, sems):
    small = [
        pltpu.make_async_copy(label_hbm, label_ref, sems.at[0]),
        pltpu.make_async_copy(rows_hbm, rows_ref, sems.at[1]),
    ]
    blocks = [
        pltpu.make_async_copy(emb_hbm.at[:, pl.ds(128 * mp, 128)], emb_ref.at[mp], in_sems.at[mp]) for mp in range(8)
    ]
    for copy in small + blocks:
        copy.start()
    for copy in small:
        copy.wait()
    c, r = label_ref[...], rows_ref[...]
    high = ((c >> 6) & 3) * 64 + ((c >> 4) & 3) * 16 + (c >> 8) * 2 + (c & 1)
    low = ((c >> 1) & 1) * 4 + ((c >> 2) & 3)
    row = lax.broadcasted_iota(I32, (16, 128), 0)
    codes = jnp.zeros((16, 128), I32)
    for k, pair in enumerate((high, low, r >> 3, r & 7)):
        codes = jnp.where(row == 2 * k, pair[0:1], codes)
        codes = jnp.where(row == 2 * k + 1, pair[1:2], codes)
    codes = codes.astype(F32).astype(BF16)
    sent = []
    for mp in range(8):
        blocks[mp].wait()
        turned = emb_ref[mp].T
        for x in range(4):
            part = turned[x * FEATS : x * FEATS + FEATS]
            msg_ref[mp, x, 0:32, :] = part[:, 0:128]
            msg_ref[mp, x, 32:64, :] = part[:, 128:256]
            msg_ref[mp, x, 64:80, :] = codes
        sent.append(pltpu.make_async_copy(msg_ref.at[mp], out_hbm.at[:, mp], out_sems.at[mp]))
        sent[mp].start()
    for copy in sent:
        copy.wait()


def lanes(n):
    return lax.broadcasted_iota(I32, (n, 128), 0).astype(F32).astype(BF16)


def sum_kernel(from_ref, msg_ref, out_ref, rows_ref):
    cluster = lanes(256)
    one, zero = jnp.ones((), BF16), jnp.zeros((), BF16)
    contract = (((1,), (1,)), ((), ()))
    sums = jnp.zeros((256, 256), F32)
    counts = jnp.zeros((16, 128), F32)
    for first in range(0, BLOCK, 4):
        a, b, p, q = [], [], [], []
        for s in range(first, first + 4):
            codes = msg_ref[s, 64:80, :]
            for t in range(2):
                high, low = codes[t : t + 1], codes[2 + t : 3 + t]
                part = msg_ref[s, 32 * t : 32 * t + 32, :]
                a.append(jnp.where(cluster == high, one, zero))
                b.append(jnp.concatenate([jnp.where(low == jnp.asarray(g, BF16), part, zero) for g in range(8)], 0))
                h, g = high.astype(F32).astype(I32), low.astype(F32).astype(I32)
                within = ((h >> 1) & 7) * 16 + (g & 3) * 4 + (g >> 2) * 2 + (h & 1)
                p.append(jnp.where(cluster[0:16] == (h >> 4).astype(F32).astype(BF16), one, zero))
                q.append(jnp.where(cluster[0:128] == within.astype(F32).astype(BF16), one, zero))
        a, b, p, q = (jnp.concatenate(blocks, 1) for blocks in (a, b, p, q))
        sums = sums + lax.dot_general(a, b, contract, preferred_element_type=F32)
        counts = counts + lax.dot_general(p, q, contract, preferred_element_type=F32)
    for m in range(16):
        out_ref[33 * m : 33 * m + 16, :] = sums[16 * m : 16 * m + 16, 0:128]
        out_ref[33 * m + 16 : 33 * m + 32, :] = sums[16 * m : 16 * m + 16, 128:256]
        out_ref[33 * m + 32 : 33 * m + 33, :] = counts[m : m + 1, :]
    codes = msg_ref[from_ref[0], 64:80, :].astype(F32).astype(I32)
    rows_ref[...] = codes[4:6] * 8 + codes[6:8]


def regroup_kernel(in_ref, out_ref, s_ref):
    slot = lax.broadcasted_iota(I32, (32, 128), 1) // FEATS
    parts = []
    for x in range(4):
        first, *others = (in_ref[33 * (4 * zl + x) : 33 * (4 * zl + x) + 32, :] for zl in range(4))
        parts.append((first + others[0]) + (others[1] + others[2]))
    first, *others = (in_ref[33 * 4 * zl + 32 : 33 * 4 * zl + 33, :] for zl in range(4))
    counts = (first + others[0]) + (others[1] + others[2])
    for low in range(4):
        rows = jnp.zeros((32, 128), F32)
        for x in range(4):
            shift = ((x - low) * FEATS) % 128
            moved = pltpu.roll(parts[x], shift, 1) if shift else parts[x]
            rows = jnp.where(slot == x, moved, rows)
        s_ref[...] = rows
        for zh in range(8):
            for r1 in range(2):
                at = 17 * RING.index(zh) + 4 * low + 2 * r1
                out_ref[at : at + 2, :] = s_ref[16 * r1 + 2 * zh : 16 * r1 + 2 * zh + 2, :]
    for zh in range(8):
        at = 17 * zh + 16
        out_ref[at : at + 1, :] = counts


def finish_kernel(at_ref, in_ref, old_ref, out_ref):
    sums, count_row = in_ref[0:16, :], in_ref[16:17, :]
    for zh in range(1, 8):
        sums = sums + in_ref[17 * zh : 17 * zh + 16, :]
        count_row = count_row + in_ref[17 * zh + 16 : 17 * zh + 17, :]
    lane = lax.broadcasted_iota(I32, (16, 128), 1)
    own = lane == at_ref[0] + lax.broadcasted_iota(I32, (16, 128), 0)
    counts = jnp.sum(jnp.where(own, count_row, 0.0), axis=1, keepdims=True)
    out_ref[...] = (sums + old_ref[...]) / (counts + 1.0)


def member_kernel(after_ref, place_ref, mine_ref, theirs_ref, *refs):
    *line_refs, own_ref, first_ref, second_ref = refs
    core, y = place_ref[0], place_ref[1]
    lane = lax.broadcasted_iota(I32, (128, ROWS), 1)
    outs = (own_ref.at[0:128], own_ref.at[128:256], first_ref, second_ref)
    for k, r in enumerate((mine_ref[...], theirs_ref[...])):
        at = jnp.where(((r >> 8) & 1) == core, (((r >> 9) ^ y) << 8) + (r & 255), -1)
        at = jnp.concatenate([at, jnp.zeros((6, 128), I32)], 0).astype(F32).T.astype(I32)
        for s in range(2):
            total = jnp.zeros((128, 1024), F32)
            for away, line_ref in zip((0, 1, 3, 2), line_refs):
                pick = jnp.where(lane + 256 * away == at[:, s : s + 1], 1.0, 0.0).astype(BF16)
                total = total + jnp.dot(pick, line_ref[...], preferred_element_type=F32)
            outs[2 * k + s][...] = total.astype(BF16)


def match_kernel(len_ref, own_ref, first_ref, second_ref, out_ref):
    i = lax.broadcasted_iota(I32, (128, 128), 0)
    j = lax.broadcasted_iota(I32, (128, 128), 1)
    for s, other_ref in enumerate((first_ref, second_ref)):
        one = own_ref[128 * s : 128 * s + 128, :] + other_ref[...]
        gram = lax.dot_general(one, one, (((1,), (1,)), ((), ())), preferred_element_type=F32)
        diagonal = jnp.where(i == j, gram, 0.0)
        down = lax.rsqrt(jnp.sum(diagonal, axis=1, keepdims=True) + 1e-06)
        across = lax.rsqrt(jnp.sum(diagonal, axis=0, keepdims=True) + 1e-06)
        cosine = gram * down * across
        length = len_ref[s]
        largest = jnp.max(jnp.where((i < length) & (i != j), cosine, -2.0), axis=0, keepdims=True)
        out_ref[s : s + 1, :] = jnp.where(j[0:1] < length, largest, 0.0)


VMEM = pl.BlockSpec(memory_space=pltpu.VMEM)
HBM = pl.BlockSpec(memory_space=pltpu.HBM)
SMEM = pl.BlockSpec(memory_space=pltpu.SMEM)


def local(embeddings, assignments, old_centroids, slab_rows, slab_len):
    zh, x, y, core = (lax.axis_index(name).astype(I32) for name in ("zh", "x", "y", "c"))
    messages = pl.pallas_call(
        pack_kernel,
        out_shape=pltpu.HBM((4, 8, MSG, 128), BF16),
        in_specs=[HBM] * 3,
        out_specs=HBM,
        scratch_shapes=[
            pltpu.VMEM((8, ROWS, 128), BF16),
            pltpu.VMEM((2, 128), I32),
            pltpu.VMEM((2, 128), I32),
            pltpu.VMEM((8, 4, MSG, 128), BF16),
            pltpu.SemaphoreType.DMA((8,)),
            pltpu.SemaphoreType.DMA((8,)),
            pltpu.SemaphoreType.DMA((2,)),
        ],
        compiler_params=params(8),
        cost_estimate=cost(1 << 20, 3 << 19),
        name="pack",
    )(*(pltpu.with_memory_space_constraint(a, pltpu.HBM) for a in (embeddings, assignments.reshape(2, 128), slab_rows)))
    messages = lax.all_to_all(messages.reshape(BLOCK, MSG, 128), ("x", "y", "c"), 0, 0, tiled=True)
    parts, other_rows = pl.pallas_call(
        sum_kernel,
        out_shape=(pltpu.VMEM((528, 128), F32), pltpu.VMEM((2, 128), I32)),
        in_specs=[SMEM, VMEM],
        out_specs=(VMEM, VMEM),
        compiler_params=params(20),
        cost_estimate=cost(1 << 31, 1 << 20),
        name="sums",
    )((x * 8 + y * 2 + 1 - core).reshape(1), messages)
    embeddings, parts = lax.optimization_barrier((embeddings, parts))
    line = [embeddings] + [lax.ppermute(embeddings, "y", [(i, i ^ d) for i in range(4)]) for d in (1, 3, 2)]
    parts = lax.all_to_all(parts.reshape(16, 33, 1, 128), ("zl", "x"), 0, 0, tiled=True)
    parts = pl.pallas_call(
        regroup_kernel,
        out_shape=pltpu.VMEM((136, 128), F32),
        in_specs=[VMEM],
        out_specs=VMEM,
        scratch_shapes=[pltpu.VMEM((32, 128), F32)],
        compiler_params=params(4),
        cost_estimate=cost(1 << 18, 1 << 19),
        name="regroup",
    )(parts.reshape(528, 128))
    after = parts
    parts = lax.all_to_all(parts.reshape(8, 17, 1, 128), "zh", 0, 0, axis_index_groups=[RING], tiled=True)
    members = [jax.ShapeDtypeStruct((n, 1024), BF16) for n in (256, 128, 128)]
    own, *others = pl.pallas_call(
        member_kernel,
        out_shape=members,
        in_specs=[pl.BlockSpec(memory_space=pl.ANY), SMEM] + [VMEM] * 6,
        out_specs=[VMEM] * 3,
        compiler_params=params(16),
        cost_estimate=cost(0, 0),
        name="members",
    )(after, jnp.stack([core, y]), slab_rows, other_rows, *line)
    others = [lax.ppermute(other, "c", [(0, 1), (1, 0)]) for other in others]
    best_cosine = pl.pallas_call(
        match_kernel,
        out_shape=jax.ShapeDtypeStruct((2, 128), F32),
        in_specs=[SMEM] + [VMEM] * 3,
        out_specs=VMEM,
        compiler_params=params(8),
        cost_estimate=cost(0, 0),
        name="match",
    )(slab_len, own, *others)
    parts, best_cosine = lax.optimization_barrier((parts, best_cosine))
    centroids = pl.pallas_call(
        finish_kernel,
        out_shape=jax.ShapeDtypeStruct((16, 128), F32),
        in_specs=[SMEM, VMEM, VMEM],
        out_specs=VMEM,
        compiler_params=params(4),
        cost_estimate=cost(1 << 18, 1 << 18),
        name="finish",
    )((zh * 16).reshape(1), parts.reshape(136, 128), old_centroids)
    return (centroids, best_cosine)


def solution(mesh):
    fine = Mesh(mesh.devices.reshape(SIZES), NAMES)
    dp, mp = ("zh", "zl", "x"), ("y", "c")
    placed = (
        P(dp + mp, None),
        P(dp + mp),
        P(dp, mp),
        P(dp + mp, None),
        P(dp + mp),
    )
    return jax.shard_map(
        local,
        mesh=fine,
        in_specs=placed,
        out_specs=(P(dp, mp), P(dp + mp, None)),
        check_vma=False,
    )
```

```python
import functools

import jax
import jax.numpy as jnp
from jax import lax
from jax.experimental import pallas as pl
from jax.experimental.pallas import tpu as pltpu
from jax.sharding import Mesh, PartitionSpec as P

F32, BF16, I32 = jnp.float32, jnp.bfloat16, jnp.int32
SIZES = (8, 4, 4, 4, 2)
NAMES = ("zh", "zl", "x", "y", "c")
BLOCK = 32
ROWS = 256
FEATS = 32
MSG = 80
MIB = 1 << 20
FIRST = (2, 4)
BLOCK_ORDER = [k ^ 20 for k in range(BLOCK)]
FIRST_ZL = 1
PLANE_ORDER = [k ^ (4 * FIRST_ZL) for k in range(16)]
FIRST_ZH = 4
RING_ORDER = [k ^ FIRST_ZH for k in range(8)]


def params(mib):
    return pltpu.CompilerParams(vmem_limit_bytes=mib * MIB)


def cost(flops, moved):
    return pl.CostEstimate(flops=flops, bytes_accessed=moved, transcendentals=0)


def pack_kernel(emb_hbm, label_hbm, rows_hbm, out_hbm, emb_ref, label_ref, rows_ref, msg_ref, in_sems, out_sems, sems):
    small = [
        pltpu.make_async_copy(label_hbm, label_ref, sems.at[0]),
        pltpu.make_async_copy(rows_hbm, rows_ref, sems.at[1]),
    ]
    halves = [pl.ds(0, 512), pl.ds(512, 512)]
    blocks = [pltpu.make_async_copy(emb_hbm.at[:, at], emb_ref.at[:, at], in_sems.at[k]) for k, at in enumerate(halves)]
    for copy in blocks + small:
        copy.start()
    for copy in small:
        copy.wait()
    c, r = label_ref[...], rows_ref[...]
    high = ((c >> 6) & 3) * 64 + ((c >> 4) & 3) * 16 + (c >> 8) * 2 + (c & 1)
    low = ((c >> 1) & 1) * 4 + ((c >> 2) & 3)
    row = lax.broadcasted_iota(I32, (16, 128), 0)
    codes = jnp.zeros((16, 128), I32)
    for k, pair in enumerate((high, low, r >> 3, r & 7)):
        codes = jnp.where(row == 2 * k, pair[0:1], codes)
        codes = jnp.where(row == 2 * k + 1, pair[1:2], codes)
    codes = codes.astype(F32).astype(BF16)
    sent = []
    for k in range(2):
        blocks[k].wait()
        for mp in range(4 * k, 4 * k + 4):
            turned = emb_ref[:, 128 * mp : 128 * mp + 128].T
            for x in range(4):
                part, at = turned[x * FEATS : x * FEATS + FEATS], (x ^ FIRST[0], mp ^ FIRST[1])
                msg_ref[*at, 0:32, :] = part[:, 0:128]
                msg_ref[*at, 32:64, :] = part[:, 128:256]
                msg_ref[*at, 64:80, :] = codes
        at = pl.ds((4 * k) ^ FIRST[1], 4)
        sent.append(pltpu.make_async_copy(msg_ref.at[:, at], out_hbm.at[:, at], out_sems.at[k]))
        sent[k].start()
    for copy in sent:
        copy.wait()


def lanes(n):
    return lax.broadcasted_iota(I32, (n, 128), 0).astype(F32).astype(BF16)


def sum_kernel(from_ref, msg_ref, out_ref, rows_ref):
    cluster = lanes(256)
    one, zero = jnp.ones((), BF16), jnp.zeros((), BF16)
    contract = (((1,), (1,)), ((), ()))
    sums = jnp.zeros((256, 256), F32)
    counts = jnp.zeros((16, 128), F32)
    for first in range(0, BLOCK, 4):
        a, b, p, q = [], [], [], []
        for s in range(first, first + 4):
            codes = msg_ref[s, 64:80, :]
            for t in range(2):
                high, low = codes[t : t + 1], codes[2 + t : 3 + t]
                part = msg_ref[s, 32 * t : 32 * t + 32, :]
                a.append(jnp.where(cluster == high, one, zero))
                b.append(jnp.concatenate([jnp.where(low == jnp.asarray(g, BF16), part, zero) for g in range(8)], 0))
                h, g = high.astype(F32).astype(I32), low.astype(F32).astype(I32)
                within = ((h >> 1) & 7) * 16 + (g & 3) * 4 + (g >> 2) * 2 + (h & 1)
                p.append(jnp.where(cluster[0:16] == (h >> 4).astype(F32).astype(BF16), one, zero))
                q.append(jnp.where(cluster[0:128] == within.astype(F32).astype(BF16), one, zero))
        a, b, p, q = (jnp.concatenate(blocks, 1) for blocks in (a, b, p, q))
        sums = sums + lax.dot_general(a, b, contract, preferred_element_type=F32)
        counts = counts + lax.dot_general(p, q, contract, preferred_element_type=F32)
    for m in range(16):
        at = 33 * PLANE_ORDER[m]
        out_ref[at : at + 16, :] = sums[16 * m : 16 * m + 16, 0:128]
        out_ref[at + 16 : at + 32, :] = sums[16 * m : 16 * m + 16, 128:256]
        out_ref[at + 32 : at + 33, :] = counts[m : m + 1, :]
    for k in range(2):
        codes = msg_ref[from_ref[0] ^ k, 64:80, :].astype(F32).astype(I32)
        rows_ref[2 * k : 2 * k + 2, :] = codes[4:6] * 8 + codes[6:8]


def regroup_kernel(in_ref, out_ref, s_ref):
    slot = lax.broadcasted_iota(I32, (32, 128), 1) // FEATS
    parts = []
    for x in range(4):
        first, *others = (in_ref[33 * (4 * zl + x) : 33 * (4 * zl + x) + 32, :] for zl in range(4))
        parts.append((first + others[0]) + (others[1] + others[2]))
    first, *others = (in_ref[33 * 4 * zl + 32 : 33 * 4 * zl + 33, :] for zl in range(4))
    counts = (first + others[0]) + (others[1] + others[2])
    for low in range(4):
        rows = jnp.zeros((32, 128), F32)
        for x in range(4):
            shift = ((x - low) * FEATS) % 128
            moved = pltpu.roll(parts[x], shift, 1) if shift else parts[x]
            rows = jnp.where(slot == x, moved, rows)
        s_ref[...] = rows
        for zh in range(8):
            for r1 in range(2):
                at = 17 * (zh ^ FIRST_ZH) + 4 * low + 2 * r1
                out_ref[at : at + 2, :] = s_ref[16 * r1 + 2 * zh : 16 * r1 + 2 * zh + 2, :]
    for zh in range(8):
        at = 17 * zh + 16
        out_ref[at : at + 1, :] = counts


def finish_kernel(at_ref, in_ref, old_ref, out_ref):
    sums, count_row = in_ref[0:16, :], in_ref[16:17, :]
    for zh in range(1, 8):
        sums = sums + in_ref[17 * zh : 17 * zh + 16, :]
        count_row = count_row + in_ref[17 * zh + 16 : 17 * zh + 17, :]
    lane = lax.broadcasted_iota(I32, (16, 128), 1)
    own = lane == at_ref[0] + lax.broadcasted_iota(I32, (16, 128), 0)
    counts = jnp.sum(jnp.where(own, count_row, 0.0), axis=1, keepdims=True)
    out_ref[...] = (sums + old_ref[...]) / (counts + 1.0)


def member_kernel(of, after_ref, place_ref, rows_ref, *refs):
    line_refs, out_refs = refs[:4], refs[4:]
    core, y = place_ref[0], place_ref[1]
    lane = lax.broadcasted_iota(I32, (128, ROWS), 1)
    r = rows_ref[2 * of : 2 * of + 2, :]
    at = jnp.where(((r >> 8) & 1) == core, (((r >> 9) ^ y) << 8) + (r & 255), -1)
    at = jnp.concatenate([at, jnp.zeros((6, 128), I32)], 0).astype(F32).T.astype(I32)
    for s, out_ref in enumerate(out_refs):
        total = jnp.zeros((128, 1024), F32)
        for away, line_ref in zip((0, 1, 3, 2), line_refs):
            pick = jnp.where(lane + 256 * away == at[:, s : s + 1], 1.0, 0.0).astype(BF16)
            total = total + jnp.dot(pick, line_ref[...], preferred_element_type=F32)
        out_ref[...] = total.astype(BF16)


def match_kernel(len_ref, *refs):
    i = lax.broadcasted_iota(I32, (128, 128), 0)
    j = lax.broadcasted_iota(I32, (128, 128), 1)
    own_refs, other_refs, out_ref = refs[0:2], refs[2:4], refs[4]
    for s in range(2):
        one = own_refs[s][...] + other_refs[s][...]
        gram = lax.dot_general(one, one, (((1,), (1,)), ((), ())), preferred_element_type=F32)
        diagonal = jnp.where(i == j, gram, 0.0)
        down = lax.rsqrt(jnp.sum(diagonal, axis=1, keepdims=True) + 1e-06)
        across = lax.rsqrt(jnp.sum(diagonal, axis=0, keepdims=True) + 1e-06)
        cosine = gram * down * across
        length = len_ref[s]
        largest = jnp.max(jnp.where((i < length) & (i != j), cosine, -2.0), axis=0, keepdims=True)
        out_ref[s : s + 1, :] = jnp.where(j[0:1] < length, largest, 0.0)


VMEM = pl.BlockSpec(memory_space=pltpu.VMEM)
HBM = pl.BlockSpec(memory_space=pltpu.HBM)
SMEM = pl.BlockSpec(memory_space=pltpu.SMEM)


def local(embeddings, assignments, old_centroids, slab_rows, slab_len):
    zh, x, y, core = (lax.axis_index(name).astype(I32) for name in ("zh", "x", "y", "c"))
    messages = pl.pallas_call(
        pack_kernel,
        out_shape=pltpu.HBM((4, 8, MSG, 128), BF16),
        in_specs=[HBM] * 3,
        out_specs=HBM,
        scratch_shapes=[
            pltpu.VMEM((ROWS, 1024), BF16),
            pltpu.VMEM((2, 128), I32),
            pltpu.VMEM((2, 128), I32),
            pltpu.VMEM((4, 8, MSG, 128), BF16),
            pltpu.SemaphoreType.DMA((2,)),
            pltpu.SemaphoreType.DMA((2,)),
            pltpu.SemaphoreType.DMA((2,)),
        ],
        compiler_params=params(8),
        cost_estimate=cost(1 << 20, 3 << 19),
        name="pack",
    )(*(pltpu.with_memory_space_constraint(a, pltpu.HBM) for a in (embeddings, assignments.reshape(2, 128), slab_rows)))
    messages = lax.all_to_all(messages.reshape(BLOCK, MSG, 128), ("x", "y", "c"), 0, 0, axis_index_groups=[BLOCK_ORDER], tiled=True)
    parts, rows = pl.pallas_call(
        sum_kernel,
        out_shape=(pltpu.VMEM((528, 128), F32), pltpu.VMEM((4, 128), I32)),
        in_specs=[SMEM, VMEM],
        out_specs=(VMEM, VMEM),
        compiler_params=params(20),
        cost_estimate=cost(1 << 31, 1 << 20),
        name="sums",
    )(((x * 8 + y * 2 + core) ^ BLOCK_ORDER[0]).reshape(1), messages)
    embeddings, parts = lax.optimization_barrier((embeddings, parts))
    line = [embeddings] + [lax.ppermute(embeddings, "y", [(i, i ^ d) for i in range(4)]) for d in (1, 3, 2)]
    parts = lax.all_to_all(parts.reshape(16, 33, 1, 128), ("zl", "x"), 0, 0, axis_index_groups=[PLANE_ORDER], tiled=True)
    parts = pl.pallas_call(
        regroup_kernel,
        out_shape=pltpu.VMEM((136, 128), F32),
        in_specs=[VMEM],
        out_specs=VMEM,
        scratch_shapes=[pltpu.VMEM((32, 128), F32)],
        compiler_params=params(4),
        cost_estimate=cost(1 << 18, 1 << 19),
        name="regroup",
    )(parts.reshape(528, 128))
    after = parts
    parts = lax.all_to_all(parts.reshape(8, 17, 1, 128), "zh", 0, 0, axis_index_groups=[RING_ORDER], tiled=True)
    place = jnp.stack([core, y])
    own, others = (
        pl.pallas_call(
            functools.partial(member_kernel, of),
            out_shape=[jax.ShapeDtypeStruct((128, 1024), BF16)] * 2,
            in_specs=[pl.BlockSpec(memory_space=pl.ANY), SMEM] + [VMEM] * 5,
            out_specs=[VMEM] * 2,
            compiler_params=params(16),
            cost_estimate=cost(0, 0),
            name="members",
        )(after, place, rows, *line)
        for of in range(2)
    )
    others = [lax.ppermute(other, "c", [(0, 1), (1, 0)]) for other in others]
    best_cosine = pl.pallas_call(
        match_kernel,
        out_shape=jax.ShapeDtypeStruct((2, 128), F32),
        in_specs=[SMEM] + [VMEM] * 4,
        out_specs=VMEM,
        compiler_params=params(8),
        cost_estimate=cost(0, 0),
        name="match",
    )(slab_len, *own, *others)
    parts, best_cosine = lax.optimization_barrier((parts, best_cosine))
    centroids = pl.pallas_call(
        finish_kernel,
        out_shape=jax.ShapeDtypeStruct((16, 128), F32),
        in_specs=[SMEM, VMEM, VMEM],
        out_specs=VMEM,
        compiler_params=params(4),
        cost_estimate=cost(1 << 18, 1 << 18),
        name="finish",
    )((zh * 16).reshape(1), parts.reshape(136, 128), old_centroids)
    return (centroids, best_cosine)


def solution(mesh):
    fine = Mesh(mesh.devices.reshape(SIZES), NAMES)
    dp, mp = ("zh", "zl", "x"), ("y", "c")
    placed = (
        P(dp + mp, None),
        P(dp + mp),
        P(dp, mp),
        P(dp + mp, None),
        P(dp + mp),
    )
    return jax.shard_map(
        local,
        mesh=fine,
        in_specs=placed,
        out_specs=(P(dp, mp), P(dp + mp, None)),
        check_vma=False,
    )
```

```python
import functools

import jax
import jax.numpy as jnp
from jax import lax
from jax.experimental import pallas as pl
from jax.experimental.pallas import tpu as pltpu
from jax.sharding import Mesh, PartitionSpec as P

F32, BF16, I32 = jnp.float32, jnp.bfloat16, jnp.int32
SIZES = (8, 4, 4, 4, 2)
NAMES = ("zh", "zl", "x", "y", "c")
BLOCK = 32
ROWS = 256
FEATS = 32
MSG = 80
MIB = 1 << 20
FIRST = (2, 4)
BLOCK_ORDER = [k ^ 20 for k in range(BLOCK)]
FIRST_ZL = 1
PLANE_ORDER = [k ^ (4 * FIRST_ZL) for k in range(16)]
FIRST_ZH = 5
RING_ORDER = [k ^ FIRST_ZH for k in range(8)]


def params(mib):
    return pltpu.CompilerParams(vmem_limit_bytes=mib * MIB)


def cost(flops, moved):
    return pl.CostEstimate(flops=flops, bytes_accessed=moved, transcendentals=0)


def pack_kernel(emb_hbm, label_hbm, rows_hbm, out_hbm, emb_ref, label_ref, rows_ref, msg_ref, in_sems, out_sems, sems):
    small = [
        pltpu.make_async_copy(label_hbm, label_ref, sems.at[0]),
        pltpu.make_async_copy(rows_hbm, rows_ref, sems.at[1]),
    ]
    halves = [pl.ds(0, 512), pl.ds(512, 512)]
    blocks = [pltpu.make_async_copy(emb_hbm.at[:, at], emb_ref.at[:, at], in_sems.at[k]) for k, at in enumerate(halves)]
    for copy in blocks + small:
        copy.start()
    for copy in small:
        copy.wait()
    c, r = label_ref[...], rows_ref[...]
    high = ((c >> 6) & 3) * 64 + ((c >> 4) & 3) * 16 + (c >> 8) * 2 + (c & 1)
    low = ((c >> 1) & 1) * 4 + ((c >> 2) & 3)
    row = lax.broadcasted_iota(I32, (16, 128), 0)
    codes = jnp.zeros((16, 128), I32)
    for k, pair in enumerate((high, low, r >> 3, r & 7)):
        codes = jnp.where(row == 2 * k, pair[0:1], codes)
        codes = jnp.where(row == 2 * k + 1, pair[1:2], codes)
    codes = codes.astype(F32).astype(BF16)
    sent = []
    for k in range(2):
        blocks[k].wait()
        for mp in range(4 * k, 4 * k + 4):
            turned = emb_ref[:, 128 * mp : 128 * mp + 128].T
            for x in range(4):
                part, at = turned[x * FEATS : x * FEATS + FEATS], (x ^ FIRST[0], mp ^ FIRST[1])
                msg_ref[*at, 0:32, :] = part[:, 0:128]
                msg_ref[*at, 32:64, :] = part[:, 128:256]
                msg_ref[*at, 64:80, :] = codes
        at = pl.ds((4 * k) ^ FIRST[1], 4)
        sent.append(pltpu.make_async_copy(msg_ref.at[:, at], out_hbm.at[:, at], out_sems.at[k]))
        sent[k].start()
    for copy in sent:
        copy.wait()


def lanes(n):
    return lax.broadcasted_iota(I32, (n, 128), 0).astype(F32).astype(BF16)


def sum_kernel(from_ref, msg_ref, out_ref, rows_ref):
    cluster = lanes(256)
    one, zero = jnp.ones((), BF16), jnp.zeros((), BF16)
    contract = (((1,), (1,)), ((), ()))
    sums = jnp.zeros((256, 256), F32)
    counts = jnp.zeros((16, 128), F32)
    for first in range(0, BLOCK, 4):
        a, b, p, q = [], [], [], []
        for s in range(first, first + 4):
            codes = msg_ref[s, 64:80, :]
            for t in range(2):
                high, low = codes[t : t + 1], codes[2 + t : 3 + t]
                part = msg_ref[s, 32 * t : 32 * t + 32, :]
                a.append(jnp.where(cluster == high, one, zero))
                b.append(jnp.concatenate([jnp.where(low == jnp.asarray(g, BF16), part, zero) for g in range(8)], 0))
                h, g = high.astype(F32).astype(I32), low.astype(F32).astype(I32)
                within = ((h >> 1) & 7) * 16 + (g & 3) * 4 + (g >> 2) * 2 + (h & 1)
                p.append(jnp.where(cluster[0:16] == (h >> 4).astype(F32).astype(BF16), one, zero))
                q.append(jnp.where(cluster[0:128] == within.astype(F32).astype(BF16), one, zero))
        a, b, p, q = (jnp.concatenate(blocks, 1) for blocks in (a, b, p, q))
        sums = sums + lax.dot_general(a, b, contract, preferred_element_type=F32)
        counts = counts + lax.dot_general(p, q, contract, preferred_element_type=F32)
    for m in range(16):
        at = 33 * PLANE_ORDER[m]
        out_ref[at : at + 16, :] = sums[16 * m : 16 * m + 16, 0:128]
        out_ref[at + 16 : at + 32, :] = sums[16 * m : 16 * m + 16, 128:256]
        out_ref[at + 32 : at + 33, :] = counts[m : m + 1, :]
    for k in range(2):
        codes = msg_ref[from_ref[0] ^ k, 64:80, :].astype(F32).astype(I32)
        rows_ref[2 * k : 2 * k + 2, :] = codes[4:6] * 8 + codes[6:8]


def regroup_kernel(in_ref, out_ref, s_ref):
    slot = lax.broadcasted_iota(I32, (32, 128), 1) // FEATS
    parts = []
    for x in range(4):
        first, *others = (in_ref[33 * (4 * zl + x) : 33 * (4 * zl + x) + 32, :] for zl in range(4))
        parts.append((first + others[0]) + (others[1] + others[2]))
    first, *others = (in_ref[33 * 4 * zl + 32 : 33 * 4 * zl + 33, :] for zl in range(4))
    counts = (first + others[0]) + (others[1] + others[2])
    for low in range(4):
        rows = jnp.zeros((32, 128), F32)
        for x in range(4):
            shift = ((x - low) * FEATS) % 128
            moved = pltpu.roll(parts[x], shift, 1) if shift else parts[x]
            rows = jnp.where(slot == x, moved, rows)
        s_ref[...] = rows
        for zh in range(8):
            for r1 in range(2):
                at = 17 * (zh ^ FIRST_ZH) + 4 * low + 2 * r1
                out_ref[at : at + 2, :] = s_ref[16 * r1 + 2 * zh : 16 * r1 + 2 * zh + 2, :]
    for zh in range(8):
        at = 17 * zh + 16
        out_ref[at : at + 1, :] = counts


def finish_kernel(at_ref, in_ref, old_ref, out_ref):
    sums, count_row = in_ref[0:16, :], in_ref[16:17, :]
    for zh in range(1, 8):
        sums = sums + in_ref[17 * zh : 17 * zh + 16, :]
        count_row = count_row + in_ref[17 * zh + 16 : 17 * zh + 17, :]
    lane = lax.broadcasted_iota(I32, (16, 128), 1)
    own = lane == at_ref[0] + lax.broadcasted_iota(I32, (16, 128), 0)
    counts = jnp.sum(jnp.where(own, count_row, 0.0), axis=1, keepdims=True)
    out_ref[...] = (sums + old_ref[...]) / (counts + 1.0)


def member_kernel(of, after_ref, place_ref, rows_ref, *refs):
    line_refs, out_refs = refs[:4], refs[4:]
    core, y = place_ref[0], place_ref[1]
    lane = lax.broadcasted_iota(I32, (128, ROWS), 1)
    r = rows_ref[2 * of : 2 * of + 2, :]
    at = jnp.where(((r >> 8) & 1) == core, (((r >> 9) ^ y) << 8) + (r & 255), -1)
    at = jnp.concatenate([at, jnp.zeros((6, 128), I32)], 0).astype(F32).T.astype(I32)
    for s, out_ref in enumerate(out_refs):
        total = jnp.zeros((128, 1024), F32)
        for away, line_ref in zip((0, 1, 3, 2), line_refs):
            pick = jnp.where(lane + 256 * away == at[:, s : s + 1], 1.0, 0.0).astype(BF16)
            total = total + jnp.dot(pick, line_ref[...], preferred_element_type=F32)
        out_ref[...] = total.astype(BF16)


def match_kernel(len_hbm, *refs):
    i = lax.broadcasted_iota(I32, (128, 128), 0)
    j = lax.broadcasted_iota(I32, (128, 128), 1)
    own_refs, other_refs, (out_ref, len_ref, sem) = refs[0:2], refs[2:4], refs[4:7]
    lengths = pltpu.make_async_copy(len_hbm, len_ref, sem)
    lengths.start()
    i = lax.broadcasted_iota(I32, (128, 128), 0)
    j = lax.broadcasted_iota(I32, (128, 128), 1)
    cosines = []
    for s in range(2):
        one = own_refs[s][...] + other_refs[s][...]
        gram = lax.dot_general(one, one, (((1,), (1,)), ((), ())), preferred_element_type=F32)
        diagonal = jnp.where(i == j, gram, 0.0)
        down = lax.rsqrt(jnp.sum(diagonal, axis=1, keepdims=True) + 1e-06)
        across = lax.rsqrt(jnp.sum(diagonal, axis=0, keepdims=True) + 1e-06)
        cosines.append(gram * down * across)
    lengths.wait()
    for s in range(2):
        length = len_ref[s]
        largest = jnp.max(jnp.where((i < length) & (i != j), cosines[s], -2.0), axis=0, keepdims=True)
        out_ref[s : s + 1, :] = jnp.where(j[0:1] < length, largest, 0.0)


VMEM = pl.BlockSpec(memory_space=pltpu.VMEM)
HBM = pl.BlockSpec(memory_space=pltpu.HBM)
SMEM = pl.BlockSpec(memory_space=pltpu.SMEM)


def local(embeddings, assignments, old_centroids, slab_rows, slab_len):
    zh, x, y, core = (lax.axis_index(name).astype(I32) for name in ("zh", "x", "y", "c"))
    messages = pl.pallas_call(
        pack_kernel,
        out_shape=pltpu.HBM((4, 8, MSG, 128), BF16),
        in_specs=[HBM] * 3,
        out_specs=HBM,
        scratch_shapes=[
            pltpu.VMEM((ROWS, 1024), BF16),
            pltpu.VMEM((2, 128), I32),
            pltpu.VMEM((2, 128), I32),
            pltpu.VMEM((4, 8, MSG, 128), BF16),
            pltpu.SemaphoreType.DMA((2,)),
            pltpu.SemaphoreType.DMA((2,)),
            pltpu.SemaphoreType.DMA((2,)),
        ],
        compiler_params=params(8),
        cost_estimate=cost(1 << 20, 3 << 19),
        name="pack",
    )(*(pltpu.with_memory_space_constraint(a, pltpu.HBM) for a in (embeddings, assignments.reshape(2, 128), slab_rows)))
    messages = lax.all_to_all(messages.reshape(BLOCK, MSG, 128), ("x", "y", "c"), 0, 0, axis_index_groups=[BLOCK_ORDER], tiled=True)
    parts, rows = pl.pallas_call(
        sum_kernel,
        out_shape=(pltpu.VMEM((528, 128), F32), pltpu.VMEM((4, 128), I32)),
        in_specs=[SMEM, VMEM],
        out_specs=(VMEM, VMEM),
        compiler_params=params(20),
        cost_estimate=cost(1 << 31, 1 << 20),
        name="sums",
    )(((x * 8 + y * 2 + core) ^ BLOCK_ORDER[0]).reshape(1), messages)
    embeddings, parts = lax.optimization_barrier((embeddings, parts))
    line = [embeddings] + [lax.ppermute(embeddings, "y", [(i, i ^ d) for i in range(4)]) for d in (1, 3, 2)]
    parts = lax.all_to_all(parts.reshape(16, 33, 1, 128), ("zl", "x"), 0, 0, axis_index_groups=[PLANE_ORDER], tiled=True)
    parts = pl.pallas_call(
        regroup_kernel,
        out_shape=pltpu.VMEM((136, 128), F32),
        in_specs=[VMEM],
        out_specs=VMEM,
        scratch_shapes=[pltpu.VMEM((32, 128), F32)],
        compiler_params=params(4),
        cost_estimate=cost(1 << 18, 1 << 19),
        name="regroup",
    )(parts.reshape(528, 128))
    after = parts
    parts = lax.all_to_all(parts.reshape(8, 17, 1, 128), "zh", 0, 0, axis_index_groups=[RING_ORDER], tiled=True)
    place = jnp.stack([core, y])
    own, others = (
        pl.pallas_call(
            functools.partial(member_kernel, of),
            out_shape=[jax.ShapeDtypeStruct((128, 1024), BF16)] * 2,
            in_specs=[pl.BlockSpec(memory_space=pl.ANY), SMEM] + [VMEM] * 5,
            out_specs=[VMEM] * 2,
            compiler_params=params(16),
            cost_estimate=cost(0, 0),
            name="members",
        )(after, place, rows, *line)
        for of in range(2)
    )
    others = [lax.ppermute(other, "c", [(0, 1), (1, 0)]) for other in others]
    best_cosine = pl.pallas_call(
        match_kernel,
        out_shape=jax.ShapeDtypeStruct((2, 128), F32),
        in_specs=[HBM] + [VMEM] * 4,
        out_specs=VMEM,
        scratch_shapes=[pltpu.SMEM((2,), I32), pltpu.SemaphoreType.DMA],
        compiler_params=params(8),
        cost_estimate=cost(0, 0),
        name="match",
    )(pltpu.with_memory_space_constraint(slab_len, pltpu.HBM), *own, *others)
    parts, best_cosine = lax.optimization_barrier((parts, best_cosine))
    centroids = pl.pallas_call(
        finish_kernel,
        out_shape=jax.ShapeDtypeStruct((16, 128), F32),
        in_specs=[SMEM, VMEM, VMEM],
        out_specs=VMEM,
        compiler_params=params(4),
        cost_estimate=cost(1 << 18, 1 << 18),
        name="finish",
    )((zh * 16).reshape(1), parts.reshape(136, 128), old_centroids)
    return (centroids, best_cosine)


def solution(mesh):
    fine = Mesh(mesh.devices.reshape(SIZES), NAMES)
    dp, mp = ("zh", "zl", "x"), ("y", "c")
    placed = (
        P(dp + mp, None),
        P(dp + mp),
        P(dp, mp),
        P(dp + mp, None),
        P(dp + mp),
    )
    return jax.shard_map(
        local,
        mesh=fine,
        in_specs=placed,
        out_specs=(P(dp, mp), P(dp + mp, None)),
        check_vma=False,
    )
```

```python
import functools

import jax
import jax.numpy as jnp
from jax import lax
from jax.experimental import pallas as pl
from jax.experimental.pallas import tpu as pltpu
from jax.sharding import Mesh, PartitionSpec as P

F32, BF16, I32 = jnp.float32, jnp.bfloat16, jnp.int32
SIZES = (8, 4, 4, 4, 2)
NAMES = ("zh", "zl", "x", "y", "c")
BLOCK = 32
ROWS = 256
FEATS = 32
MSG = 80
MIB = 1 << 20
FIRST = (2, 4)
BLOCK_ORDER = [k ^ 20 for k in range(BLOCK)]
FIRST_ZL = 1
PLANE_ORDER = [k ^ (4 * FIRST_ZL) for k in range(16)]
FIRST_ZH = 5
RING_ORDER = [k ^ FIRST_ZH for k in range(8)]


def params(mib):
    return pltpu.CompilerParams(vmem_limit_bytes=mib * MIB)


def cost(flops, moved):
    return pl.CostEstimate(flops=flops, bytes_accessed=moved, transcendentals=0)


def pack_kernel(emb_hbm, label_hbm, rows_hbm, out_hbm, emb_ref, label_ref, rows_ref, msg_ref, in_sems, out_sems, sems):
    small = [
        pltpu.make_async_copy(label_hbm, label_ref, sems.at[0]),
        pltpu.make_async_copy(rows_hbm, rows_ref, sems.at[1]),
    ]
    halves = [pl.ds(0, 512), pl.ds(512, 512)]
    blocks = [pltpu.make_async_copy(emb_hbm.at[:, at], emb_ref.at[:, at], in_sems.at[k]) for k, at in enumerate(halves)]
    for copy in blocks + small:
        copy.start()
    for copy in small:
        copy.wait()
    c, r = label_ref[...], rows_ref[...]
    high = ((c >> 6) & 3) * 64 + ((c >> 4) & 3) * 16 + (c >> 8) * 2 + (c & 1)
    low = ((c >> 1) & 1) * 4 + ((c >> 2) & 3)
    row = lax.broadcasted_iota(I32, (16, 128), 0)
    codes = jnp.zeros((16, 128), I32)
    for k, pair in enumerate((high, low, r >> 3, r & 7)):
        codes = jnp.where(row == 2 * k, pair[0:1], codes)
        codes = jnp.where(row == 2 * k + 1, pair[1:2], codes)
    codes = codes.astype(F32).astype(BF16)
    sent = []
    for k in range(2):
        blocks[k].wait()
        for mp in range(4 * k, 4 * k + 4):
            turned = emb_ref[:, 128 * mp : 128 * mp + 128].T
            for x in range(4):
                part, at = turned[x * FEATS : x * FEATS + FEATS], (x ^ FIRST[0], mp ^ FIRST[1])
                msg_ref[*at, 0:32, :] = part[:, 0:128]
                msg_ref[*at, 32:64, :] = part[:, 128:256]
                msg_ref[*at, 64:80, :] = codes
        at = pl.ds((4 * k) ^ FIRST[1], 4)
        sent.append(pltpu.make_async_copy(msg_ref.at[:, at], out_hbm.at[:, at], out_sems.at[k]))
        sent[k].start()
    for copy in sent:
        copy.wait()


def lanes(n):
    return lax.broadcasted_iota(I32, (n, 128), 0).astype(F32).astype(BF16)


def sum_kernel(from_ref, msg_ref, out_ref, rows_ref):
    cluster = lanes(256)
    one, zero = jnp.ones((), BF16), jnp.zeros((), BF16)
    contract = (((1,), (1,)), ((), ()))
    sums = jnp.zeros((256, 256), F32)
    counts = jnp.zeros((16, 128), F32)
    for first in range(0, BLOCK, 4):
        a, b, p, q = [], [], [], []
        for s in range(first, first + 4):
            codes = msg_ref[s, 64:80, :]
            for t in range(2):
                high, low = codes[t : t + 1], codes[2 + t : 3 + t]
                part = msg_ref[s, 32 * t : 32 * t + 32, :]
                a.append(jnp.where(cluster == high, one, zero))
                b.append(jnp.concatenate([jnp.where(low == jnp.asarray(g, BF16), part, zero) for g in range(8)], 0))
                h, g = high.astype(F32).astype(I32), low.astype(F32).astype(I32)
                within = ((h >> 1) & 7) * 16 + (g & 3) * 4 + (g >> 2) * 2 + (h & 1)
                p.append(jnp.where(cluster[0:16] == (h >> 4).astype(F32).astype(BF16), one, zero))
                q.append(jnp.where(cluster[0:128] == within.astype(F32).astype(BF16), one, zero))
        a, b, p, q = (jnp.concatenate(blocks, 1) for blocks in (a, b, p, q))
        sums = sums + lax.dot_general(a, b, contract, preferred_element_type=F32)
        counts = counts + lax.dot_general(p, q, contract, preferred_element_type=F32)
    for m in range(16):
        at = 33 * PLANE_ORDER[m]
        out_ref[at : at + 16, :] = sums[16 * m : 16 * m + 16, 0:128]
        out_ref[at + 16 : at + 32, :] = sums[16 * m : 16 * m + 16, 128:256]
        out_ref[at + 32 : at + 33, :] = counts[m : m + 1, :]
    for k in range(2):
        codes = msg_ref[from_ref[0] ^ k, 64:80, :].astype(F32).astype(I32)
        rows_ref[2 * k : 2 * k + 2, :] = codes[4:6] * 8 + codes[6:8]


def regroup_kernel(in_ref, out_ref, s_ref):
    slot = lax.broadcasted_iota(I32, (32, 128), 1) // FEATS
    parts = []
    for x in range(4):
        first, *others = (in_ref[33 * (4 * zl + x) : 33 * (4 * zl + x) + 32, :] for zl in range(4))
        parts.append((first + others[0]) + (others[1] + others[2]))
    first, *others = (in_ref[33 * 4 * zl + 32 : 33 * 4 * zl + 33, :] for zl in range(4))
    counts = (first + others[0]) + (others[1] + others[2])
    for low in range(4):
        rows = jnp.zeros((32, 128), F32)
        for x in range(4):
            shift = ((x - low) * FEATS) % 128
            moved = pltpu.roll(parts[x], shift, 1) if shift else parts[x]
            rows = jnp.where(slot == x, moved, rows)
        s_ref[...] = rows
        for zh in range(8):
            for r1 in range(2):
                at = 17 * (zh ^ FIRST_ZH) + 4 * low + 2 * r1
                out_ref[at : at + 2, :] = s_ref[16 * r1 + 2 * zh : 16 * r1 + 2 * zh + 2, :]
    for zh in range(8):
        at = 17 * zh + 16
        out_ref[at : at + 1, :] = counts


def finish_kernel(at_ref, in_ref, old_ref, out_ref):
    sums, count_row = in_ref[0:16, :], in_ref[16:17, :]
    for zh in range(1, 8):
        sums = sums + in_ref[17 * zh : 17 * zh + 16, :]
        count_row = count_row + in_ref[17 * zh + 16 : 17 * zh + 17, :]
    lane = lax.broadcasted_iota(I32, (16, 128), 1)
    own = lane == at_ref[0] + lax.broadcasted_iota(I32, (16, 128), 0)
    counts = jnp.sum(jnp.where(own, count_row, 0.0), axis=1, keepdims=True)
    out_ref[...] = (sums + old_ref[...]) / (counts + 1.0)


def member_kernel(of, after_ref, place_ref, rows_ref, *refs):
    line_refs, out_refs = refs[:3], refs[3:]
    core, y = place_ref[0], place_ref[1]
    lane = lax.broadcasted_iota(I32, (128, ROWS), 1)
    r = rows_ref[2 * of : 2 * of + 2, :]
    away, far = (r >> 9) ^ y, ((r >> 8) & 1) ^ core
    block = jnp.where(away == 1 + 2 * core, 1 + far, jnp.where(far == 1, -1, jnp.where(away == 0, 0, jnp.where(away == 2, 3, -1))))
    at = jnp.where(block < 0, -1, (block << 8) + (r & 255))
    at = jnp.concatenate([at, jnp.zeros((6, 128), I32)], 0).astype(F32).T.astype(I32)
    for s, out_ref in enumerate(out_refs):
        total = jnp.zeros((128, 1024), F32)
        for first, line_ref in zip((0, 1, 3), line_refs):
            for k in range(line_ref.shape[0] // ROWS):
                pick = jnp.where(lane + ROWS * (first + k) == at[:, s : s + 1], 1.0, 0.0).astype(BF16)
                rows = line_ref[ROWS * k : ROWS * k + ROWS, :]
                total = total + jnp.dot(pick, rows, preferred_element_type=F32)
        out_ref[...] = total.astype(BF16)


def match_kernel(len_hbm, *refs):
    i = lax.broadcasted_iota(I32, (128, 128), 0)
    j = lax.broadcasted_iota(I32, (128, 128), 1)
    own_refs, other_refs, (out_ref, len_ref, sem) = refs[0:2], refs[2:4], refs[4:7]
    lengths = pltpu.make_async_copy(len_hbm, len_ref, sem)
    lengths.start()
    i = lax.broadcasted_iota(I32, (128, 128), 0)
    j = lax.broadcasted_iota(I32, (128, 128), 1)
    cosines = []
    for s in range(2):
        one = own_refs[s][...] + other_refs[s][...]
        gram = lax.dot_general(one, one, (((1,), (1,)), ((), ())), preferred_element_type=F32)
        diagonal = jnp.where(i == j, gram, 0.0)
        down = lax.rsqrt(jnp.sum(diagonal, axis=1, keepdims=True) + 1e-06)
        across = lax.rsqrt(jnp.sum(diagonal, axis=0, keepdims=True) + 1e-06)
        cosines.append(gram * down * across)
    lengths.wait()
    for s in range(2):
        length = len_ref[s]
        largest = jnp.max(jnp.where((i < length) & (i != j), cosines[s], -2.0), axis=0, keepdims=True)
        out_ref[s : s + 1, :] = jnp.where(j[0:1] < length, largest, 0.0)


VMEM = pl.BlockSpec(memory_space=pltpu.VMEM)
HBM = pl.BlockSpec(memory_space=pltpu.HBM)
SMEM = pl.BlockSpec(memory_space=pltpu.SMEM)


def local(embeddings, assignments, old_centroids, slab_rows, slab_len):
    zh, x, y, core = (lax.axis_index(name).astype(I32) for name in ("zh", "x", "y", "c"))
    messages = pl.pallas_call(
        pack_kernel,
        out_shape=pltpu.HBM((4, 8, MSG, 128), BF16),
        in_specs=[HBM] * 3,
        out_specs=HBM,
        scratch_shapes=[
            pltpu.VMEM((ROWS, 1024), BF16),
            pltpu.VMEM((2, 128), I32),
            pltpu.VMEM((2, 128), I32),
            pltpu.VMEM((4, 8, MSG, 128), BF16),
            pltpu.SemaphoreType.DMA((2,)),
            pltpu.SemaphoreType.DMA((2,)),
            pltpu.SemaphoreType.DMA((2,)),
        ],
        compiler_params=params(8),
        cost_estimate=cost(1 << 20, 3 << 19),
        name="pack",
    )(*(pltpu.with_memory_space_constraint(a, pltpu.HBM) for a in (embeddings, assignments.reshape(2, 128), slab_rows)))
    messages = lax.all_to_all(messages.reshape(BLOCK, MSG, 128), ("x", "y", "c"), 0, 0, axis_index_groups=[BLOCK_ORDER], tiled=True)
    parts, rows = pl.pallas_call(
        sum_kernel,
        out_shape=(pltpu.VMEM((528, 128), F32), pltpu.VMEM((4, 128), I32)),
        in_specs=[SMEM, VMEM],
        out_specs=(VMEM, VMEM),
        compiler_params=params(20),
        cost_estimate=cost(1 << 31, 1 << 20),
        name="sums",
    )(((x * 8 + y * 2 + core) ^ BLOCK_ORDER[0]).reshape(1), messages)
    partner = lax.ppermute(embeddings, "c", [(0, 1), (1, 0)])
    embeddings, partner, parts = lax.optimization_barrier((embeddings, partner, parts))
    near = [(2 * i + c, 2 * (i ^ (1 + 2 * c)) + c) for i in range(4) for c in range(2)]
    line = [
        embeddings,
        lax.ppermute(jnp.concatenate([embeddings, partner]), ("y", "c"), near),
        lax.ppermute(embeddings, "y", [(i, i ^ 2) for i in range(4)]),
    ]
    parts = lax.all_to_all(parts.reshape(16, 33, 1, 128), ("zl", "x"), 0, 0, axis_index_groups=[PLANE_ORDER], tiled=True)
    parts = pl.pallas_call(
        regroup_kernel,
        out_shape=pltpu.VMEM((136, 128), F32),
        in_specs=[VMEM],
        out_specs=VMEM,
        scratch_shapes=[pltpu.VMEM((32, 128), F32)],
        compiler_params=params(4),
        cost_estimate=cost(1 << 18, 1 << 19),
        name="regroup",
    )(parts.reshape(528, 128))
    after = parts
    parts = lax.all_to_all(parts.reshape(8, 17, 1, 128), "zh", 0, 0, axis_index_groups=[RING_ORDER], tiled=True)
    place = jnp.stack([core, y])
    own, others = (
        pl.pallas_call(
            functools.partial(member_kernel, of),
            out_shape=[jax.ShapeDtypeStruct((128, 1024), BF16)] * 2,
            in_specs=[pl.BlockSpec(memory_space=pl.ANY), SMEM] + [VMEM] * 4,
            out_specs=[VMEM] * 2,
            compiler_params=params(16),
            cost_estimate=cost(0, 0),
            name="members",
        )(after, place, rows, *line)
        for of in range(2)
    )
    others = [lax.ppermute(other, "c", [(0, 1), (1, 0)]) for other in others]
    best_cosine = pl.pallas_call(
        match_kernel,
        out_shape=jax.ShapeDtypeStruct((2, 128), F32),
        in_specs=[HBM] + [VMEM] * 4,
        out_specs=VMEM,
        scratch_shapes=[pltpu.SMEM((2,), I32), pltpu.SemaphoreType.DMA],
        compiler_params=params(8),
        cost_estimate=cost(0, 0),
        name="match",
    )(pltpu.with_memory_space_constraint(slab_len, pltpu.HBM), *own, *others)
    parts, best_cosine = lax.optimization_barrier((parts, best_cosine))
    centroids = pl.pallas_call(
        finish_kernel,
        out_shape=jax.ShapeDtypeStruct((16, 128), F32),
        in_specs=[SMEM, VMEM, VMEM],
        out_specs=VMEM,
        compiler_params=params(4),
        cost_estimate=cost(1 << 18, 1 << 18),
        name="finish",
    )((zh * 16).reshape(1), parts.reshape(136, 128), old_centroids)
    return (centroids, best_cosine)


def solution(mesh):
    fine = Mesh(mesh.devices.reshape(SIZES), NAMES)
    dp, mp = ("zh", "zl", "x"), ("y", "c")
    placed = (
        P(dp + mp, None),
        P(dp + mp),
        P(dp, mp),
        P(dp + mp, None),
        P(dp + mp),
    )
    return jax.shard_map(
        local,
        mesh=fine,
        in_specs=placed,
        out_specs=(P(dp, mp), P(dp + mp, None)),
        check_vma=False,
    )
```

```python
import functools

import jax
import jax.numpy as jnp
from jax import lax
from jax.experimental import pallas as pl
from jax.experimental.pallas import tpu as pltpu
from jax.sharding import Mesh, PartitionSpec as P

F32, BF16, I32 = jnp.float32, jnp.bfloat16, jnp.int32
SIZES = (8, 4, 4, 4, 2)
NAMES = ("zh", "zl", "x", "y", "c")
BLOCK = 32
ROWS = 256
FEATS = 32
MSG = 80
MIB = 1 << 20
FIRST = (2, 4)
BLOCK_ORDER = [k ^ 20 for k in range(BLOCK)]
PLANE_FIRST = (1, 2)
PLANE_ORDER = [k ^ 6 for k in range(16)]
FIRST_ZH = 5
RING_ORDER = [k ^ FIRST_ZH for k in range(8)]


def params(mib):
    return pltpu.CompilerParams(vmem_limit_bytes=mib * MIB)


def cost(flops, moved):
    return pl.CostEstimate(flops=flops, bytes_accessed=moved, transcendentals=0)


def pack_kernel(emb_hbm, label_hbm, rows_hbm, out_hbm, emb_ref, label_ref, rows_ref, msg_ref, in_sems, out_sems, sems):
    small = [
        pltpu.make_async_copy(label_hbm, label_ref, sems.at[0]),
        pltpu.make_async_copy(rows_hbm, rows_ref, sems.at[1]),
    ]
    halves = [pl.ds(0, 512), pl.ds(512, 512)]
    blocks = [pltpu.make_async_copy(emb_hbm.at[:, at], emb_ref.at[:, at], in_sems.at[k]) for k, at in enumerate(halves)]
    for copy in blocks + small:
        copy.start()
    for copy in small:
        copy.wait()
    c, r = label_ref[...], rows_ref[...]
    high = ((c >> 6) & 3) * 64 + ((c >> 4) & 3) * 16 + (c >> 8) * 2 + (c & 1)
    low = ((c >> 1) & 1) * 4 + ((c >> 2) & 3)
    row = lax.broadcasted_iota(I32, (16, 128), 0)
    codes = jnp.zeros((16, 128), I32)
    for k, pair in enumerate((high, low, r >> 3, r & 7)):
        codes = jnp.where(row == 2 * k, pair[0:1], codes)
        codes = jnp.where(row == 2 * k + 1, pair[1:2], codes)
    codes = codes.astype(F32).astype(BF16)
    sent = []
    for k in range(2):
        blocks[k].wait()
        for mp in range(4 * k, 4 * k + 4):
            turned = emb_ref[:, 128 * mp : 128 * mp + 128].T
            for x in range(4):
                part, at = turned[x * FEATS : x * FEATS + FEATS], (x ^ FIRST[0], mp ^ FIRST[1])
                msg_ref[*at, 0:32, :] = part[:, 0:128]
                msg_ref[*at, 32:64, :] = part[:, 128:256]
                msg_ref[*at, 64:80, :] = codes
        at = pl.ds((4 * k) ^ FIRST[1], 4)
        sent.append(pltpu.make_async_copy(msg_ref.at[:, at], out_hbm.at[:, at], out_sems.at[k]))
        sent[k].start()
    for copy in sent:
        copy.wait()


def lanes(n):
    return lax.broadcasted_iota(I32, (n, 128), 0).astype(F32).astype(BF16)


def sum_kernel(from_ref, msg_ref, out_ref, rows_ref):
    cluster = lanes(256)
    one, zero = jnp.ones((), BF16), jnp.zeros((), BF16)
    contract = (((1,), (1,)), ((), ()))
    sums = jnp.zeros((256, 256), F32)
    counts = jnp.zeros((16, 128), F32)
    for first in range(0, BLOCK, 4):
        a, b, p, q = [], [], [], []
        for s in range(first, first + 4):
            codes = msg_ref[s, 64:80, :]
            for t in range(2):
                high, low = codes[t : t + 1], codes[2 + t : 3 + t]
                part = msg_ref[s, 32 * t : 32 * t + 32, :]
                a.append(jnp.where(cluster == high, one, zero))
                b.append(jnp.concatenate([jnp.where(low == jnp.asarray(g, BF16), part, zero) for g in range(8)], 0))
                h, g = high.astype(F32).astype(I32), low.astype(F32).astype(I32)
                within = ((h >> 1) & 7) * 16 + (g & 3) * 4 + (g >> 2) * 2 + (h & 1)
                p.append(jnp.where(cluster[0:16] == (h >> 4).astype(F32).astype(BF16), one, zero))
                q.append(jnp.where(cluster[0:128] == within.astype(F32).astype(BF16), one, zero))
        a, b, p, q = (jnp.concatenate(blocks, 1) for blocks in (a, b, p, q))
        sums = sums + lax.dot_general(a, b, contract, preferred_element_type=F32)
        counts = counts + lax.dot_general(p, q, contract, preferred_element_type=F32)
    for m in range(16):
        at = 33 * PLANE_ORDER[m]
        out_ref[at : at + 16, :] = sums[16 * m : 16 * m + 16, 0:128]
        out_ref[at + 16 : at + 32, :] = sums[16 * m : 16 * m + 16, 128:256]
        out_ref[at + 32 : at + 33, :] = counts[m : m + 1, :]
    for k in range(2):
        codes = msg_ref[from_ref[0] ^ k, 64:80, :].astype(F32).astype(I32)
        rows_ref[2 * k : 2 * k + 2, :] = codes[4:6] * 8 + codes[6:8]


def regroup_kernel(in_ref, out_ref, s_ref):
    slot = lax.broadcasted_iota(I32, (32, 128), 1) // FEATS
    parts = []
    for x in range(4):
        first, *others = (in_ref[33 * at : 33 * at + 32, :] for at in range(x ^ PLANE_FIRST[1], 16, 4))
        parts.append((first + others[0]) + (others[1] + others[2]))
    first, *others = (in_ref[33 * 4 * zl + 32 : 33 * 4 * zl + 33, :] for zl in range(4))
    counts = (first + others[0]) + (others[1] + others[2])
    for low in range(4):
        rows = jnp.zeros((32, 128), F32)
        for x in range(4):
            shift = ((x - low) * FEATS) % 128
            moved = pltpu.roll(parts[x], shift, 1) if shift else parts[x]
            rows = jnp.where(slot == x, moved, rows)
        s_ref[...] = rows
        for zh in range(8):
            for r1 in range(2):
                at = 17 * (zh ^ FIRST_ZH) + 4 * low + 2 * r1
                out_ref[at : at + 2, :] = s_ref[16 * r1 + 2 * zh : 16 * r1 + 2 * zh + 2, :]
    for zh in range(8):
        at = 17 * zh + 16
        out_ref[at : at + 1, :] = counts


def finish_kernel(at_ref, in_ref, old_ref, out_ref):
    sums, count_row = in_ref[0:16, :], in_ref[16:17, :]
    for zh in range(1, 8):
        sums = sums + in_ref[17 * zh : 17 * zh + 16, :]
        count_row = count_row + in_ref[17 * zh + 16 : 17 * zh + 17, :]
    lane = lax.broadcasted_iota(I32, (16, 128), 1)
    own = lane == at_ref[0] + lax.broadcasted_iota(I32, (16, 128), 0)
    counts = jnp.sum(jnp.where(own, count_row, 0.0), axis=1, keepdims=True)
    out_ref[...] = (sums + old_ref[...]) / (counts + 1.0)


def member_kernel(of, after_ref, place_ref, rows_ref, *refs):
    line_refs, out_refs = refs[:3], refs[3:]
    core, y = place_ref[0], place_ref[1]
    r = rows_ref[2 * of : 2 * of + 2, :]
    away, far = (r >> 9) ^ y, ((r >> 8) & 1) ^ core
    block = jnp.where(away == 1 + 2 * core, 1 + far, jnp.where(far == 1, -1, jnp.where(away == 0, 0, jnp.where(away == 2, 3, -1))))
    at = jnp.where(block < 0, -1, (block << 8) + (r & 255))
    at = jnp.concatenate([at, jnp.zeros((6, 128), I32)], 0).astype(F32).T.astype(I32)
    at = jnp.concatenate([at[:, 0:1], at[:, 1:2]], 0)
    lane = lax.broadcasted_iota(I32, (256, ROWS), 1)
    total = jnp.zeros((256, 1024), F32)
    for first, line_ref in zip((0, 1, 3), line_refs):
        for k in range(line_ref.shape[0] // ROWS):
            pick = jnp.where(lane + ROWS * (first + k) == at, 1.0, 0.0).astype(BF16)
            rows = line_ref[ROWS * k : ROWS * k + ROWS, :]
            total = total + jnp.dot(pick, rows, preferred_element_type=F32)
    for s, out_ref in enumerate(out_refs):
        out_ref[...] = total[128 * s : 128 * s + 128].astype(BF16)


def match_kernel(len_hbm, *refs):
    i = lax.broadcasted_iota(I32, (128, 128), 0)
    j = lax.broadcasted_iota(I32, (128, 128), 1)
    own_refs, other_refs, (out_ref, len_ref, sem) = refs[0:2], refs[2:4], refs[4:7]
    lengths = pltpu.make_async_copy(len_hbm, len_ref, sem)
    lengths.start()
    i = lax.broadcasted_iota(I32, (128, 128), 0)
    j = lax.broadcasted_iota(I32, (128, 128), 1)
    cosines = []
    for s in range(2):
        one = own_refs[s][...] + other_refs[s][...]
        gram = lax.dot_general(one, one, (((1,), (1,)), ((), ())), preferred_element_type=F32)
        diagonal = jnp.where(i == j, gram, 0.0)
        down = lax.rsqrt(jnp.sum(diagonal, axis=1, keepdims=True) + 1e-06)
        across = lax.rsqrt(jnp.sum(diagonal, axis=0, keepdims=True) + 1e-06)
        cosines.append(gram * down * across)
    lengths.wait()
    for s in range(2):
        length = len_ref[s]
        largest = jnp.max(jnp.where((i < length) & (i != j), cosines[s], -2.0), axis=0, keepdims=True)
        out_ref[s : s + 1, :] = jnp.where(j[0:1] < length, largest, 0.0)


VMEM = pl.BlockSpec(memory_space=pltpu.VMEM)
HBM = pl.BlockSpec(memory_space=pltpu.HBM)
SMEM = pl.BlockSpec(memory_space=pltpu.SMEM)


def local(embeddings, assignments, old_centroids, slab_rows, slab_len):
    zh, x, y, core = (lax.axis_index(name).astype(I32) for name in ("zh", "x", "y", "c"))
    messages = pl.pallas_call(
        pack_kernel,
        out_shape=pltpu.HBM((4, 8, MSG, 128), BF16),
        in_specs=[HBM] * 3,
        out_specs=HBM,
        scratch_shapes=[
            pltpu.VMEM((ROWS, 1024), BF16),
            pltpu.VMEM((2, 128), I32),
            pltpu.VMEM((2, 128), I32),
            pltpu.VMEM((4, 8, MSG, 128), BF16),
            pltpu.SemaphoreType.DMA((2,)),
            pltpu.SemaphoreType.DMA((2,)),
            pltpu.SemaphoreType.DMA((2,)),
        ],
        compiler_params=params(8),
        cost_estimate=cost(1 << 20, 3 << 19),
        name="pack",
    )(*(pltpu.with_memory_space_constraint(a, pltpu.HBM) for a in (embeddings, assignments.reshape(2, 128), slab_rows)))
    messages = lax.all_to_all(messages.reshape(BLOCK, MSG, 128), ("x", "y", "c"), 0, 0, axis_index_groups=[BLOCK_ORDER], tiled=True)
    parts, rows = pl.pallas_call(
        sum_kernel,
        out_shape=(pltpu.VMEM((528, 128), F32), pltpu.VMEM((4, 128), I32)),
        in_specs=[SMEM, VMEM],
        out_specs=(VMEM, VMEM),
        compiler_params=params(20),
        cost_estimate=cost(1 << 31, 1 << 20),
        name="sums",
    )(((x * 8 + y * 2 + core) ^ BLOCK_ORDER[0]).reshape(1), messages)
    partner = lax.ppermute(embeddings, "c", [(0, 1), (1, 0)])
    embeddings, partner, parts = lax.optimization_barrier((embeddings, partner, parts))
    near = [(2 * i + c, 2 * (i ^ (1 + 2 * c)) + c) for i in range(4) for c in range(2)]
    line = [
        embeddings,
        lax.ppermute(jnp.concatenate([embeddings, partner]), ("y", "c"), near),
        lax.ppermute(embeddings, "y", [(i, i ^ 2) for i in range(4)]),
    ]
    parts = lax.all_to_all(parts.reshape(16, 33, 1, 128), ("zl", "x"), 0, 0, axis_index_groups=[PLANE_ORDER], tiled=True)
    parts = pl.pallas_call(
        regroup_kernel,
        out_shape=pltpu.VMEM((136, 128), F32),
        in_specs=[VMEM],
        out_specs=VMEM,
        scratch_shapes=[pltpu.VMEM((32, 128), F32)],
        compiler_params=params(4),
        cost_estimate=cost(1 << 18, 1 << 19),
        name="regroup",
    )(parts.reshape(528, 128))
    after = parts
    parts = lax.all_to_all(parts.reshape(8, 17, 1, 128), "zh", 0, 0, axis_index_groups=[RING_ORDER], tiled=True)
    place = jnp.stack([core, y])
    own, others = (
        pl.pallas_call(
            functools.partial(member_kernel, of),
            out_shape=[jax.ShapeDtypeStruct((128, 1024), BF16)] * 2,
            in_specs=[pl.BlockSpec(memory_space=pl.ANY), SMEM] + [VMEM] * 4,
            out_specs=[VMEM] * 2,
            compiler_params=params(16),
            cost_estimate=cost(0, 0),
            name="members",
        )(after, place, rows, *line)
        for of in range(2)
    )
    others = [lax.ppermute(other, "c", [(0, 1), (1, 0)]) for other in others]
    best_cosine = pl.pallas_call(
        match_kernel,
        out_shape=jax.ShapeDtypeStruct((2, 128), F32),
        in_specs=[HBM] + [VMEM] * 4,
        out_specs=VMEM,
        scratch_shapes=[pltpu.SMEM((2,), I32), pltpu.SemaphoreType.DMA],
        compiler_params=params(8),
        cost_estimate=cost(0, 0),
        name="match",
    )(pltpu.with_memory_space_constraint(slab_len, pltpu.HBM), *own, *others)
    parts, best_cosine = lax.optimization_barrier((parts, best_cosine))
    centroids = pl.pallas_call(
        finish_kernel,
        out_shape=jax.ShapeDtypeStruct((16, 128), F32),
        in_specs=[SMEM, VMEM, VMEM],
        out_specs=VMEM,
        compiler_params=params(4),
        cost_estimate=cost(1 << 18, 1 << 18),
        name="finish",
    )((zh * 16).reshape(1), parts.reshape(136, 128), old_centroids)
    return (centroids, best_cosine)


def solution(mesh):
    fine = Mesh(mesh.devices.reshape(SIZES), NAMES)
    dp, mp = ("zh", "zl", "x"), ("y", "c")
    placed = (
        P(dp + mp, None),
        P(dp + mp),
        P(dp, mp),
        P(dp + mp, None),
        P(dp + mp),
    )
    return jax.shard_map(
        local,
        mesh=fine,
        in_specs=placed,
        out_specs=(P(dp, mp), P(dp + mp, None)),
        check_vma=False,
    )
```

```python
import functools

import jax
import jax.numpy as jnp
from jax import lax
from jax.experimental import pallas as pl
from jax.experimental.pallas import tpu as pltpu
from jax.sharding import Mesh, PartitionSpec as P

F32, BF16, I32 = jnp.float32, jnp.bfloat16, jnp.int32
SIZES = (8, 4, 4, 4, 2)
NAMES = ("zh", "zl", "x", "y", "c")
BLOCK = 32
ROWS = 256
FEATS = 32
MSG = 80
MIB = 1 << 20
FIRST = (2, 4)
BLOCK_ORDER = [k ^ 20 for k in range(BLOCK)]
PLANE_FIRST = (1, 2)
PLANE_ORDER = [k ^ 6 for k in range(16)]
FIRST_ZH = 5
RING_ORDER = [k ^ FIRST_ZH for k in range(8)]


def params(mib):
    return pltpu.CompilerParams(vmem_limit_bytes=mib * MIB)


def cost(flops, moved):
    return pl.CostEstimate(flops=flops, bytes_accessed=moved, transcendentals=0)


def pack_kernel(emb_hbm, label_hbm, rows_hbm, out_hbm, emb_ref, label_ref, rows_ref, msg_ref, in_sems, out_sems, sems):
    small = [
        pltpu.make_async_copy(label_hbm, label_ref, sems.at[0]),
        pltpu.make_async_copy(rows_hbm, rows_ref, sems.at[1]),
    ]
    halves = [pl.ds(0, 512), pl.ds(512, 512)]
    blocks = [pltpu.make_async_copy(emb_hbm.at[:, at], emb_ref.at[:, at], in_sems.at[k]) for k, at in enumerate(halves)]
    for copy in blocks + small:
        copy.start()
    for copy in small:
        copy.wait()
    c, r = label_ref[...], rows_ref[...]
    high = ((c >> 6) & 3) * 64 + ((c >> 4) & 3) * 16 + (c >> 8) * 2 + (c & 1)
    low = ((c >> 1) & 1) * 4 + ((c >> 2) & 3)
    row = lax.broadcasted_iota(I32, (16, 128), 0)
    codes = jnp.zeros((16, 128), I32)
    for k, pair in enumerate((high, low, r >> 3, r & 7)):
        codes = jnp.where(row == 2 * k, pair[0:1], codes)
        codes = jnp.where(row == 2 * k + 1, pair[1:2], codes)
    codes = codes.astype(F32).astype(BF16)
    sent = []
    for k in range(2):
        blocks[k].wait()
        for mp in range(4 * k, 4 * k + 4):
            turned = emb_ref[:, 128 * mp : 128 * mp + 128].T
            for x in range(4):
                part, at = turned[x * FEATS : x * FEATS + FEATS], (x ^ FIRST[0], mp ^ FIRST[1])
                msg_ref[*at, 0:32, :] = part[:, 0:128]
                msg_ref[*at, 32:64, :] = part[:, 128:256]
                msg_ref[*at, 64:80, :] = codes
        at = pl.ds((4 * k) ^ FIRST[1], 4)
        sent.append(pltpu.make_async_copy(msg_ref.at[:, at], out_hbm.at[:, at], out_sems.at[k]))
        sent[k].start()
    for copy in sent:
        copy.wait()


def lanes(n):
    return lax.broadcasted_iota(I32, (n, 128), 0).astype(F32).astype(BF16)


def sum_kernel(from_ref, msg_ref, out_ref, rows_ref):
    cluster = lanes(256)
    one, zero = jnp.ones((), BF16), jnp.zeros((), BF16)
    contract = (((1,), (1,)), ((), ()))
    sums = jnp.zeros((256, 256), F32)
    for first in range(0, BLOCK, 4):
        a, b = [], []
        for s in range(first, first + 4):
            codes = msg_ref[s, 64:80, :]
            for t in range(2):
                high, low = codes[t : t + 1], codes[2 + t : 3 + t]
                part = msg_ref[s, 32 * t : 32 * t + 32, :]
                a.append(jnp.where(cluster == high, one, zero))
                b.append(jnp.concatenate([jnp.where(low == jnp.asarray(g, BF16), part, zero) for g in range(8)], 0))
        a, b = (jnp.concatenate(blocks, 1) for blocks in (a, b))
        sums = sums + lax.dot_general(a, b, contract, preferred_element_type=F32)
    p, q = [], []
    for k in range(8):
        codes = msg_ref[(from_ref[0] & 24) + k, 64:80, :].astype(F32).astype(I32)
        for t in range(2):
            high, low = codes[t : t + 1], codes[2 + t : 3 + t]
            within = ((high >> 1) & 7) * 16 + (low & 3) * 4 + (low >> 2) * 2 + (high & 1)
            p.append(jnp.where(cluster[0:16] == (high >> 4).astype(F32).astype(BF16), one, zero))
            q.append(jnp.where(cluster[0:128] == within.astype(F32).astype(BF16), one, zero))
    p, q = (jnp.concatenate(blocks, 1) for blocks in (p, q))
    counts = lax.dot_general(p, q, contract, preferred_element_type=F32)
    for m in range(16):
        at = 33 * PLANE_ORDER[m]
        out_ref[at : at + 16, :] = sums[16 * m : 16 * m + 16, 0:128]
        out_ref[at + 16 : at + 32, :] = sums[16 * m : 16 * m + 16, 128:256]
        out_ref[at + 32 : at + 33, :] = counts[m : m + 1, :]
    for k in range(2):
        codes = msg_ref[from_ref[0] ^ k, 64:80, :].astype(F32).astype(I32)
        rows_ref[2 * k : 2 * k + 2, :] = codes[4:6] * 8 + codes[6:8]


def regroup_kernel(in_ref, out_ref, s_ref):
    slot = lax.broadcasted_iota(I32, (32, 128), 1) // FEATS
    parts = []
    for x in range(4):
        first, *others = (in_ref[33 * at : 33 * at + 32, :] for at in range(x ^ PLANE_FIRST[1], 16, 4))
        parts.append((first + others[0]) + (others[1] + others[2]))
    counts = in_ref[32:33, :]
    for k in range(1, 16):
        counts = counts + in_ref[33 * k + 32 : 33 * k + 33, :]
    for low in range(4):
        rows = jnp.zeros((32, 128), F32)
        for x in range(4):
            shift = ((x - low) * FEATS) % 128
            moved = pltpu.roll(parts[x], shift, 1) if shift else parts[x]
            rows = jnp.where(slot == x, moved, rows)
        s_ref[...] = rows
        for zh in range(8):
            for r1 in range(2):
                at = 17 * (zh ^ FIRST_ZH) + 4 * low + 2 * r1
                out_ref[at : at + 2, :] = s_ref[16 * r1 + 2 * zh : 16 * r1 + 2 * zh + 2, :]
    for zh in range(8):
        at = 17 * zh + 16
        out_ref[at : at + 1, :] = counts


def finish_kernel(at_ref, in_ref, old_ref, out_ref):
    sums, count_row = in_ref[0:16, :], in_ref[16:17, :]
    for zh in range(1, 8):
        sums = sums + in_ref[17 * zh : 17 * zh + 16, :]
        count_row = count_row + in_ref[17 * zh + 16 : 17 * zh + 17, :]
    lane = lax.broadcasted_iota(I32, (16, 128), 1)
    own = lane == at_ref[0] + lax.broadcasted_iota(I32, (16, 128), 0)
    counts = jnp.sum(jnp.where(own, count_row, 0.0), axis=1, keepdims=True)
    out_ref[...] = (sums + old_ref[...]) / (counts + 1.0)


def member_kernel(of, after_ref, place_ref, rows_ref, *refs):
    line_refs, out_refs = refs[:3], refs[3:]
    core, y = place_ref[0], place_ref[1]
    r = rows_ref[2 * of : 2 * of + 2, :]
    away, far = (r >> 9) ^ y, ((r >> 8) & 1) ^ core
    block = jnp.where(away == 1 + 2 * core, 1 + far, jnp.where(far == 1, -1, jnp.where(away == 0, 0, jnp.where(away == 2, 3, -1))))
    at = jnp.where(block < 0, -1, (block << 8) + (r & 255))
    at = jnp.concatenate([at, jnp.zeros((6, 128), I32)], 0).astype(F32).T.astype(I32)
    at = jnp.concatenate([at[:, 0:1], at[:, 1:2]], 0)
    lane = lax.broadcasted_iota(I32, (256, ROWS), 1)
    total = jnp.zeros((256, 1024), F32)
    for first, line_ref in zip((0, 1, 3), line_refs):
        for k in range(line_ref.shape[0] // ROWS):
            pick = jnp.where(lane + ROWS * (first + k) == at, 1.0, 0.0).astype(BF16)
            rows = line_ref[ROWS * k : ROWS * k + ROWS, :]
            total = total + jnp.dot(pick, rows, preferred_element_type=F32)
    for s, out_ref in enumerate(out_refs):
        out_ref[...] = total[128 * s : 128 * s + 128].astype(BF16)


def match_kernel(len_hbm, *refs):
    i = lax.broadcasted_iota(I32, (128, 128), 0)
    j = lax.broadcasted_iota(I32, (128, 128), 1)
    own_refs, other_refs, (out_ref, len_ref, sem) = refs[0:2], refs[2:4], refs[4:7]
    lengths = pltpu.make_async_copy(len_hbm, len_ref, sem)
    lengths.start()
    i = lax.broadcasted_iota(I32, (128, 128), 0)
    j = lax.broadcasted_iota(I32, (128, 128), 1)
    cosines = []
    for s in range(2):
        one = own_refs[s][...] + other_refs[s][...]
        gram = lax.dot_general(one, one, (((1,), (1,)), ((), ())), preferred_element_type=F32)
        diagonal = jnp.where(i == j, gram, 0.0)
        down = lax.rsqrt(jnp.sum(diagonal, axis=1, keepdims=True) + 1e-06)
        across = lax.rsqrt(jnp.sum(diagonal, axis=0, keepdims=True) + 1e-06)
        cosines.append(gram * down * across)
    lengths.wait()
    for s in range(2):
        length = len_ref[s]
        largest = jnp.max(jnp.where((i < length) & (i != j), cosines[s], -2.0), axis=0, keepdims=True)
        out_ref[s : s + 1, :] = jnp.where(j[0:1] < length, largest, 0.0)


VMEM = pl.BlockSpec(memory_space=pltpu.VMEM)
HBM = pl.BlockSpec(memory_space=pltpu.HBM)
SMEM = pl.BlockSpec(memory_space=pltpu.SMEM)


def local(embeddings, assignments, old_centroids, slab_rows, slab_len):
    zh, x, y, core = (lax.axis_index(name).astype(I32) for name in ("zh", "x", "y", "c"))
    messages = pl.pallas_call(
        pack_kernel,
        out_shape=pltpu.HBM((4, 8, MSG, 128), BF16),
        in_specs=[HBM] * 3,
        out_specs=HBM,
        scratch_shapes=[
            pltpu.VMEM((ROWS, 1024), BF16),
            pltpu.VMEM((2, 128), I32),
            pltpu.VMEM((2, 128), I32),
            pltpu.VMEM((4, 8, MSG, 128), BF16),
            pltpu.SemaphoreType.DMA((2,)),
            pltpu.SemaphoreType.DMA((2,)),
            pltpu.SemaphoreType.DMA((2,)),
        ],
        compiler_params=params(8),
        cost_estimate=cost(1 << 20, 3 << 19),
        name="pack",
    )(*(pltpu.with_memory_space_constraint(a, pltpu.HBM) for a in (embeddings, assignments.reshape(2, 128), slab_rows)))
    messages = lax.all_to_all(messages.reshape(BLOCK, MSG, 128), ("x", "y", "c"), 0, 0, axis_index_groups=[BLOCK_ORDER], tiled=True)
    parts, rows = pl.pallas_call(
        sum_kernel,
        out_shape=(pltpu.VMEM((528, 128), F32), pltpu.VMEM((4, 128), I32)),
        in_specs=[SMEM, VMEM],
        out_specs=(VMEM, VMEM),
        compiler_params=params(20),
        cost_estimate=cost(1 << 31, 1 << 20),
        name="sums",
    )(((x * 8 + y * 2 + core) ^ BLOCK_ORDER[0]).reshape(1), messages)
    partner = lax.ppermute(embeddings, "c", [(0, 1), (1, 0)])
    embeddings, partner, parts = lax.optimization_barrier((embeddings, partner, parts))
    near = [(2 * i + c, 2 * (i ^ (1 + 2 * c)) + c) for i in range(4) for c in range(2)]
    line = [
        embeddings,
        lax.ppermute(jnp.concatenate([embeddings, partner]), ("y", "c"), near),
        lax.ppermute(embeddings, "y", [(i, i ^ 2) for i in range(4)]),
    ]
    parts = lax.all_to_all(parts.reshape(16, 33, 1, 128), ("zl", "x"), 0, 0, axis_index_groups=[PLANE_ORDER], tiled=True)
    parts = pl.pallas_call(
        regroup_kernel,
        out_shape=pltpu.VMEM((136, 128), F32),
        in_specs=[VMEM],
        out_specs=VMEM,
        scratch_shapes=[pltpu.VMEM((32, 128), F32)],
        compiler_params=params(4),
        cost_estimate=cost(1 << 18, 1 << 19),
        name="regroup",
    )(parts.reshape(528, 128))
    after = parts
    parts = lax.all_to_all(parts.reshape(8, 17, 1, 128), "zh", 0, 0, axis_index_groups=[RING_ORDER], tiled=True)
    place = jnp.stack([core, y])
    own, others = (
        pl.pallas_call(
            functools.partial(member_kernel, of),
            out_shape=[jax.ShapeDtypeStruct((128, 1024), BF16)] * 2,
            in_specs=[pl.BlockSpec(memory_space=pl.ANY), SMEM] + [VMEM] * 4,
            out_specs=[VMEM] * 2,
            compiler_params=params(16),
            cost_estimate=cost(0, 0),
            name="members",
        )(after, place, rows, *line)
        for of in range(2)
    )
    others = [lax.ppermute(other, "c", [(0, 1), (1, 0)]) for other in others]
    best_cosine = pl.pallas_call(
        match_kernel,
        out_shape=jax.ShapeDtypeStruct((2, 128), F32),
        in_specs=[HBM] + [VMEM] * 4,
        out_specs=VMEM,
        scratch_shapes=[pltpu.SMEM((2,), I32), pltpu.SemaphoreType.DMA],
        compiler_params=params(8),
        cost_estimate=cost(0, 0),
        name="match",
    )(pltpu.with_memory_space_constraint(slab_len, pltpu.HBM), *own, *others)
    parts, best_cosine = lax.optimization_barrier((parts, best_cosine))
    centroids = pl.pallas_call(
        finish_kernel,
        out_shape=jax.ShapeDtypeStruct((16, 128), F32),
        in_specs=[SMEM, VMEM, VMEM],
        out_specs=VMEM,
        compiler_params=params(4),
        cost_estimate=cost(1 << 18, 1 << 18),
        name="finish",
    )((zh * 16).reshape(1), parts.reshape(136, 128), old_centroids)
    return (centroids, best_cosine)


def solution(mesh):
    fine = Mesh(mesh.devices.reshape(SIZES), NAMES)
    dp, mp = ("zh", "zl", "x"), ("y", "c")
    placed = (
        P(dp + mp, None),
        P(dp + mp),
        P(dp, mp),
        P(dp + mp, None),
        P(dp + mp),
    )
    return jax.shard_map(
        local,
        mesh=fine,
        in_specs=placed,
        out_specs=(P(dp, mp), P(dp + mp, None)),
        check_vma=False,
    )
```

```python
import jax
import jax.numpy as jnp
from jax import lax
from jax.experimental import pallas as pl
from jax.experimental.pallas import tpu as pltpu
from jax.sharding import Mesh, PartitionSpec as P

F32, BF16, I32 = jnp.float32, jnp.bfloat16, jnp.int32
SIZES = (8, 4, 4, 4, 2)
NAMES = ("zh", "zl", "x", "y", "c")
BLOCK = 32
ROWS = 256
FEATS = 32
MSG = 80
MIB = 1 << 20
FIRST = (2, 4)
BLOCK_ORDER = [k ^ 20 for k in range(BLOCK)]
PLANE_FIRST = (1, 2)
PLANE_ORDER = [k ^ 6 for k in range(16)]
FIRST_ZH = 5
RING_ORDER = [k ^ FIRST_ZH for k in range(8)]


def params(mib):
    return pltpu.CompilerParams(vmem_limit_bytes=mib * MIB)


def cost(flops, moved):
    return pl.CostEstimate(flops=flops, bytes_accessed=moved, transcendentals=0)


def pack_kernel(emb_hbm, label_hbm, rows_hbm, len_hbm, out_hbm, emb_ref, label_ref, rows_ref, len_ref, msg_ref, in_sems, out_sems, sems):
    small = [
        pltpu.make_async_copy(label_hbm, label_ref, sems.at[0]),
        pltpu.make_async_copy(rows_hbm, rows_ref, sems.at[1]),
        pltpu.make_async_copy(len_hbm, len_ref, sems.at[2]),
    ]
    halves = [pl.ds(0, 512), pl.ds(512, 512)]
    blocks = [pltpu.make_async_copy(emb_hbm.at[:, at], emb_ref.at[:, at], in_sems.at[k]) for k, at in enumerate(halves)]
    for copy in blocks + small:
        copy.start()
    for copy in small:
        copy.wait()
    c, r = label_ref[...], rows_ref[...]
    high = ((c >> 6) & 3) * 64 + ((c >> 4) & 3) * 16 + (c >> 8) * 2 + (c & 1)
    low = ((c >> 1) & 1) * 4 + ((c >> 2) & 3)
    row = lax.broadcasted_iota(I32, (16, 128), 0)
    codes = jnp.zeros((16, 128), I32)
    for k, pair in enumerate((high, low, r >> 3, r & 7)):
        codes = jnp.where(row == 2 * k, pair[0:1], codes)
        codes = jnp.where(row == 2 * k + 1, pair[1:2], codes)
    for k in range(2):
        codes = jnp.where(row == 8 + k, len_ref[k], codes)
    codes = codes.astype(F32).astype(BF16)
    sent = []
    for k in range(2):
        blocks[k].wait()
        for mp in range(4 * k, 4 * k + 4):
            turned = emb_ref[:, 128 * mp : 128 * mp + 128].T
            for x in range(4):
                part, at = turned[x * FEATS : x * FEATS + FEATS], (x ^ FIRST[0], mp ^ FIRST[1])
                msg_ref[*at, 0:32, :] = part[:, 0:128]
                msg_ref[*at, 32:64, :] = part[:, 128:256]
                msg_ref[*at, 64:80, :] = codes
        at = pl.ds((4 * k) ^ FIRST[1], 4)
        sent.append(pltpu.make_async_copy(msg_ref.at[:, at], out_hbm.at[:, at], out_sems.at[k]))
        sent[k].start()
    for copy in sent:
        copy.wait()


def lanes(n):
    return lax.broadcasted_iota(I32, (n, 128), 0).astype(F32).astype(BF16)


def sum_kernel(from_ref, msg_ref, out_ref, rows_ref, len_ref):
    cluster = lanes(256)
    one, zero = jnp.ones((), BF16), jnp.zeros((), BF16)
    contract = (((1,), (1,)), ((), ()))
    sums = jnp.zeros((256, 256), F32)
    for first in range(0, BLOCK, 4):
        a, b = [], []
        for s in range(first, first + 4):
            codes = msg_ref[s, 64:80, :]
            for t in range(2):
                high, low = codes[t : t + 1], codes[2 + t : 3 + t]
                part = msg_ref[s, 32 * t : 32 * t + 32, :]
                a.append(jnp.where(cluster == high, one, zero))
                b.append(jnp.concatenate([jnp.where(low == jnp.asarray(g, BF16), part, zero) for g in range(8)], 0))
        a, b = (jnp.concatenate(blocks, 1) for blocks in (a, b))
        sums = sums + lax.dot_general(a, b, contract, preferred_element_type=F32)
    p, q = [], []
    for k in range(8):
        codes = msg_ref[(from_ref[0] & 24) + k, 64:80, :].astype(F32).astype(I32)
        for t in range(2):
            high, low = codes[t : t + 1], codes[2 + t : 3 + t]
            within = ((high >> 1) & 7) * 16 + (low & 3) * 4 + (low >> 2) * 2 + (high & 1)
            p.append(jnp.where(cluster[0:16] == (high >> 4).astype(F32).astype(BF16), one, zero))
            q.append(jnp.where(cluster[0:128] == within.astype(F32).astype(BF16), one, zero))
    p, q = (jnp.concatenate(blocks, 1) for blocks in (p, q))
    counts = lax.dot_general(p, q, contract, preferred_element_type=F32)
    for m in range(16):
        at = 33 * PLANE_ORDER[m]
        out_ref[at : at + 16, :] = sums[16 * m : 16 * m + 16, 0:128]
        out_ref[at + 16 : at + 32, :] = sums[16 * m : 16 * m + 16, 128:256]
        out_ref[at + 32 : at + 33, :] = counts[m : m + 1, :]
    for k in range(2):
        codes = msg_ref[from_ref[0] ^ k, 64:80, :].astype(F32).astype(I32)
        rows_ref[2 * k : 2 * k + 2, :] = codes[4:6] * 8 + codes[6:8]
        if k == 0:
            len_ref[...] = codes[8:10]


def regroup_kernel(in_ref, out_ref, s_ref):
    slot = lax.broadcasted_iota(I32, (32, 128), 1) // FEATS
    parts = []
    for x in range(4):
        first, *others = (in_ref[33 * at : 33 * at + 32, :] for at in range(x ^ PLANE_FIRST[1], 16, 4))
        parts.append((first + others[0]) + (others[1] + others[2]))
    counts = in_ref[32:33, :]
    for k in range(1, 16):
        counts = counts + in_ref[33 * k + 32 : 33 * k + 33, :]
    for low in range(4):
        rows = jnp.zeros((32, 128), F32)
        for x in range(4):
            shift = ((x - low) * FEATS) % 128
            moved = pltpu.roll(parts[x], shift, 1) if shift else parts[x]
            rows = jnp.where(slot == x, moved, rows)
        s_ref[...] = rows
        for zh in range(8):
            for r1 in range(2):
                at = 17 * (zh ^ FIRST_ZH) + 4 * low + 2 * r1
                out_ref[at : at + 2, :] = s_ref[16 * r1 + 2 * zh : 16 * r1 + 2 * zh + 2, :]
    for zh in range(8):
        at = 17 * zh + 16
        out_ref[at : at + 1, :] = counts


def finish_kernel(at_ref, in_ref, old_ref, out_ref):
    sums, count_row = in_ref[0:16, :], in_ref[16:17, :]
    for zh in range(1, 8):
        sums = sums + in_ref[17 * zh : 17 * zh + 16, :]
        count_row = count_row + in_ref[17 * zh + 16 : 17 * zh + 17, :]
    lane = lax.broadcasted_iota(I32, (16, 128), 1)
    own = lane == at_ref[0] + lax.broadcasted_iota(I32, (16, 128), 0)
    counts = jnp.sum(jnp.where(own, count_row, 0.0), axis=1, keepdims=True)
    out_ref[...] = (sums + old_ref[...]) / (counts + 1.0)


def member_kernel(after_ref, place_ref, rows_ref, *refs):
    line_refs, (own_ref, *other_refs) = refs[:3], refs[3:]
    core, y = place_ref[0], place_ref[1]
    r = rows_ref[...]
    away, far = (r >> 9) ^ y, ((r >> 8) & 1) ^ core
    block = jnp.where(away == 1 + 2 * core, 1 + far, jnp.where(far == 1, -1, jnp.where(away == 0, 0, jnp.where(away == 2, 3, -1))))
    at = jnp.where(block < 0, -1, (block << 8) + (r & 255))
    at = jnp.concatenate([at, jnp.zeros((4, 128), I32)], 0).astype(F32).T.astype(I32)
    at = jnp.concatenate([at[:, s : s + 1] for s in range(4)], 0)
    lane = lax.broadcasted_iota(I32, (512, ROWS), 1)
    picks = [jnp.where(lane + ROWS * k == at, 1.0, 0.0).astype(BF16) for k in range(4)]
    for n in range(0, 1024, 256):
        blocks = [line_ref[k : k + ROWS, n : n + 256] for line_ref in line_refs for k in range(0, line_ref.shape[0], ROWS)]
        total = sum(jnp.dot(pick, block, preferred_element_type=F32) for pick, block in zip(picks, blocks)).astype(BF16)
        own_ref[:, n : n + 256] = total[0:256]
        for s in range(2):
            other_refs[s][:, n : n + 256] = total[256 + 128 * s : 384 + 128 * s]


def match_kernel(len_ref, own_ref, *refs):
    *other_refs, out_ref = refs
    i = lax.broadcasted_iota(I32, (128, 128), 0)
    j = lax.broadcasted_iota(I32, (128, 128), 1)
    for s in range(2):
        one = own_ref[128 * s : 128 * s + 128, :] + other_refs[s][...]
        gram = lax.dot_general(one, one, (((1,), (1,)), ((), ())), preferred_element_type=F32)
        diagonal = jnp.where(i == j, gram, 0.0)
        down = lax.rsqrt(jnp.sum(diagonal, axis=1, keepdims=True) + 1e-06)
        across = lax.rsqrt(jnp.sum(diagonal, axis=0, keepdims=True) + 1e-06)
        cosine = gram * down * across
        length = len_ref[s : s + 1, :]
        largest = jnp.max(jnp.where((i < length) & (i != j), cosine, -2.0), axis=0, keepdims=True)
        out_ref[s : s + 1, :] = jnp.where(j[0:1] < length, largest, 0.0)


VMEM = pl.BlockSpec(memory_space=pltpu.VMEM)
HBM = pl.BlockSpec(memory_space=pltpu.HBM)
SMEM = pl.BlockSpec(memory_space=pltpu.SMEM)


def local(embeddings, assignments, old_centroids, slab_rows, slab_len):
    zh, x, y, core = (lax.axis_index(name).astype(I32) for name in ("zh", "x", "y", "c"))
    messages = pl.pallas_call(
        pack_kernel,
        out_shape=pltpu.HBM((4, 8, MSG, 128), BF16),
        in_specs=[HBM] * 4,
        out_specs=HBM,
        scratch_shapes=[
            pltpu.VMEM((ROWS, 1024), BF16),
            pltpu.VMEM((2, 128), I32),
            pltpu.VMEM((2, 128), I32),
            pltpu.SMEM((2,), I32),
            pltpu.VMEM((4, 8, MSG, 128), BF16),
            pltpu.SemaphoreType.DMA((2,)),
            pltpu.SemaphoreType.DMA((2,)),
            pltpu.SemaphoreType.DMA((3,)),
        ],
        compiler_params=params(8),
        cost_estimate=cost(1 << 20, 3 << 19),
        name="pack",
    )(*(pltpu.with_memory_space_constraint(a, pltpu.HBM) for a in (embeddings, assignments.reshape(2, 128), slab_rows, slab_len)))
    messages = lax.all_to_all(messages.reshape(BLOCK, MSG, 128), ("x", "y", "c"), 0, 0, axis_index_groups=[BLOCK_ORDER], tiled=True)
    parts, rows, lengths = pl.pallas_call(
        sum_kernel,
        out_shape=(pltpu.VMEM((528, 128), F32), pltpu.VMEM((4, 128), I32), pltpu.VMEM((2, 128), I32)),
        in_specs=[SMEM, VMEM],
        out_specs=(VMEM, VMEM, VMEM),
        compiler_params=params(20),
        cost_estimate=cost(1 << 31, 1 << 20),
        name="sums",
    )(((x * 8 + y * 2 + core) ^ BLOCK_ORDER[0]).reshape(1), messages)
    partner = lax.ppermute(embeddings, "c", [(0, 1), (1, 0)])
    embeddings, partner, parts = lax.optimization_barrier((embeddings, partner, parts))
    near = [(2 * i + c, 2 * (i ^ (1 + 2 * c)) + c) for i in range(4) for c in range(2)]
    line = [
        embeddings,
        lax.ppermute(jnp.concatenate([embeddings, partner]), ("y", "c"), near),
        lax.ppermute(embeddings, "y", [(i, i ^ 2) for i in range(4)]),
    ]
    parts = lax.all_to_all(parts.reshape(16, 33, 1, 128), ("zl", "x"), 0, 0, axis_index_groups=[PLANE_ORDER], tiled=True)
    parts = pl.pallas_call(
        regroup_kernel,
        out_shape=pltpu.VMEM((136, 128), F32),
        in_specs=[VMEM],
        out_specs=VMEM,
        scratch_shapes=[pltpu.VMEM((32, 128), F32)],
        compiler_params=params(4),
        cost_estimate=cost(1 << 18, 1 << 19),
        name="regroup",
    )(parts.reshape(528, 128))
    after = parts
    parts = lax.all_to_all(parts.reshape(8, 17, 1, 128), "zh", 0, 0, axis_index_groups=[RING_ORDER], tiled=True)
    place = jnp.stack([core, y])
    own, *others = pl.pallas_call(
        member_kernel,
        out_shape=[jax.ShapeDtypeStruct((n, 1024), BF16) for n in (256, 128, 128)],
        in_specs=[pl.BlockSpec(memory_space=pl.ANY), SMEM] + [VMEM] * 4,
        out_specs=[VMEM] * 3,
        compiler_params=params(16),
        cost_estimate=cost(0, 0),
        name="members",
    )(after, place, rows, *line)
    others = [lax.ppermute(other, "c", [(0, 1), (1, 0)]) for other in others]
    best_cosine = pl.pallas_call(
        match_kernel,
        out_shape=jax.ShapeDtypeStruct((2, 128), F32),
        in_specs=[VMEM] * 4,
        out_specs=VMEM,
        compiler_params=params(8),
        cost_estimate=cost(0, 0),
        name="match",
    )(lengths, own, *others)
    parts, best_cosine = lax.optimization_barrier((parts, best_cosine))
    centroids = pl.pallas_call(
        finish_kernel,
        out_shape=jax.ShapeDtypeStruct((16, 128), F32),
        in_specs=[SMEM, VMEM, VMEM],
        out_specs=VMEM,
        compiler_params=params(4),
        cost_estimate=cost(1 << 18, 1 << 18),
        name="finish",
    )((zh * 16).reshape(1), parts.reshape(136, 128), old_centroids)
    return (centroids, best_cosine)


def solution(mesh):
    fine = Mesh(mesh.devices.reshape(SIZES), NAMES)
    dp, mp = ("zh", "zl", "x"), ("y", "c")
    placed = (
        P(dp + mp, None),
        P(dp + mp),
        P(dp, mp),
        P(dp + mp, None),
        P(dp + mp),
    )
    return jax.shard_map(
        local,
        mesh=fine,
        in_specs=placed,
        out_specs=(P(dp, mp), P(dp + mp, None)),
        check_vma=False,
    )
```

```python
import functools

import jax
import jax.numpy as jnp
from jax import lax
from jax.experimental import pallas as pl
from jax.experimental.pallas import tpu as pltpu
from jax.sharding import Mesh, PartitionSpec as P

F32, BF16, I32 = jnp.float32, jnp.bfloat16, jnp.int32
SIZES = (8, 4, 4, 4, 2)
NAMES = ("zh", "zl", "x", "y", "c")
BLOCK = 32
ROWS = 256
FEATS = 32
MSG = 80
MIB = 1 << 20
FIRST = (2, 4)
BLOCK_ORDER = [k ^ 20 for k in range(BLOCK)]
PLANE_FIRST = (1, 2)
PLANE_ORDER = [k ^ 6 for k in range(16)]
FIRST_ZH = 5
RING_ORDER = [k ^ FIRST_ZH for k in range(8)]


def params(mib):
    return pltpu.CompilerParams(vmem_limit_bytes=mib * MIB)


def cost(flops, moved):
    return pl.CostEstimate(flops=flops, bytes_accessed=moved, transcendentals=0)


def pack_kernel(emb_hbm, label_hbm, rows_hbm, len_hbm, out_hbm, emb_ref, label_ref, rows_ref, len_ref, msg_ref, in_sems, out_sems, sems):
    small = [
        pltpu.make_async_copy(label_hbm, label_ref, sems.at[0]),
        pltpu.make_async_copy(rows_hbm, rows_ref, sems.at[1]),
        pltpu.make_async_copy(len_hbm, len_ref, sems.at[2]),
    ]
    halves = [pl.ds(0, 512), pl.ds(512, 512)]
    blocks = [pltpu.make_async_copy(emb_hbm.at[:, at], emb_ref.at[:, at], in_sems.at[k]) for k, at in enumerate(halves)]
    for copy in blocks + small:
        copy.start()
    for copy in small:
        copy.wait()
    c, r = label_ref[...], rows_ref[...]
    high = ((c >> 6) & 3) * 64 + ((c >> 4) & 3) * 16 + (c >> 8) * 2 + (c & 1)
    low = ((c >> 1) & 1) * 4 + ((c >> 2) & 3)
    row = lax.broadcasted_iota(I32, (16, 128), 0)
    codes = jnp.zeros((16, 128), I32)
    for k, pair in enumerate((high, low, r >> 3, r & 7)):
        codes = jnp.where(row == 2 * k, pair[0:1], codes)
        codes = jnp.where(row == 2 * k + 1, pair[1:2], codes)
    for k in range(2):
        codes = jnp.where(row == 8 + k, len_ref[k], codes)
    codes = codes.astype(F32).astype(BF16)
    sent = []
    for k in range(2):
        blocks[k].wait()
        for mp in range(4 * k, 4 * k + 4):
            turned = emb_ref[:, 128 * mp : 128 * mp + 128].T
            for x in range(4):
                part, at = turned[x * FEATS : x * FEATS + FEATS], (x ^ FIRST[0], mp ^ FIRST[1])
                msg_ref[*at, 0:32, :] = part[:, 0:128]
                msg_ref[*at, 32:64, :] = part[:, 128:256]
                msg_ref[*at, 64:80, :] = codes
        at = pl.ds((4 * k) ^ FIRST[1], 4)
        sent.append(pltpu.make_async_copy(msg_ref.at[:, at], out_hbm.at[:, at], out_sems.at[k]))
        sent[k].start()
    for copy in sent:
        copy.wait()


def lanes(n):
    return lax.broadcasted_iota(I32, (n, 128), 0).astype(F32).astype(BF16)


def sum_kernel(from_ref, msg_ref, out_ref, rows_ref, len_ref):
    cluster = lanes(256)
    one, zero = jnp.ones((), BF16), jnp.zeros((), BF16)
    contract = (((1,), (1,)), ((), ()))
    sums = jnp.zeros((256, 256), F32)
    for first in range(0, BLOCK, 4):
        a, b = [], []
        for s in range(first, first + 4):
            codes = msg_ref[s, 64:80, :]
            for t in range(2):
                high, low = codes[t : t + 1], codes[2 + t : 3 + t]
                part = msg_ref[s, 32 * t : 32 * t + 32, :]
                a.append(jnp.where(cluster == high, one, zero))
                b.append(jnp.concatenate([jnp.where(low == jnp.asarray(g, BF16), part, zero) for g in range(8)], 0))
        a, b = (jnp.concatenate(blocks, 1) for blocks in (a, b))
        sums = sums + lax.dot_general(a, b, contract, preferred_element_type=F32)
    p, q = [], []
    for k in range(8):
        codes = msg_ref[(from_ref[0] & 24) + k, 64:80, :].astype(F32).astype(I32)
        for t in range(2):
            high, low = codes[t : t + 1], codes[2 + t : 3 + t]
            within = ((high >> 1) & 7) * 16 + (low & 3) * 4 + (low >> 2) * 2 + (high & 1)
            p.append(jnp.where(cluster[0:16] == (high >> 4).astype(F32).astype(BF16), one, zero))
            q.append(jnp.where(cluster[0:128] == within.astype(F32).astype(BF16), one, zero))
    p, q = (jnp.concatenate(blocks, 1) for blocks in (p, q))
    counts = lax.dot_general(p, q, contract, preferred_element_type=F32)
    for m in range(16):
        at = 33 * PLANE_ORDER[m]
        out_ref[at : at + 16, :] = sums[16 * m : 16 * m + 16, 0:128]
        out_ref[at + 16 : at + 32, :] = sums[16 * m : 16 * m + 16, 128:256]
        out_ref[at + 32 : at + 33, :] = counts[m : m + 1, :]
    for k in range(2):
        codes = msg_ref[from_ref[0] ^ k, 64:80, :].astype(F32).astype(I32)
        rows_ref[2 * k : 2 * k + 2, :] = codes[4:6] * 8 + codes[6:8]
        if k == 0:
            len_ref[...] = codes[8:10]


def regroup_kernel(in_ref, out_ref, s_ref):
    slot = lax.broadcasted_iota(I32, (32, 128), 1) // FEATS
    parts = []
    for x in range(4):
        first, *others = (in_ref[33 * at : 33 * at + 32, :] for at in range(x ^ PLANE_FIRST[1], 16, 4))
        parts.append((first + others[0]) + (others[1] + others[2]))
    counts = in_ref[32:33, :]
    for k in range(1, 16):
        counts = counts + in_ref[33 * k + 32 : 33 * k + 33, :]
    for low in range(4):
        rows = jnp.zeros((32, 128), F32)
        for x in range(4):
            shift = ((x - low) * FEATS) % 128
            moved = pltpu.roll(parts[x], shift, 1) if shift else parts[x]
            rows = jnp.where(slot == x, moved, rows)
        s_ref[...] = rows
        for zh in range(8):
            for r1 in range(2):
                at = 17 * (zh ^ FIRST_ZH) + 4 * low + 2 * r1
                out_ref[at : at + 2, :] = s_ref[16 * r1 + 2 * zh : 16 * r1 + 2 * zh + 2, :]
    for zh in range(8):
        at = 17 * zh + 16
        out_ref[at : at + 1, :] = counts


def finish_kernel(at_ref, in_ref, old_ref, out_ref):
    sums, count_row = in_ref[0:16, :], in_ref[16:17, :]
    for zh in range(1, 8):
        sums = sums + in_ref[17 * zh : 17 * zh + 16, :]
        count_row = count_row + in_ref[17 * zh + 16 : 17 * zh + 17, :]
    lane = lax.broadcasted_iota(I32, (16, 128), 1)
    own = lane == at_ref[0] + lax.broadcasted_iota(I32, (16, 128), 0)
    counts = jnp.sum(jnp.where(own, count_row, 0.0), axis=1, keepdims=True)
    out_ref[...] = (sums + old_ref[...]) / (counts + 1.0)


def member_kernel(of, after_ref, place_ref, rows_ref, *refs):
    line_refs, out_refs = refs[:3], refs[3:]
    core, y = place_ref[0], place_ref[1]
    r = rows_ref[2 * of : 2 * of + 2, :]
    away, far = (r >> 9) ^ y, ((r >> 8) & 1) ^ core
    block = jnp.where(away == 1 + 2 * core, 1 + far, jnp.where(far == 1, -1, jnp.where(away == 0, 0, jnp.where(away == 2, 3, -1))))
    at = jnp.where(block < 0, -1, (block << 8) + (r & 255))
    at = jnp.concatenate([at, jnp.zeros((6, 128), I32)], 0).astype(F32).T.astype(I32)
    at = jnp.concatenate([at[:, 0:1], at[:, 1:2]], 0)
    lane = lax.broadcasted_iota(I32, (256, ROWS), 1)
    total = jnp.zeros((256, 1024), F32)
    for first, line_ref in zip((0, 1, 3), line_refs):
        for k in range(line_ref.shape[0] // ROWS):
            pick = jnp.where(lane + ROWS * (first + k) == at, 1.0, 0.0).astype(BF16)
            rows = line_ref[ROWS * k : ROWS * k + ROWS, :]
            total = total + jnp.dot(pick, rows, preferred_element_type=F32)
    for s, out_ref in enumerate(out_refs):
        out_ref[...] = total[128 * s : 128 * s + 128].astype(BF16)


def match_kernel(len_ref, *refs):
    own_refs, other_refs, out_ref = refs[0:2], refs[2:4], refs[4]
    i = lax.broadcasted_iota(I32, (128, 128), 0)
    j = lax.broadcasted_iota(I32, (128, 128), 1)
    for s in range(2):
        one = own_refs[s][...] + other_refs[s][...]
        gram = lax.dot_general(one, one, (((1,), (1,)), ((), ())), preferred_element_type=F32)
        diagonal = jnp.where(i == j, gram, 0.0)
        down = lax.rsqrt(jnp.sum(diagonal, axis=1, keepdims=True) + 1e-06)
        across = lax.rsqrt(jnp.sum(diagonal, axis=0, keepdims=True) + 1e-06)
        cosine = gram * down * across
        length = len_ref[s : s + 1, :]
        largest = jnp.max(jnp.where((i < length) & (i != j), cosine, -2.0), axis=0, keepdims=True)
        out_ref[s : s + 1, :] = jnp.where(j[0:1] < length, largest, 0.0)


VMEM = pl.BlockSpec(memory_space=pltpu.VMEM)
HBM = pl.BlockSpec(memory_space=pltpu.HBM)
SMEM = pl.BlockSpec(memory_space=pltpu.SMEM)


def local(embeddings, assignments, old_centroids, slab_rows, slab_len):
    zh, x, y, core = (lax.axis_index(name).astype(I32) for name in ("zh", "x", "y", "c"))
    messages = pl.pallas_call(
        pack_kernel,
        out_shape=pltpu.HBM((4, 8, MSG, 128), BF16),
        in_specs=[HBM] * 4,
        out_specs=HBM,
        scratch_shapes=[
            pltpu.VMEM((ROWS, 1024), BF16),
            pltpu.VMEM((2, 128), I32),
            pltpu.VMEM((2, 128), I32),
            pltpu.SMEM((2,), I32),
            pltpu.VMEM((4, 8, MSG, 128), BF16),
            pltpu.SemaphoreType.DMA((2,)),
            pltpu.SemaphoreType.DMA((2,)),
            pltpu.SemaphoreType.DMA((3,)),
        ],
        compiler_params=params(8),
        cost_estimate=cost(1 << 20, 3 << 19),
        name="pack",
    )(*(pltpu.with_memory_space_constraint(a, pltpu.HBM) for a in (embeddings, assignments.reshape(2, 128), slab_rows, slab_len)))
    messages = lax.all_to_all(messages.reshape(BLOCK, MSG, 128), ("x", "y", "c"), 0, 0, axis_index_groups=[BLOCK_ORDER], tiled=True)
    parts, rows, lengths = pl.pallas_call(
        sum_kernel,
        out_shape=(pltpu.VMEM((528, 128), F32), pltpu.VMEM((4, 128), I32), pltpu.VMEM((2, 128), I32)),
        in_specs=[SMEM, VMEM],
        out_specs=(VMEM, VMEM, VMEM),
        compiler_params=params(20),
        cost_estimate=cost(1 << 31, 1 << 20),
        name="sums",
    )(((x * 8 + y * 2 + core) ^ BLOCK_ORDER[0]).reshape(1), messages)
    partner = lax.ppermute(embeddings, "c", [(0, 1), (1, 0)])
    embeddings, partner, parts = lax.optimization_barrier((embeddings, partner, parts))
    near = [(2 * i + c, 2 * (i ^ (1 + 2 * c)) + c) for i in range(4) for c in range(2)]
    line = [
        embeddings,
        lax.ppermute(jnp.concatenate([embeddings, partner]), ("y", "c"), near),
        lax.ppermute(embeddings, "y", [(i, i ^ 2) for i in range(4)]),
    ]
    parts = lax.all_to_all(parts.reshape(16, 33, 1, 128), ("zl", "x"), 0, 0, axis_index_groups=[PLANE_ORDER], tiled=True)
    parts = pl.pallas_call(
        regroup_kernel,
        out_shape=pltpu.VMEM((136, 128), F32),
        in_specs=[VMEM],
        out_specs=VMEM,
        scratch_shapes=[pltpu.VMEM((32, 128), F32)],
        compiler_params=params(4),
        cost_estimate=cost(1 << 18, 1 << 19),
        name="regroup",
    )(parts.reshape(528, 128))
    after = parts
    parts = lax.all_to_all(parts.reshape(8, 17, 1, 128), "zh", 0, 0, axis_index_groups=[RING_ORDER], tiled=True)
    place = jnp.stack([core, y])
    own, others = (
        pl.pallas_call(
            functools.partial(member_kernel, of),
            out_shape=[jax.ShapeDtypeStruct((128, 1024), BF16)] * 2,
            in_specs=[pl.BlockSpec(memory_space=pl.ANY), SMEM] + [VMEM] * 4,
            out_specs=[VMEM] * 2,
            compiler_params=params(16),
            cost_estimate=cost(0, 0),
            name="members",
        )(after, place, rows, *line)
        for of in range(2)
    )
    others = [lax.ppermute(other, "c", [(0, 1), (1, 0)]) for other in others]
    best_cosine = pl.pallas_call(
        match_kernel,
        out_shape=jax.ShapeDtypeStruct((2, 128), F32),
        in_specs=[VMEM] * 5,
        out_specs=VMEM,
        compiler_params=params(8),
        cost_estimate=cost(0, 0),
        name="match",
    )(lengths, *own, *others)
    parts, best_cosine = lax.optimization_barrier((parts, best_cosine))
    centroids = pl.pallas_call(
        finish_kernel,
        out_shape=jax.ShapeDtypeStruct((16, 128), F32),
        in_specs=[SMEM, VMEM, VMEM],
        out_specs=VMEM,
        compiler_params=params(4),
        cost_estimate=cost(1 << 18, 1 << 18),
        name="finish",
    )((zh * 16).reshape(1), parts.reshape(136, 128), old_centroids)
    return (centroids, best_cosine)


def solution(mesh):
    fine = Mesh(mesh.devices.reshape(SIZES), NAMES)
    dp, mp = ("zh", "zl", "x"), ("y", "c")
    placed = (
        P(dp + mp, None),
        P(dp + mp),
        P(dp, mp),
        P(dp + mp, None),
        P(dp + mp),
    )
    return jax.shard_map(
        local,
        mesh=fine,
        in_specs=placed,
        out_specs=(P(dp, mp), P(dp + mp, None)),
        check_vma=False,
    )
```

```python
import functools

import jax
import jax.numpy as jnp
from jax import lax
from jax.experimental import pallas as pl
from jax.experimental.pallas import tpu as pltpu
from jax.sharding import Mesh, PartitionSpec as P

F32, BF16, I32 = jnp.float32, jnp.bfloat16, jnp.int32
SIZES = (8, 4, 4, 4, 2)
NAMES = ("zh", "zl", "x", "y", "c")
BLOCK = 32
ROWS = 256
FEATS = 32
MSG = 80
MIB = 1 << 20
FIRST = (2, 4)
BLOCK_ORDER = [k ^ 20 for k in range(BLOCK)]
PLANE_FIRST = (1, 2)
PLANE_ORDER = [k ^ 6 for k in range(16)]
FIRST_ZH = 5
RING_ORDER = [k ^ FIRST_ZH for k in range(8)]


def params(mib):
    return pltpu.CompilerParams(vmem_limit_bytes=mib * MIB)


def cost(flops, moved):
    return pl.CostEstimate(flops=flops, bytes_accessed=moved, transcendentals=0)


def pack_kernel(emb_hbm, label_hbm, rows_hbm, len_hbm, out_hbm, emb_ref, label_ref, rows_ref, len_ref, msg_ref, in_sems, out_sems, sems):
    small = [
        pltpu.make_async_copy(label_hbm, label_ref, sems.at[0]),
        pltpu.make_async_copy(rows_hbm, rows_ref, sems.at[1]),
        pltpu.make_async_copy(len_hbm, len_ref, sems.at[2]),
    ]
    halves = [pl.ds(0, 512), pl.ds(512, 512)]
    blocks = [pltpu.make_async_copy(emb_hbm.at[:, at], emb_ref.at[:, at], in_sems.at[k]) for k, at in enumerate(halves)]
    for copy in blocks + small:
        copy.start()
    for copy in small:
        copy.wait()
    c, r = label_ref[...], rows_ref[...]
    high = ((c >> 6) & 3) * 64 + ((c >> 4) & 3) * 16 + (c >> 8) * 2 + (c & 1)
    low = ((c >> 1) & 1) * 4 + ((c >> 2) & 3)
    row = lax.broadcasted_iota(I32, (16, 128), 0)
    codes = jnp.zeros((16, 128), I32)
    for k, pair in enumerate((high, low, r >> 3, r & 7)):
        codes = jnp.where(row == 2 * k, pair[0:1], codes)
        codes = jnp.where(row == 2 * k + 1, pair[1:2], codes)
    for k in range(2):
        codes = jnp.where(row == 8 + k, len_ref[k], codes)
    codes = codes.astype(F32).astype(BF16)
    sent = []
    for k in range(2):
        blocks[k].wait()
        for mp in range(4 * k, 4 * k + 4):
            turned = emb_ref[:, 128 * mp : 128 * mp + 128].T
            for x in range(4):
                part, at = turned[x * FEATS : x * FEATS + FEATS], (x ^ FIRST[0], mp ^ FIRST[1])
                msg_ref[*at, 0:32, :] = part[:, 0:128]
                msg_ref[*at, 32:64, :] = part[:, 128:256]
                msg_ref[*at, 64:80, :] = codes
        at = pl.ds((4 * k) ^ FIRST[1], 4)
        sent.append(pltpu.make_async_copy(msg_ref.at[:, at], out_hbm.at[:, at], out_sems.at[k]))
        sent[k].start()
    for copy in sent:
        copy.wait()


def lanes(n):
    return lax.broadcasted_iota(I32, (n, 128), 0).astype(F32).astype(BF16)


def sum_kernel(from_ref, msg_ref, out_ref, rows_ref, len_ref):
    cluster = lanes(256)
    one, zero = jnp.ones((), BF16), jnp.zeros((), BF16)
    contract = (((1,), (1,)), ((), ()))
    sums = jnp.zeros((256, 256), F32)
    for first in range(0, BLOCK, 4):
        a, b = [], []
        for s in range(first, first + 4):
            codes = msg_ref[s, 64:80, :]
            for t in range(2):
                high, low = codes[t : t + 1], codes[2 + t : 3 + t]
                part = msg_ref[s, 32 * t : 32 * t + 32, :]
                a.append(jnp.where(cluster == high, one, zero))
                b.append(jnp.concatenate([jnp.where(low == jnp.asarray(g, BF16), part, zero) for g in range(8)], 0))
        a, b = (jnp.concatenate(blocks, 1) for blocks in (a, b))
        sums = sums + lax.dot_general(a, b, contract, preferred_element_type=F32)
    p, q = [], []
    for k in range(8):
        codes = msg_ref[(from_ref[0] & 24) + k, 64:80, :].astype(F32).astype(I32)
        for t in range(2):
            high, low = codes[t : t + 1], codes[2 + t : 3 + t]
            within = ((high >> 1) & 7) * 16 + (low & 3) * 4 + (low >> 2) * 2 + (high & 1)
            p.append(jnp.where(cluster[0:16] == (high >> 4).astype(F32).astype(BF16), one, zero))
            q.append(jnp.where(cluster[0:128] == within.astype(F32).astype(BF16), one, zero))
    p, q = (jnp.concatenate(blocks, 1) for blocks in (p, q))
    counts = lax.dot_general(p, q, contract, preferred_element_type=F32)
    for m in range(16):
        at = 33 * PLANE_ORDER[m]
        out_ref[at : at + 16, :] = sums[16 * m : 16 * m + 16, 0:128]
        out_ref[at + 16 : at + 32, :] = sums[16 * m : 16 * m + 16, 128:256]
        out_ref[at + 32 : at + 33, :] = counts[m : m + 1, :]
    for k in range(2):
        codes = msg_ref[from_ref[0] ^ k, 64:80, :].astype(F32).astype(I32)
        rows_ref[2 * k : 2 * k + 2, :] = codes[4:6] * 8 + codes[6:8]
        if k == 0:
            len_ref[...] = codes[8:10]


def regroup_kernel(in_ref, out_ref, s_ref):
    slot = lax.broadcasted_iota(I32, (32, 128), 1) // FEATS
    parts = []
    for x in range(4):
        first, *others = (in_ref[33 * at : 33 * at + 32, :] for at in range(x ^ PLANE_FIRST[1], 16, 4))
        parts.append((first + others[0]) + (others[1] + others[2]))
    counts = in_ref[32:33, :]
    for k in range(1, 16):
        counts = counts + in_ref[33 * k + 32 : 33 * k + 33, :]
    for low in range(4):
        rows = jnp.zeros((32, 128), F32)
        for x in range(4):
            shift = ((x - low) * FEATS) % 128
            moved = pltpu.roll(parts[x], shift, 1) if shift else parts[x]
            rows = jnp.where(slot == x, moved, rows)
        s_ref[...] = rows
        for zh in range(8):
            for r1 in range(2):
                at = 17 * (zh ^ FIRST_ZH) + 4 * low + 2 * r1
                out_ref[at : at + 2, :] = s_ref[16 * r1 + 2 * zh : 16 * r1 + 2 * zh + 2, :]
    for zh in range(8):
        at = 17 * zh + 16
        out_ref[at : at + 1, :] = counts


def finish_kernel(at_ref, in_ref, old_ref, out_ref):
    sums, count_row = in_ref[0:16, :], in_ref[16:17, :]
    for zh in range(1, 8):
        sums = sums + in_ref[17 * zh : 17 * zh + 16, :]
        count_row = count_row + in_ref[17 * zh + 16 : 17 * zh + 17, :]
    lane = lax.broadcasted_iota(I32, (16, 128), 1)
    own = lane == at_ref[0] + lax.broadcasted_iota(I32, (16, 128), 0)
    counts = jnp.sum(jnp.where(own, count_row, 0.0), axis=1, keepdims=True)
    out_ref[...] = (sums + old_ref[...]) / (counts + 1.0)


def member_kernel(of, after_ref, place_ref, rows_ref, *refs):
    line_refs, out_ref = refs[:3], refs[3]
    core, y = place_ref[0], place_ref[1]
    r = rows_ref[2 * of : 2 * of + 2, :]
    away, far = (r >> 9) ^ y, ((r >> 8) & 1) ^ core
    block = jnp.where(away == 1 + 2 * core, 1 + far, jnp.where(far == 1, -1, jnp.where(away == 0, 0, jnp.where(away == 2, 3, -1))))
    at = jnp.where(block < 0, -1, (block << 8) + (r & 255))
    at = jnp.concatenate([at, jnp.zeros((6, 128), I32)], 0).astype(F32).T.astype(I32)
    at = jnp.concatenate([at[:, 0:1], at[:, 1:2]], 0)
    lane = lax.broadcasted_iota(I32, (256, ROWS), 1)
    total = jnp.zeros((256, 1024), F32)
    for first, line_ref in zip((0, 1, 3), line_refs):
        for k in range(line_ref.shape[0] // ROWS):
            pick = jnp.where(lane + ROWS * (first + k) == at, 1.0, 0.0).astype(BF16)
            rows = line_ref[ROWS * k : ROWS * k + ROWS, :]
            total = total + jnp.dot(pick, rows, preferred_element_type=F32)
    out_ref[...] = total.astype(BF16)


def match_kernel(after_ref, len_ref, own_ref, other_ref, out_ref):
    i = lax.broadcasted_iota(I32, (128, 128), 0)
    j = lax.broadcasted_iota(I32, (128, 128), 1)
    for s in range(2):
        one = own_ref[128 * s : 128 * s + 128, :] + other_ref[128 * s : 128 * s + 128, :]
        gram = lax.dot_general(one, one, (((1,), (1,)), ((), ())), preferred_element_type=F32)
        diagonal = jnp.where(i == j, gram, 0.0)
        down = lax.rsqrt(jnp.sum(diagonal, axis=1, keepdims=True) + 1e-06)
        across = lax.rsqrt(jnp.sum(diagonal, axis=0, keepdims=True) + 1e-06)
        cosine = gram * down * across
        length = len_ref[s : s + 1, :]
        largest = jnp.max(jnp.where((i < length) & (i != j), cosine, -2.0), axis=0, keepdims=True)
        out_ref[s : s + 1, :] = jnp.where(j[0:1] < length, largest, 0.0)


VMEM = pl.BlockSpec(memory_space=pltpu.VMEM)
HBM = pl.BlockSpec(memory_space=pltpu.HBM)
SMEM = pl.BlockSpec(memory_space=pltpu.SMEM)


def local(embeddings, assignments, old_centroids, slab_rows, slab_len):
    zh, x, y, core = (lax.axis_index(name).astype(I32) for name in ("zh", "x", "y", "c"))
    messages = pl.pallas_call(
        pack_kernel,
        out_shape=pltpu.HBM((4, 8, MSG, 128), BF16),
        in_specs=[HBM] * 4,
        out_specs=HBM,
        scratch_shapes=[
            pltpu.VMEM((ROWS, 1024), BF16),
            pltpu.VMEM((2, 128), I32),
            pltpu.VMEM((2, 128), I32),
            pltpu.SMEM((2,), I32),
            pltpu.VMEM((4, 8, MSG, 128), BF16),
            pltpu.SemaphoreType.DMA((2,)),
            pltpu.SemaphoreType.DMA((2,)),
            pltpu.SemaphoreType.DMA((3,)),
        ],
        compiler_params=params(8),
        cost_estimate=cost(1 << 20, 3 << 19),
        name="pack",
    )(*(pltpu.with_memory_space_constraint(a, pltpu.HBM) for a in (embeddings, assignments.reshape(2, 128), slab_rows, slab_len)))
    messages = lax.all_to_all(messages.reshape(BLOCK, MSG, 128), ("x", "y", "c"), 0, 0, axis_index_groups=[BLOCK_ORDER], tiled=True)
    parts, rows, lengths = pl.pallas_call(
        sum_kernel,
        out_shape=(pltpu.VMEM((528, 128), F32), pltpu.VMEM((4, 128), I32), pltpu.VMEM((2, 128), I32)),
        in_specs=[SMEM, VMEM],
        out_specs=(VMEM, VMEM, VMEM),
        compiler_params=params(20),
        cost_estimate=cost(1 << 31, 1 << 20),
        name="sums",
    )(((x * 8 + y * 2 + core) ^ BLOCK_ORDER[0]).reshape(1), messages)
    partner = lax.ppermute(embeddings, "c", [(0, 1), (1, 0)])
    embeddings, partner, parts = lax.optimization_barrier((embeddings, partner, parts))
    near = [(2 * i + c, 2 * (i ^ (1 + 2 * c)) + c) for i in range(4) for c in range(2)]
    line = [
        embeddings,
        lax.ppermute(jnp.concatenate([embeddings, partner]), ("y", "c"), near),
        lax.ppermute(embeddings, "y", [(i, i ^ 2) for i in range(4)]),
    ]
    parts = lax.all_to_all(parts.reshape(16, 33, 1, 128), ("zl", "x"), 0, 0, axis_index_groups=[PLANE_ORDER], tiled=True)
    parts = pl.pallas_call(
        regroup_kernel,
        out_shape=pltpu.VMEM((136, 128), F32),
        in_specs=[VMEM],
        out_specs=VMEM,
        scratch_shapes=[pltpu.VMEM((32, 128), F32)],
        compiler_params=params(4),
        cost_estimate=cost(1 << 18, 1 << 19),
        name="regroup",
    )(parts.reshape(528, 128))
    after = parts
    parts = lax.all_to_all(parts.reshape(8, 17, 1, 128), "zh", 0, 0, axis_index_groups=[RING_ORDER], tiled=True)
    place = jnp.stack([core, y])
    own, other = (
        pl.pallas_call(
            functools.partial(member_kernel, of),
            out_shape=jax.ShapeDtypeStruct((256, 1024), BF16),
            in_specs=[pl.BlockSpec(memory_space=pl.ANY), SMEM] + [VMEM] * 4,
            out_specs=VMEM,
            compiler_params=params(16),
            cost_estimate=cost(0, 0),
            name="members",
        )(after, place, rows, *line)
        for of in range(2)
    )
    other = lax.ppermute(other, "c", [(0, 1), (1, 0)])
    centroids = pl.pallas_call(
        finish_kernel,
        out_shape=jax.ShapeDtypeStruct((16, 128), F32),
        in_specs=[SMEM, VMEM, VMEM],
        out_specs=VMEM,
        compiler_params=params(4),
        cost_estimate=cost(1 << 35, 1 << 18),
        name="finish",
    )((zh * 16).reshape(1), parts.reshape(136, 128), old_centroids)
    best_cosine = pl.pallas_call(
        match_kernel,
        out_shape=jax.ShapeDtypeStruct((2, 128), F32),
        in_specs=[HBM] + [VMEM] * 3,
        out_specs=VMEM,
        compiler_params=params(8),
        cost_estimate=cost(0, 0),
        name="match",
    )(pltpu.with_memory_space_constraint(centroids, pltpu.HBM), lengths, own, other)
    return (centroids, best_cosine)


def solution(mesh):
    fine = Mesh(mesh.devices.reshape(SIZES), NAMES)
    dp, mp = ("zh", "zl", "x"), ("y", "c")
    placed = (
        P(dp + mp, None),
        P(dp + mp),
        P(dp, mp),
        P(dp + mp, None),
        P(dp + mp),
    )
    return jax.shard_map(
        local,
        mesh=fine,
        in_specs=placed,
        out_specs=(P(dp, mp), P(dp + mp, None)),
        check_vma=False,
    )
```

```python
import functools

import jax
import jax.numpy as jnp
from jax import lax
from jax.experimental import pallas as pl
from jax.experimental.pallas import tpu as pltpu
from jax.sharding import Mesh, PartitionSpec as P

F32, BF16, I32 = jnp.float32, jnp.bfloat16, jnp.int32
SIZES = (8, 4, 4, 4, 2)
NAMES = ("zh", "zl", "x", "y", "c")
BLOCK = 32
ROWS = 256
FEATS = 32
MSG = 80
MIB = 1 << 20
FIRST = (2, 4)
BLOCK_ORDER = [k ^ 20 for k in range(BLOCK)]
PLANE_FIRST = (1, 2)
PLANE_ORDER = [k ^ 6 for k in range(16)]
FIRST_ZH = 5
RING_ORDER = [k ^ FIRST_ZH for k in range(8)]


def params(mib):
    return pltpu.CompilerParams(vmem_limit_bytes=mib * MIB)


def cost(flops, moved):
    return pl.CostEstimate(flops=flops, bytes_accessed=moved, transcendentals=0)


def pack_kernel(emb_hbm, label_hbm, rows_hbm, len_hbm, out_hbm, emb_ref, label_ref, rows_ref, len_ref, msg_ref, in_sems, out_sems, sems):
    small = [
        pltpu.make_async_copy(label_hbm, label_ref, sems.at[0]),
        pltpu.make_async_copy(rows_hbm, rows_ref, sems.at[1]),
        pltpu.make_async_copy(len_hbm, len_ref, sems.at[2]),
    ]
    halves = [pl.ds(0, 512), pl.ds(512, 512)]
    blocks = [pltpu.make_async_copy(emb_hbm.at[:, at], emb_ref.at[:, at], in_sems.at[k]) for k, at in enumerate(halves)]
    for copy in blocks + small:
        copy.start()
    for copy in small:
        copy.wait()
    c, r = label_ref[...], rows_ref[...]
    high = ((c >> 6) & 3) * 64 + ((c >> 4) & 3) * 16 + (c >> 8) * 2 + (c & 1)
    low = ((c >> 1) & 1) * 4 + ((c >> 2) & 3)
    row = lax.broadcasted_iota(I32, (16, 128), 0)
    codes = jnp.zeros((16, 128), I32)
    for k, pair in enumerate((high, low, r >> 3, r & 7)):
        codes = jnp.where(row == 2 * k, pair[0:1], codes)
        codes = jnp.where(row == 2 * k + 1, pair[1:2], codes)
    for k in range(2):
        codes = jnp.where(row == 8 + k, len_ref[k], codes)
    codes = codes.astype(F32).astype(BF16)
    sent = []
    for k in range(2):
        blocks[k].wait()
        for mp in range(4 * k, 4 * k + 4):
            turned = emb_ref[:, 128 * mp : 128 * mp + 128].T
            for x in range(4):
                part, at = turned[x * FEATS : x * FEATS + FEATS], (x ^ FIRST[0], mp ^ FIRST[1])
                msg_ref[*at, 0:32, :] = part[:, 0:128]
                msg_ref[*at, 32:64, :] = part[:, 128:256]
                msg_ref[*at, 64:80, :] = codes
        at = pl.ds((4 * k) ^ FIRST[1], 4)
        sent.append(pltpu.make_async_copy(msg_ref.at[:, at], out_hbm.at[:, at], out_sems.at[k]))
        sent[k].start()
    for copy in sent:
        copy.wait()


def lanes(n):
    return lax.broadcasted_iota(I32, (n, 128), 0).astype(F32).astype(BF16)


def sum_kernel(from_ref, msg_ref, out_ref, rows_ref, len_ref):
    cluster = lanes(256)
    one, zero = jnp.ones((), BF16), jnp.zeros((), BF16)
    contract = (((1,), (1,)), ((), ()))
    sums = jnp.zeros((256, 256), F32)
    for first in range(0, BLOCK, 4):
        a, b = [], []
        for s in range(first, first + 4):
            codes = msg_ref[s, 64:80, :]
            for t in range(2):
                high, low = codes[t : t + 1], codes[2 + t : 3 + t]
                part = msg_ref[s, 32 * t : 32 * t + 32, :]
                a.append(jnp.where(cluster == high, one, zero))
                b.append(jnp.concatenate([jnp.where(low == jnp.asarray(g, BF16), part, zero) for g in range(8)], 0))
        a, b = (jnp.concatenate(blocks, 1) for blocks in (a, b))
        sums = sums + lax.dot_general(a, b, contract, preferred_element_type=F32)
    p, q = [], []
    for k in range(8):
        codes = msg_ref[(from_ref[0] & 24) + k, 64:80, :].astype(F32).astype(I32)
        for t in range(2):
            high, low = codes[t : t + 1], codes[2 + t : 3 + t]
            within = ((high >> 1) & 7) * 16 + (low & 3) * 4 + (low >> 2) * 2 + (high & 1)
            p.append(jnp.where(cluster[0:16] == (high >> 4).astype(F32).astype(BF16), one, zero))
            q.append(jnp.where(cluster[0:128] == within.astype(F32).astype(BF16), one, zero))
    p, q = (jnp.concatenate(blocks, 1) for blocks in (p, q))
    counts = lax.dot_general(p, q, contract, preferred_element_type=F32)
    for m in range(16):
        at = 33 * PLANE_ORDER[m]
        out_ref[at : at + 16, :] = sums[16 * m : 16 * m + 16, 0:128]
        out_ref[at + 16 : at + 32, :] = sums[16 * m : 16 * m + 16, 128:256]
        out_ref[at + 32 : at + 33, :] = counts[m : m + 1, :]
    for k in range(2):
        codes = msg_ref[from_ref[0] ^ k, 64:80, :].astype(F32).astype(I32)
        rows_ref[2 * k : 2 * k + 2, :] = codes[4:6] * 8 + codes[6:8]
        if k == 0:
            len_ref[...] = codes[8:10]


def regroup_kernel(in_ref, out_ref, s_ref):
    slot = lax.broadcasted_iota(I32, (32, 128), 1) // FEATS
    parts = []
    for x in range(4):
        first, *others = (in_ref[33 * at : 33 * at + 32, :] for at in range(x ^ PLANE_FIRST[1], 16, 4))
        parts.append((first + others[0]) + (others[1] + others[2]))
    counts = in_ref[32:33, :]
    for k in range(1, 16):
        counts = counts + in_ref[33 * k + 32 : 33 * k + 33, :]
    for low in range(4):
        rows = jnp.zeros((32, 128), F32)
        for x in range(4):
            shift = ((x - low) * FEATS) % 128
            moved = pltpu.roll(parts[x], shift, 1) if shift else parts[x]
            rows = jnp.where(slot == x, moved, rows)
        s_ref[...] = rows
        for zh in range(8):
            for r1 in range(2):
                at = 17 * (zh ^ FIRST_ZH) + 4 * low + 2 * r1
                out_ref[at : at + 2, :] = s_ref[16 * r1 + 2 * zh : 16 * r1 + 2 * zh + 2, :]
    for zh in range(8):
        at = 17 * zh + 16
        out_ref[at : at + 1, :] = counts


def finish_kernel(at_ref, in_ref, old_ref, out_ref):
    sums, count_row = in_ref[0:16, :], in_ref[16:17, :]
    for zh in range(1, 8):
        sums = sums + in_ref[17 * zh : 17 * zh + 16, :]
        count_row = count_row + in_ref[17 * zh + 16 : 17 * zh + 17, :]
    lane = lax.broadcasted_iota(I32, (16, 128), 1)
    own = lane == at_ref[0] + lax.broadcasted_iota(I32, (16, 128), 0)
    counts = jnp.sum(jnp.where(own, count_row, 0.0), axis=1, keepdims=True)
    out_ref[...] = (sums + old_ref[...]) / (counts + 1.0)


def member_kernel(of, after_ref, place_ref, rows_ref, *refs):
    line_refs, out_refs = refs[:3], refs[3:]
    core, y = place_ref[0], place_ref[1]
    r = rows_ref[2 * of : 2 * of + 2, :]
    away, far = (r >> 9) ^ y, ((r >> 8) & 1) ^ core
    block = jnp.where(away == 2 - core, 1 + far, jnp.where(far == 1, -1, jnp.where(away == 0, 0, jnp.where(away == 3, 3, -1))))
    at = jnp.where(block < 0, -1, (block << 8) + (r & 255))
    at = jnp.concatenate([at, jnp.zeros((6, 128), I32)], 0).astype(F32).T.astype(I32)
    at = jnp.concatenate([at[:, 0:1], at[:, 1:2]], 0)
    lane = lax.broadcasted_iota(I32, (256, ROWS), 1)
    total = jnp.zeros((256, 1024), F32)
    for first, line_ref in zip((0, 1, 3), line_refs):
        for k in range(line_ref.shape[0] // ROWS):
            pick = jnp.where(lane + ROWS * (first + k) == at, 1.0, 0.0).astype(BF16)
            rows = line_ref[ROWS * k : ROWS * k + ROWS, :]
            total = total + jnp.dot(pick, rows, preferred_element_type=F32)
    for s, out_ref in enumerate(out_refs):
        out_ref[...] = total[128 * s : 128 * s + 128].astype(BF16)


def match_kernel(len_ref, *refs):
    own_refs, other_refs, out_ref = refs[0:2], refs[2:4], refs[4]
    i = lax.broadcasted_iota(I32, (128, 128), 0)
    j = lax.broadcasted_iota(I32, (128, 128), 1)
    for s in range(2):
        one = own_refs[s][...] + other_refs[s][...]
        gram = lax.dot_general(one, one, (((1,), (1,)), ((), ())), preferred_element_type=F32)
        diagonal = jnp.where(i == j, gram, 0.0)
        down = lax.rsqrt(jnp.sum(diagonal, axis=1, keepdims=True) + 1e-06)
        across = lax.rsqrt(jnp.sum(diagonal, axis=0, keepdims=True) + 1e-06)
        cosine = gram * down * across
        length = len_ref[s : s + 1, :]
        largest = jnp.max(jnp.where((i < length) & (i != j), cosine, -2.0), axis=0, keepdims=True)
        out_ref[s : s + 1, :] = jnp.where(j[0:1] < length, largest, 0.0)


VMEM = pl.BlockSpec(memory_space=pltpu.VMEM)
HBM = pl.BlockSpec(memory_space=pltpu.HBM)
SMEM = pl.BlockSpec(memory_space=pltpu.SMEM)


def local(embeddings, assignments, old_centroids, slab_rows, slab_len):
    zh, x, y, core = (lax.axis_index(name).astype(I32) for name in ("zh", "x", "y", "c"))
    messages = pl.pallas_call(
        pack_kernel,
        out_shape=pltpu.HBM((4, 8, MSG, 128), BF16),
        in_specs=[HBM] * 4,
        out_specs=HBM,
        scratch_shapes=[
            pltpu.VMEM((ROWS, 1024), BF16),
            pltpu.VMEM((2, 128), I32),
            pltpu.VMEM((2, 128), I32),
            pltpu.SMEM((2,), I32),
            pltpu.VMEM((4, 8, MSG, 128), BF16),
            pltpu.SemaphoreType.DMA((2,)),
            pltpu.SemaphoreType.DMA((2,)),
            pltpu.SemaphoreType.DMA((3,)),
        ],
        compiler_params=params(8),
        cost_estimate=cost(1 << 20, 3 << 19),
        name="pack",
    )(*(pltpu.with_memory_space_constraint(a, pltpu.HBM) for a in (embeddings, assignments.reshape(2, 128), slab_rows, slab_len)))
    messages = lax.all_to_all(messages.reshape(BLOCK, MSG, 128), ("x", "y", "c"), 0, 0, axis_index_groups=[BLOCK_ORDER], tiled=True)
    parts, rows, lengths = pl.pallas_call(
        sum_kernel,
        out_shape=(pltpu.VMEM((528, 128), F32), pltpu.VMEM((4, 128), I32), pltpu.VMEM((2, 128), I32)),
        in_specs=[SMEM, VMEM],
        out_specs=(VMEM, VMEM, VMEM),
        compiler_params=params(20),
        cost_estimate=cost(1 << 31, 1 << 20),
        name="sums",
    )(((x * 8 + y * 2 + core) ^ BLOCK_ORDER[0]).reshape(1), messages)
    partner = lax.ppermute(embeddings, "c", [(0, 1), (1, 0)])
    embeddings, partner, parts = lax.optimization_barrier((embeddings, partner, parts))
    near = [(2 * i + c, 2 * (i ^ (2 - c)) + c) for i in range(4) for c in range(2)]
    line = [
        embeddings,
        lax.ppermute(jnp.concatenate([embeddings, partner]), ("y", "c"), near),
        lax.ppermute(embeddings, "y", [(i, i ^ 3) for i in range(4)]),
    ]
    parts = lax.all_to_all(parts.reshape(16, 33, 1, 128), ("zl", "x"), 0, 0, axis_index_groups=[PLANE_ORDER], tiled=True)
    parts = pl.pallas_call(
        regroup_kernel,
        out_shape=pltpu.VMEM((136, 128), F32),
        in_specs=[VMEM],
        out_specs=VMEM,
        scratch_shapes=[pltpu.VMEM((32, 128), F32)],
        compiler_params=params(4),
        cost_estimate=cost(1 << 18, 1 << 19),
        name="regroup",
    )(parts.reshape(528, 128))
    after = parts
    parts = lax.all_to_all(parts.reshape(8, 17, 1, 128), "zh", 0, 0, axis_index_groups=[RING_ORDER], tiled=True)
    place = jnp.stack([core, y])
    own, others = (
        pl.pallas_call(
            functools.partial(member_kernel, of),
            out_shape=[jax.ShapeDtypeStruct((128, 1024), BF16)] * 2,
            in_specs=[pl.BlockSpec(memory_space=pl.ANY), SMEM] + [VMEM] * 4,
            out_specs=[VMEM] * 2,
            compiler_params=params(16),
            cost_estimate=cost(0, 0),
            name="members",
        )(after, place, rows, *line)
        for of in range(2)
    )
    others = [lax.ppermute(other, "c", [(0, 1), (1, 0)]) for other in others]
    best_cosine = pl.pallas_call(
        match_kernel,
        out_shape=jax.ShapeDtypeStruct((2, 128), F32),
        in_specs=[VMEM] * 5,
        out_specs=VMEM,
        compiler_params=params(8),
        cost_estimate=cost(0, 0),
        name="match",
    )(lengths, *own, *others)
    parts, best_cosine = lax.optimization_barrier((parts, best_cosine))
    centroids = pl.pallas_call(
        finish_kernel,
        out_shape=jax.ShapeDtypeStruct((16, 128), F32),
        in_specs=[SMEM, VMEM, VMEM],
        out_specs=VMEM,
        compiler_params=params(4),
        cost_estimate=cost(1 << 18, 1 << 18),
        name="finish",
    )((zh * 16).reshape(1), parts.reshape(136, 128), old_centroids)
    return (centroids, best_cosine)


def solution(mesh):
    fine = Mesh(mesh.devices.reshape(SIZES), NAMES)
    dp, mp = ("zh", "zl", "x"), ("y", "c")
    placed = (
        P(dp + mp, None),
        P(dp + mp),
        P(dp, mp),
        P(dp + mp, None),
        P(dp + mp),
    )
    return jax.shard_map(
        local,
        mesh=fine,
        in_specs=placed,
        out_specs=(P(dp, mp), P(dp + mp, None)),
        check_vma=False,
    )
```
